32 devices in a mesh: req: 16 (over z, y, x), tp: 2 (over core).
Axes of the slice: x: 2, y: 2, z: 4, core: 2. Of those that a mesh axis runs over, the one named last changes fastest.
Arguments:
- patches: bfloat16 [7168, 1664], P('req', 'tp'), may hold values from -48 to 48
- ln_gain: bfloat16 [1664], P('tp'), may hold values from 0.099609375 to 1.8984375
- ln_bias: bfloat16 [1664], P('tp'), may hold values from -3 to 3
- merge_weight: bfloat16 [4, 1664, 1664], P(None, 'tp'), may hold values from -0.078125 to 0.078125
- text_rows: bfloat16 [8192, 1664], P('req', 'tp'), may hold values from -48 to 48
- norm_gain: bfloat16 [1664], replicated, may hold values from 0.099609375 to 1.8984375
- qkv_weight: bfloat16 [1664, 4992], P('req', 'tp'), may hold values from -0.15625 to 0.15625
- token_pos: int32 [1792], P('req'), may hold values from 0 to 8191, as said below
- text_len: int32 [2], replicated, may hold values from 1 to 4096, as said below
Outputs:
- qkv_rows: bfloat16 [8192, 4992], P('req', 'tp')
The draws below stay inside these ranges and needn't reach their ends.
Inputs may be any that keep to these rules, and one draw needn't show every extreme that they name: `token_pos`: all distinct. A device's merged tokens form 8 images of consecutive rows, each a multiple of 2 and at most 16 tokens, each written to consecutive positions that one device holds; a device's images go to 8 different devices and every device receives exactly 8 images. In every draw some image has 16 tokens. `text_len`: every image position of a request lies below its length.
All inputs are finite; a program needn't handle non-finite values.
Results may differ from the reference program's by a relative error of at most 0.0063.
Values may be sent and summed in bfloat16 or wider, within the bound.
No kernel may reach another device: no remote copies, remote signals or barrier semaphores. Data moves between devices by JAX's collectives and lax.ppermute only.
A program may use at most 128 MiB of HBM per device.

```python
import math
import jax
import jax.numpy as jnp
from jax import lax

DV = 1664
D = 1664
TXT_DEV = 512
SEQ = 4096
IMG_CAP = 16
IMGS = 8
M_DEV = 112
PATCHES = 7168
MERGED = 1792
TOKENS = 8192
REQS = 2
QKV = 4992
N_REQ = 16


def image_layout(key):
    devices = N_REQ
    quantum = IMG_CAP // 8
    stride = devices // IMGS
    slot_total = IMGS * 7
    subkeys = jax.random.split(jax.random.fold_in(key, 7), 6)
    perm_keys = jax.random.split(subkeys[0], devices)
    ranks = jax.vmap(lambda one_key: jax.random.permutation(one_key, slot_total))(perm_keys).astype(jnp.int32)
    forced_dev = jax.random.randint(subkeys[1], (), 0, devices)
    forced_img = jax.random.randint(subkeys[2], (), 0, IMGS)
    slot_image = jnp.arange(slot_total, dtype=jnp.int32) // 7
    forced = (jnp.arange(devices, dtype=jnp.int32)[:, None] == forced_dev) & (slot_image[None, :] == forced_img)
    scores = jnp.where(forced, ranks - slot_total, ranks)
    order = jnp.argsort(scores, axis=1)
    placed = jnp.argsort(order, axis=1)
    chosen = (placed < 6 * IMGS).astype(jnp.int32)
    counts = jnp.sum(chosen.reshape(devices, IMGS, 7), axis=2)
    image_sizes = quantum * (1 + counts)
    image_ids = jnp.arange(IMGS, dtype=jnp.int32)
    recv_source = (jnp.arange(devices, dtype=jnp.int32)[:, None] - image_ids[None, :] * stride) % devices
    recv_sizes = image_sizes[recv_source, image_ids[None, :]]
    spare = TXT_DEV - jnp.sum(recv_sizes, axis=1)
    weights = jax.random.randint(subkeys[3], (devices, IMGS + 1), 1, 64)
    gap_sizes = spare[:, None] * weights // jnp.sum(weights, axis=1, keepdims=True)
    local_start = jnp.cumsum(recv_sizes, axis=1) - recv_sizes + jnp.cumsum(gap_sizes[:, :IMGS], axis=1)
    receiver = jax.random.permutation(subkeys[4], devices).astype(jnp.int32)
    global_start = receiver[:, None] * TXT_DEV + local_start
    send_target = (jnp.arange(devices, dtype=jnp.int32)[:, None] + image_ids[None, :] * stride) % devices
    send_start = global_start[send_target, image_ids[None, :]]
    bounds = jnp.cumsum(image_sizes, axis=1)
    tokens = jnp.arange(M_DEV, dtype=jnp.int32)
    image_of = jnp.sum((tokens[None, :, None] >= bounds[:, None, :]).astype(jnp.int32), axis=2)
    offset_before = jnp.take_along_axis(bounds - image_sizes, image_of, axis=1)
    first_pos = jnp.take_along_axis(send_start, image_of, axis=1)
    positions_src = first_pos + tokens[None, :] - offset_before
    sender = jax.random.permutation(subkeys[5], devices).astype(jnp.int32)
    positions = jnp.zeros((devices, M_DEV), jnp.int32).at[sender].set(positions_src)
    return positions.reshape(-1).astype(jnp.int32)


def draw_token_pos(key, part):
    return image_layout(key)


def draw_text_len(key, part):
    positions = image_layout(key)
    request = positions // SEQ
    last_image = jax.ops.segment_max(positions % SEQ + 1, request, num_segments=REQS)
    last_image = jnp.maximum(last_image, 1)
    drawn_len = jax.random.randint(jax.random.fold_in(key, 11), (REQS,), SEQ // 2, SEQ + 1)
    return jnp.maximum(last_image, drawn_len).astype(jnp.int32)


def rough_field(key, row_total, col_total):
    subkeys = jax.random.split(key, 4)
    noise = jax.random.normal(subkeys[0], (row_total, col_total), jnp.float32)
    rising = math.log(3.0)
    row_scale = jnp.exp(jax.random.uniform(subkeys[1], (row_total, 1), jnp.float32, 0.0, math.log(10.0)))
    col_scale = jnp.exp(rising * jnp.arange(col_total, dtype=jnp.float32) / (col_total - 1) + jax.random.uniform(subkeys[2], (1, col_total), jnp.float32, -0.7, 0.7))
    offset = 0.5 * jax.random.normal(subkeys[3], (row_total, 1), jnp.float32)
    field = row_scale * (noise * col_scale + offset) / 3.0
    return jnp.clip(field, -48.0, 48.0)


def draw_patches(key, part):
    return rough_field(jax.random.fold_in(key, 21), PATCHES, DV).astype(jnp.bfloat16)


def draw_text_rows(key, part):
    return rough_field(jax.random.fold_in(key, 23), TOKENS, D).astype(jnp.bfloat16)


def steps_of(stream_key, extent, pieces, low, top_value):
    loudness, own = 1.0, jax.random.fold_in(stream_key, 6)
    for axis_at, blocks in pieces:
        heights = jnp.exp(jax.random.uniform(jax.random.fold_in(own, axis_at), (blocks,), jnp.float32, low / len(pieces), top_value / len(pieces)))
        loudness = loudness * jnp.repeat(heights, extent[axis_at] // blocks).reshape([-1 if axis == axis_at else 1 for axis in range(len(extent))])
    return loudness


def bell_draw(rng, shape, width, reach, shards=(), held_as=jnp.bfloat16):
    array = width * jax.random.normal(rng, shape, jnp.float32)
    if shards:
        array = array * steps_of(rng, shape, shards, -0.22, 0.18)
    return jnp.clip(array, -reach, reach).astype(held_as)


def setup_inputs(seed: int = 0) -> dict:
    splits = jax.random.split(jax.random.key(seed), 10)
    patches = draw_patches(jax.random.fold_in(splits[9], 71), 0)
    ln_gain = jnp.clip(1.0 + 0.18 * jax.random.normal(splits[1], (DV,), jnp.float32), 0.099609375, 1.8984375).astype(jnp.bfloat16)
    ln_bias = bell_draw(splits[2], (DV,), 0.5, 3.0, ((0, 2),))
    merge_weight = bell_draw(splits[3], (4, DV, D), (4 * DV) ** -0.5, 0.078125, ((1, 2),))
    text_rows = draw_text_rows(jax.random.fold_in(splits[9], 71), 0)
    norm_gain = jnp.clip(1.0 + 0.18 * jax.random.normal(splits[5], (D,), jnp.float32), 0.099609375, 1.8984375).astype(jnp.bfloat16)
    qkv_weight = bell_draw(splits[6], (D, QKV), D ** -0.5, 0.15625, ((0, 16), (1, 2)))
    token_pos = draw_token_pos(jax.random.fold_in(splits[9], 71), 0)
    text_len = draw_text_len(jax.random.fold_in(splits[9], 71), 0)
    return {"patches": patches, "ln_gain": ln_gain, "ln_bias": ln_bias, "merge_weight": merge_weight, "text_rows": text_rows, "norm_gain": norm_gain, "qkv_weight": qkv_weight, "token_pos": token_pos, "text_len": text_len}


EPSILON = 1e-06

def reference(patches, ln_gain, ln_bias, merge_weight, text_rows, norm_gain, qkv_weight, token_pos, text_len):
    values = patches.astype(jnp.float32)
    row_mean = lax.optimization_barrier(jnp.sum(values, axis=1, keepdims=True)) / DV
    second = lax.optimization_barrier(jnp.sum(values * values, axis=1, keepdims=True)) / DV
    normed = ((values - row_mean) * lax.rsqrt(second - row_mean * row_mean + EPSILON) * ln_gain.astype(jnp.float32) + ln_bias.astype(jnp.float32)).astype(jnp.bfloat16)
    grouped = normed.reshape(MERGED, 4 * DV)
    merged = jnp.dot(grouped, merge_weight.reshape(4 * DV, D), preferred_element_type=jnp.float32).astype(jnp.bfloat16)
    combined = text_rows.at[token_pos].set(merged)
    full_rows = combined.astype(jnp.float32)
    scaled = (full_rows * lax.rsqrt(lax.optimization_barrier(jnp.mean(full_rows * full_rows, axis=1, keepdims=True)) + EPSILON) * norm_gain.astype(jnp.float32)).astype(jnp.bfloat16)
    projected = jnp.dot(scaled, qkv_weight, preferred_element_type=jnp.float32)
    position = jnp.arange(TOKENS, dtype=jnp.int32)
    limits = text_len[position // SEQ]
    keep_row = position % SEQ < limits
    return jnp.where(keep_row[:, None], projected, 0.0).astype(jnp.bfloat16)
```

```python
import functools

import jax
import jax.numpy as jnp
from jax import lax
from jax.sharding import PartitionSpec as P

DV = 1664
SEQ = 4096
IMG_CAP = 16
EPSILON = 1e-06


def folded_ring(count):
    odd = list(range(1, count, 2))
    even = list(range(0, count, 2))
    return even[:1] + odd + even[:0:-1]


def tp_shift(value, n_tp, distance):
    return lax.ppermute(value, "tp", [(i, (i + distance) % n_tp) for i in range(n_tp)])


def tp_gather(value, n_tp, axis):
    me = lax.axis_index("tp")
    width = value.shape[axis]
    if n_tp == 2:
        other = tp_shift(value, 2, 1)
        first = jnp.where(me == 0, value, other)
        second = jnp.where(me == 0, other, value)
        return jnp.concatenate([first, second], axis=axis)
    shape = list(value.shape)
    shape[axis] = width * n_tp
    whole = jnp.zeros(shape, value.dtype)
    for distance in range(n_tp):
        block = value if distance == 0 else tp_shift(value, n_tp, distance)
        whole = lax.dynamic_update_slice_in_dim(
            whole, block, (me - distance) % n_tp * width, axis
        )
    return whole


def tp_scatter_sum(value, n_tp, axis):
    me = lax.axis_index("tp")
    width = value.shape[axis] // n_tp
    total = lax.dynamic_slice_in_dim(value, me * width, width, axis)
    for distance in range(1, n_tp):
        block = lax.dynamic_slice_in_dim(value, (me + distance) % n_tp * width, width, axis)
        total = total + tp_shift(block, n_tp, distance)
    return total


def weight_groups(weight, n_req):
    lines = n_req // 4
    order = folded_ring(lines)
    following = {order[i]: order[(i + 1) % lines] for i in range(lines)}
    line_perm = [(z * 4 + p, following[z] * 4 + p) for z in range(lines) for p in range(4)]
    x_perm = [(i, i ^ 1) for i in range(n_req)]
    y_perm = [(i, i ^ 2) for i in range(n_req)]
    preceding = jnp.array([order[order.index(z) - 1] for z in range(lines)], jnp.int32)
    plane = lax.axis_index("req") // 4
    rows = weight.shape[0]
    cut = rows // 16 * 8
    held = weight
    groups = []
    for step in range(lines):
        by_x = lax.ppermute(held, "req", x_perm)
        by_y = lax.ppermute(held, "req", y_perm)
        upper = lax.ppermute(by_y[:cut], "req", x_perm)
        lower = lax.ppermute(by_x[cut:], "req", y_perm)
        groups.append((plane, [(0, held), (1, by_x), (2, by_y), (3, upper, lower)]))
        if step < lines - 1:
            held = lax.ppermute(held, "req", line_perm)
            plane = preceding[plane]
    return groups


def shards(
    n_req, n_tp,
    patches, ln_gain, ln_bias, merge_weight, text_rows, norm_gain, qkv_weight, token_pos, text_len,
):
    row_count, width = text_rows.shape
    me = lax.axis_index("req")
    groups = weight_groups(qkv_weight, n_req)
    text_full = tp_gather(text_rows.T, n_tp, 0)

    values = patches.astype(jnp.float32)
    sum_part = jnp.sum(values, axis=1)
    square_part = jnp.sum(values * values, axis=1)
    sum_total, square_total = lax.psum((sum_part, square_part), "tp")
    row_mean = (sum_total / DV)[:, None]
    second = (square_total / DV)[:, None]
    normed = (
        (values - row_mean)
        * lax.rsqrt(second - row_mean * row_mean + EPSILON)
        * ln_gain.astype(jnp.float32)
        + ln_bias.astype(jnp.float32)
    ).astype(jnp.bfloat16)
    grouped = normed.reshape(patches.shape[0] // 4, 4, patches.shape[1])
    partial_value = jnp.einsum(
        "mkf,kfd->md", grouped, merge_weight, preferred_element_type=jnp.float32
    )
    merged = tp_scatter_sum(partial_value, n_tp, 1).astype(jnp.bfloat16)

    token_count = token_pos.shape[0]
    target = token_pos // row_count
    same = target[:, None] == target[None, :]
    ids = jnp.arange(token_count, dtype=jnp.int32)
    before = jnp.sum((same & (ids[None, :] < ids[:, None])).astype(jnp.int32), axis=1)
    slot = target * IMG_CAP + before
    slot_count = n_req * IMG_CAP
    place = (
        jnp.arange(slot_count, dtype=jnp.int32)[:, None] == slot[None, :]
    ).astype(jnp.bfloat16)
    code = token_pos % row_count + 1
    code_cols = jnp.stack([code // 256, code % 256], axis=1).astype(jnp.bfloat16)
    padding = (-width - 2) % 128
    payload = jnp.concatenate(
        [merged, code_cols, jnp.zeros((token_count, padding), jnp.bfloat16)], axis=1
    )
    outgoing = jnp.dot(place, payload, preferred_element_type=jnp.float32).astype(jnp.bfloat16)
    arrived = lax.all_to_all(
        outgoing.reshape(n_req, IMG_CAP, -1), "req", split_axis=0, concat_axis=0
    ).reshape(slot_count, -1)
    local = (
        arrived[:, width].astype(jnp.int32) * 256 + arrived[:, width + 1].astype(jnp.int32) - 1
    )
    hit = local[:, None] == jnp.arange(row_count, dtype=jnp.int32)[None, :]
    image_rows = tp_gather(arrived[:, :width], n_tp, 1)
    image_part = lax.dot_general(
        image_rows,
        hit.astype(jnp.bfloat16),
        (((0,), (0,)), ((), ())),
        preferred_element_type=jnp.float32,
    )
    full = jnp.where(jnp.any(hit, axis=0)[None, :], image_part, text_full.astype(jnp.float32))
    scaled = (
        full
        * lax.rsqrt(jnp.mean(full * full, axis=0, keepdims=True) + EPSILON)
        * norm_gain.astype(jnp.float32)[:, None]
    ).astype(jnp.bfloat16)

    rows = qkv_weight.shape[0]
    corner = me % 4
    total = None
    for plane, pieces in groups:
        lefts, rights = [], []
        for flip, *blocks in pieces:
            start = (plane * 4 + (corner ^ flip)) * rows
            rights.append(lax.dynamic_slice_in_dim(scaled, start, rows, 0))
            lefts.extend(blocks)
        part = lax.dot_general(
            jnp.concatenate(lefts, axis=0),
            jnp.concatenate(rights, axis=0),
            (((0,), (0,)), ((), ())),
            preferred_element_type=jnp.float32,
        )
        total = part if total is None else total + part

    position = me * row_count + jnp.arange(row_count, dtype=jnp.int32)
    request_ids = jnp.arange(text_len.shape[0], dtype=jnp.int32)
    limits = jnp.sum(
        jnp.where((position // SEQ)[:, None] == request_ids[None, :], text_len[None, :], 0), axis=1
    )
    keep_row = position % SEQ < limits
    return jnp.where(keep_row[None, :], total, 0.0).astype(jnp.bfloat16).T


def solution(mesh):
    placed = (
        P("req", "tp"),
        P("tp"),
        P("tp"),
        P(None, "tp", None),
        P("req", "tp"),
        P(),
        P("req", "tp"),
        P("req"),
        P(),
    )
    body = functools.partial(shards, mesh.shape["req"], mesh.shape["tp"])
    return jax.shard_map(
        body, mesh=mesh, in_specs=placed, out_specs=P("req", "tp"), check_vma=False
    )
```

```python
import functools

import jax
import jax.numpy as jnp
from jax import lax
from jax.sharding import PartitionSpec as P

DV = 1664
SEQ = 4096
IMG_CAP = 16
EPSILON = 1e-06


def folded_ring(count):
    odd = list(range(1, count, 2))
    even = list(range(0, count, 2))
    return even[:1] + odd + even[:0:-1]


def tp_shift(value, n_tp, distance):
    return lax.ppermute(value, "tp", [(i, (i + distance) % n_tp) for i in range(n_tp)])


def tp_gather(value, n_tp, axis):
    me = lax.axis_index("tp")
    width = value.shape[axis]
    if n_tp == 2:
        other = tp_shift(value, 2, 1)
        first = jnp.where(me == 0, value, other)
        second = jnp.where(me == 0, other, value)
        return jnp.concatenate([first, second], axis=axis)
    shape = list(value.shape)
    shape[axis] = width * n_tp
    whole = jnp.zeros(shape, value.dtype)
    for distance in range(n_tp):
        block = value if distance == 0 else tp_shift(value, n_tp, distance)
        whole = lax.dynamic_update_slice_in_dim(
            whole, block, (me - distance) % n_tp * width, axis
        )
    return whole


def tp_scatter_sum(value, n_tp, axis):
    me = lax.axis_index("tp")
    width = value.shape[axis] // n_tp
    total = lax.dynamic_slice_in_dim(value, me * width, width, axis)
    for distance in range(1, n_tp):
        block = lax.dynamic_slice_in_dim(value, (me + distance) % n_tp * width, width, axis)
        total = total + tp_shift(block, n_tp, distance)
    return total


def tie(*values):
    return lax.optimization_barrier(values)


class WeightRing:
    def __init__(self, weight, n_req):
        lines = n_req // 4
        order = folded_ring(lines)
        following = {order[i]: order[(i + 1) % lines] for i in range(lines)}
        self.line_perm = [(z * 4 + p, following[z] * 4 + p) for z in range(lines) for p in range(4)]
        self.x_perm = [(i, i ^ 1) for i in range(n_req)]
        self.y_perm = [(i, i ^ 2) for i in range(n_req)]
        self.preceding = jnp.array([order[order.index(z) - 1] for z in range(lines)], jnp.int32)
        self.lines = lines
        self.cut = weight.shape[0] // 16 * 8

    def along_line(self, block):
        return lax.ppermute(block, "req", self.line_perm)

    def to_sides(self, block):
        return lax.ppermute(block, "req", self.x_perm), lax.ppermute(block, "req", self.y_perm)

    def to_corner(self, by_x, by_y):
        upper = lax.ppermute(by_y[: self.cut], "req", self.x_perm)
        lower = lax.ppermute(by_x[self.cut :], "req", self.y_perm)
        return upper, lower


def shards(
    n_req, n_tp,
    patches, ln_gain, ln_bias, merge_weight, text_rows, norm_gain, qkv_weight, token_pos, text_len,
):
    row_count, width = text_rows.shape
    me = lax.axis_index("req")
    ring = WeightRing(qkv_weight, n_req)
    lines = ring.lines
    held = [qkv_weight]
    sides = []
    corners = []

    def next_line(deps=()):
        if len(held) < lines:
            held.append(ring.along_line(held[-1]))

    def next_sides():
        if len(sides) < lines:
            sides.append(ring.to_sides(held[len(sides)]))

    def next_corner():
        if len(corners) < lines:
            corners.append(ring.to_corner(*sides[len(corners)]))

    next_line()
    next_sides()
    text_other = text_rows.T
    text_full = tp_gather(text_other, n_tp, 0)

    values = patches.astype(jnp.float32)
    sum_part = jnp.sum(values, axis=1)
    square_part = jnp.sum(values * values, axis=1)
    sum_total, square_total = lax.psum((sum_part, square_part), "tp")
    row_mean = (sum_total / DV)[:, None]
    second = (square_total / DV)[:, None]
    normed = (
        (values - row_mean)
        * lax.rsqrt(second - row_mean * row_mean + EPSILON)
        * ln_gain.astype(jnp.float32)
        + ln_bias.astype(jnp.float32)
    ).astype(jnp.bfloat16)

    normed, held[-1], sides[0] = tie(normed, held[-1], sides[0])
    next_line()
    next_sides()
    next_corner()

    grouped = normed.reshape(patches.shape[0] // 4, 4, patches.shape[1])
    partial_value = jnp.einsum(
        "mkf,kfd->md", grouped, merge_weight, preferred_element_type=jnp.float32
    )

    partial_value, held[-1] = tie(partial_value, held[-1])
    next_line()
    next_sides()
    merged = tp_scatter_sum(partial_value, n_tp, 1).astype(jnp.bfloat16)

    token_count = token_pos.shape[0]
    target = token_pos // row_count
    same = target[:, None] == target[None, :]
    ids = jnp.arange(token_count, dtype=jnp.int32)
    before = jnp.sum((same & (ids[None, :] < ids[:, None])).astype(jnp.int32), axis=1)
    slot = target * IMG_CAP + before
    slot_count = n_req * IMG_CAP
    place = (
        jnp.arange(slot_count, dtype=jnp.int32)[:, None] == slot[None, :]
    ).astype(jnp.bfloat16)
    code = token_pos % row_count + 1
    code_cols = jnp.stack([code // 256, code % 256], axis=1).astype(jnp.bfloat16)
    padding = (-width - 2) % 128
    payload = jnp.concatenate(
        [merged, code_cols, jnp.zeros((token_count, padding), jnp.bfloat16)], axis=1
    )
    outgoing = jnp.dot(place, payload, preferred_element_type=jnp.float32).astype(jnp.bfloat16)
    arrived = lax.all_to_all(
        outgoing.reshape(n_req, IMG_CAP, -1), "req", split_axis=0, concat_axis=0
    ).reshape(slot_count, -1)

    arrived, held[-1], sides[1] = tie(arrived, held[-1], sides[1])
    next_corner()
    next_sides()
    local = (
        arrived[:, width].astype(jnp.int32) * 256 + arrived[:, width + 1].astype(jnp.int32) - 1
    )
    hit = local[:, None] == jnp.arange(row_count, dtype=jnp.int32)[None, :]
    image_rows = tp_gather(arrived[:, :width], n_tp, 1)
    image_part = lax.dot_general(
        image_rows,
        hit.astype(jnp.bfloat16),
        (((0,), (0,)), ((), ())),
        preferred_element_type=jnp.float32,
    )
    full = jnp.where(jnp.any(hit, axis=0)[None, :], image_part, text_full.astype(jnp.float32))
    full, sides[2 % lines] = tie(full, sides[2 % lines])
    next_corner()
    scaled = (
        full
        * lax.rsqrt(jnp.mean(full * full, axis=0, keepdims=True) + EPSILON)
        * norm_gain.astype(jnp.float32)[:, None]
    ).astype(jnp.bfloat16)

    while len(corners) < lines:
        next_line()
        next_sides()
        next_corner()

    rows = qkv_weight.shape[0]
    corner = me % 4

    def product(plane, flip, blocks, first=0):
        count = sum(block.shape[0] for block in blocks)
        start = (plane * 4 + (corner ^ flip)) * rows + first
        return lax.dot_general(
            blocks[0] if len(blocks) == 1 else jnp.concatenate(blocks, axis=0),
            lax.dynamic_slice_in_dim(scaled, start, count, 0),
            (((0,), (0,)), ((), ())),
            preferred_element_type=jnp.float32,
        )

    def product_of(pieces):
        lefts = [block for _, _, _, block in pieces]
        rights = [
            lax.dynamic_slice_in_dim(
                scaled, (plane * 4 + (corner ^ flip)) * rows + first, block.shape[0], 0
            )
            for plane, flip, first, block in pieces
        ]
        return lax.dot_general(
            jnp.concatenate(lefts, axis=0),
            jnp.concatenate(rights, axis=0),
            (((0,), (0,)), ((), ())),
            preferred_element_type=jnp.float32,
        )

    plane = me // 4
    total = jnp.zeros((qkv_weight.shape[1], row_count), jnp.float32)
    cut = ring.cut
    for step in range(lines):
        by_x, by_y = sides[step]
        upper, lower = corners[step]
        total = total + product_of(
            [(plane, 0, 0, held[step]), (plane, 1, 0, by_x), (plane, 2, 0, by_y)]
        )
        total = total + product_of([(plane, 3, 0, upper), (plane, 3, cut, lower)])
        plane = ring.preceding[plane]

    position = me * row_count + jnp.arange(row_count, dtype=jnp.int32)
    request_ids = jnp.arange(text_len.shape[0], dtype=jnp.int32)
    limits = jnp.sum(
        jnp.where((position // SEQ)[:, None] == request_ids[None, :], text_len[None, :], 0), axis=1
    )
    keep_row = position % SEQ < limits
    return jnp.where(keep_row[None, :], total, 0.0).astype(jnp.bfloat16).T


def solution(mesh):
    placed = (
        P("req", "tp"),
        P("tp"),
        P("tp"),
        P(None, "tp", None),
        P("req", "tp"),
        P(),
        P("req", "tp"),
        P("req"),
        P(),
    )
    body = functools.partial(shards, mesh.shape["req"], mesh.shape["tp"])
    return jax.shard_map(
        body, mesh=mesh, in_specs=placed, out_specs=P("req", "tp"), check_vma=False
    )
```

```python
import functools

import jax
import jax.numpy as jnp
import numpy as np
from jax import lax
from jax.experimental import pallas as pl
from jax.experimental.pallas import tpu as pltpu
from jax.sharding import PartitionSpec as P

DV = 1664
SEQ = 4096
IMG_CAP = 16
EPSILON = 1e-06


def folded_ring(count):
    odd = list(range(1, count, 2))
    even = list(range(0, count, 2))
    return even[:1] + odd + even[:0:-1]


def tp_shift(value, n_tp, distance):
    return lax.ppermute(value, "tp", [(i, (i + distance) % n_tp) for i in range(n_tp)])


def tp_gather(value, n_tp, axis):
    me = lax.axis_index("tp")
    width = value.shape[axis]
    if n_tp == 2:
        other = tp_shift(value, 2, 1)
        first = jnp.where(me == 0, value, other)
        second = jnp.where(me == 0, other, value)
        return jnp.concatenate([first, second], axis=axis)
    shape = list(value.shape)
    shape[axis] = width * n_tp
    whole = jnp.zeros(shape, value.dtype)
    for distance in range(n_tp):
        block = value if distance == 0 else tp_shift(value, n_tp, distance)
        whole = lax.dynamic_update_slice_in_dim(
            whole, block, (me - distance) % n_tp * width, axis
        )
    return whole


def tp_scatter_sum(value, n_tp, axis):
    me = lax.axis_index("tp")
    width = value.shape[axis] // n_tp
    total = lax.dynamic_slice_in_dim(value, me * width, width, axis)
    for distance in range(1, n_tp):
        block = lax.dynamic_slice_in_dim(value, (me + distance) % n_tp * width, width, axis)
        total = total + tp_shift(block, n_tp, distance)
    return total


def tie(*values):
    return lax.optimization_barrier(values)


def ring_tables(n_req):
    lines = n_req // 4
    order = folded_ring(lines)
    following = {order[i]: order[(i + 1) % lines] for i in range(lines)}
    line_perm = [(z * 4 + p, following[z] * 4 + p) for z in range(lines) for p in range(4)]
    table = np.zeros((n_req, n_req), np.int32)
    for index in range(n_req):
        for step in range(lines):
            z = order[(order.index(index // 4) - step) % lines]
            for flip in range(4):
                table[index, step * 4 + flip] = z * 4 + ((index % 4) ^ flip)
    return lines, line_perm, table


def multiply(order, scaled, pieces, extra=None, total=None, keep=None):
    columns = pieces[0][2].shape[1]
    positions = scaled.shape[2]
    tile = 640 if columns > 640 else columns
    spec = [(slot, first, block.shape[0]) for slot, first, block in pieces]

    def body(order_ref, scaled_ref, *refs):
        refs = list(refs)
        out_ref = refs.pop()
        value = None
        if total is not None:
            value = refs.pop(0)[...]
        if keep is not None:
            keep_ref = refs.pop(0)
        if extra is not None:
            value_part = lax.dot_general(
                refs.pop(0)[...],
                refs.pop(0)[...],
                (((0,), (0,)), ((), ())),
                preferred_element_type=jnp.float32,
            )
            value = value_part if value is None else value + value_part
        for (slot, first, count), ref in zip(spec, refs):
            value_part = lax.dot_general(
                ref[...],
                scaled_ref[order_ref[slot], pl.ds(first, count), :],
                (((0,), (0,)), ((), ())),
                preferred_element_type=jnp.float32,
            )
            value = value_part if value is None else value + value_part
        if keep is not None:
            value = jnp.where(keep_ref[...] > 0, value, 0.0)
        out_ref[...] = value.astype(out_ref.dtype)

    operands = [scaled]
    specs = [pl.BlockSpec(scaled.shape, lambda i, order_ref: (0, 0, 0))]
    if total is not None:
        operands.append(total)
        specs.append(pl.BlockSpec((tile, positions), lambda i, order_ref: (i, 0)))
    if keep is not None:
        operands.append(keep)
        specs.append(pl.BlockSpec(keep.shape, lambda i, order_ref: (0, 0)))
    if extra is not None:
        operands.extend(extra)
        specs.append(pl.BlockSpec((extra[0].shape[0], tile), lambda i, order_ref: (0, i)))
        specs.append(pl.BlockSpec(extra[1].shape, lambda i, order_ref: (0, 0)))
    for _, _, block in pieces:
        operands.append(block)
        specs.append(pl.BlockSpec((block.shape[0], tile), lambda i, order_ref: (0, i)))
    depth = sum(count for _, _, count in spec) + (extra[0].shape[0] if extra is not None else 0)
    return pl.pallas_call(
        body,
        out_shape=jax.ShapeDtypeStruct(
            (columns, positions), jnp.float32 if keep is None else jnp.bfloat16
        ),
        grid_spec=pltpu.PrefetchScalarGridSpec(
            num_scalar_prefetch=1,
            grid=(pl.cdiv(columns, tile),),
            in_specs=specs,
            out_specs=pl.BlockSpec((tile, positions), lambda i, order_ref: (i, 0)),
        ),
        compiler_params=pltpu.CompilerParams(vmem_limit_bytes=40 << 20),
        cost_estimate=pl.CostEstimate(
            flops=2 * depth * columns * positions,
            bytes_accessed=2 * depth * (columns + positions) + 8 * columns * positions,
            transcendentals=0,
        ),
    )(order, *operands)


def shards(
    n_req, n_tp,
    patches, ln_gain, ln_bias, merge_weight, text_rows, norm_gain, qkv_weight, token_pos, text_len,
):
    row_count, width = text_rows.shape
    me = lax.axis_index("req")
    lines, line_perm, table = ring_tables(n_req)
    x_perm = [(i, i ^ 1) for i in range(n_req)]
    y_perm = [(i, i ^ 2) for i in range(n_req)]
    rows = qkv_weight.shape[0]
    direct = rows * 4 // 5 // 16 * 16
    cut = direct // 32 * 16 or direct // 2
    order = lax.dynamic_slice_in_dim(jnp.asarray(table), me, 1, 0).reshape(-1)

    def along_line(block):
        return lax.ppermute(block, "req", line_perm)

    def to_sides(block):
        return lax.ppermute(block, "req", x_perm), lax.ppermute(block, "req", y_perm)

    def to_corner(by_x, by_y):
        upper = lax.ppermute(by_y[:cut], "req", x_perm)
        lower = lax.ppermute(by_x[cut:], "req", y_perm)
        return upper, lower

    held = [qkv_weight[:direct]]
    sides = []
    corners = []
    held.append(along_line(held[0]))
    sides.append(to_sides(held[0]))
    gathered = lax.all_gather(qkv_weight[direct:], "req", axis=0, tiled=True)
    text_full = tp_gather(text_rows.T, n_tp, 0)

    token_count = token_pos.shape[0]
    target = lax.div(token_pos, row_count)
    same = target[:, None] == target[None, :]
    ids = jnp.arange(token_count, dtype=jnp.int32)
    before = jnp.sum((same & (ids[None, :] < ids[:, None])).astype(jnp.int32), axis=1)
    slot = target * IMG_CAP + before
    slot_count = n_req * IMG_CAP
    place = (
        jnp.arange(slot_count, dtype=jnp.int32)[:, None] == slot[None, :]
    ).astype(jnp.bfloat16)
    code = lax.rem(token_pos, row_count) + 1
    code_cols = jnp.stack([lax.div(code, 256), lax.rem(code, 256)], axis=1).astype(jnp.bfloat16)

    values = patches.astype(jnp.float32)
    sum_part = jnp.sum(values, axis=1)
    square_part = jnp.sum(values * values, axis=1)
    sum_total, square_total = lax.psum((sum_part, square_part), "tp")
    row_mean = (sum_total / DV)[:, None]
    second = (square_total / DV)[:, None]
    normed = (
        (values - row_mean)
        * lax.rsqrt(second - row_mean * row_mean + EPSILON)
        * ln_gain.astype(jnp.float32)
        + ln_bias.astype(jnp.float32)
    ).astype(jnp.bfloat16)

    normed, held[1], sides[0], place, code_cols, order = tie(
        normed, held[1], sides[0], place, code_cols, order
    )
    held.append(along_line(held[1]))
    sides.append(to_sides(held[1]))
    corners.append(to_corner(*sides[0]))

    grouped = normed.reshape(patches.shape[0] // 4, 4, patches.shape[1])
    partial_value = jnp.einsum(
        "mkf,kfd->md", grouped, merge_weight, preferred_element_type=jnp.float32
    )
    merged = tp_scatter_sum(partial_value, n_tp, 1).astype(jnp.bfloat16)
    padding = (-width - 2) % 128
    payload = jnp.concatenate(
        [merged, code_cols, jnp.zeros((token_count, padding), jnp.bfloat16)], axis=1
    )
    outgoing = jnp.dot(place, payload, preferred_element_type=jnp.float32).astype(jnp.bfloat16)

    outgoing, held[2], sides[1], corners[0] = tie(outgoing, held[2], sides[1], corners[0])
    held.append(along_line(held[2]))
    sides.append(to_sides(held[2]))
    corners.append(to_corner(*sides[1]))

    arrived = lax.all_to_all(
        outgoing.reshape(n_req, IMG_CAP, -1), "req", split_axis=0, concat_axis=0
    ).reshape(slot_count, -1)
    local = (
        arrived[:, width].astype(jnp.int32) * 256 + arrived[:, width + 1].astype(jnp.int32) - 1
    )
    hit = local[:, None] == jnp.arange(row_count, dtype=jnp.int32)[None, :]
    image_rows = tp_gather(arrived[:, :width], n_tp, 1)
    image_part = lax.dot_general(
        image_rows,
        hit.astype(jnp.bfloat16),
        (((0,), (0,)), ((), ())),
        preferred_element_type=jnp.float32,
    )
    full = jnp.where(jnp.any(hit, axis=0)[None, :], image_part, text_full.astype(jnp.float32))
    scaled = (
        full
        * lax.rsqrt(jnp.mean(full * full, axis=0, keepdims=True) + EPSILON)
        * norm_gain.astype(jnp.float32)[:, None]
    ).astype(jnp.bfloat16)

    scaled, held[3], sides[2], corners[1], gathered = tie(
        scaled, held[3], sides[2], corners[1], gathered
    )
    for step in range(3, lines):
        if step < lines - 1:
            held.append(along_line(held[step]))
        sides.append(to_sides(held[step]))
        corners.append(to_corner(*sides[step - 1]))
    blocks = scaled.reshape(n_req, rows, row_count)
    rest = blocks[:, direct:].reshape(-1, row_count)

    def pieces_of(step):
        by_x, by_y = sides[step]
        return [(step * 4, 0, held[step]), (step * 4 + 1, 0, by_x), (step * 4 + 2, 0, by_y)]

    def corner_of(step):
        upper, lower = corners[step]
        return [(step * 4 + 3, 0, upper), (step * 4 + 3, cut, lower)]

    total = multiply(
        order, blocks,
        pieces_of(0) + corner_of(0) + pieces_of(1) + corner_of(1),
        extra=(gathered, rest),
    )
    total, sides[-1], corners[-1] = tie(total, sides[-1], corners[-1])
    corners.append(to_corner(*sides[-1]))
    late = []
    for step in range(2, lines - 1):
        late += pieces_of(step) + corner_of(step)
    total = multiply(order, blocks, late + pieces_of(lines - 1), total=total)

    position = me * row_count + jnp.arange(row_count, dtype=jnp.int32)
    request_ids = jnp.arange(text_len.shape[0], dtype=jnp.int32)
    limits = jnp.sum(
        jnp.where(
            lax.div(position, SEQ)[None, :] == request_ids[:, None], text_len[:, None], 0
        ),
        axis=0,
        keepdims=True,
    )
    keep = (lax.rem(position, SEQ)[None, :] < limits).astype(jnp.int32)
    return multiply(order, blocks, corner_of(lines - 1), total=total, keep=keep).T


def solution(mesh):
    placed = (
        P("req", "tp"),
        P("tp"),
        P("tp"),
        P(None, "tp", None),
        P("req", "tp"),
        P(),
        P("req", "tp"),
        P("req"),
        P(),
    )
    body = functools.partial(shards, mesh.shape["req"], mesh.shape["tp"])
    return jax.shard_map(
        body, mesh=mesh, in_specs=placed, out_specs=P("req", "tp"), check_vma=False
    )
```

```python
import functools

import jax
import jax.numpy as jnp
import numpy as np
from jax import lax
from jax.experimental import pallas as pl
from jax.experimental.pallas import tpu as pltpu
from jax.sharding import PartitionSpec as P

DV = 1664
SEQ = 4096
IMG_CAP = 16
EPSILON = 1e-06
VMEM = 56 << 20
LIGHT = pl.CostEstimate(flops=1000, bytes_accessed=1000, transcendentals=0)


def folded_ring(count):
    odd = list(range(1, count, 2))
    even = list(range(0, count, 2))
    return even[:1] + odd + even[:0:-1]


def tp_shift(value, n_tp, distance):
    return lax.ppermute(value, "tp", [(i, (i + distance) % n_tp) for i in range(n_tp)])


def tp_scatter_sum(value, n_tp, axis):
    me = lax.axis_index("tp")
    width = value.shape[axis] // n_tp
    total = lax.dynamic_slice_in_dim(value, me * width, width, axis)
    for distance in range(1, n_tp):
        block = lax.dynamic_slice_in_dim(value, (me + distance) % n_tp * width, width, axis)
        total = total + tp_shift(block, n_tp, distance)
    return total


def ring_tables(n_req):
    lines = n_req // 4
    order = folded_ring(lines)
    following = {order[i]: order[(i + 1) % lines] for i in range(lines)}
    line_perm = [(z * 4 + p, following[z] * 4 + p) for z in range(lines) for p in range(4)]
    table = np.zeros((n_req, n_req), np.int32)
    for index in range(n_req):
        for step in range(lines):
            z = order[(order.index(index // 4) - step) % lines]
            for flip in range(4):
                table[index, step * 4 + flip] = z * 4 + ((index % 4) ^ flip)
    return lines, line_perm, table


def multiply(order, scaled, pieces, extra=None, total=None, keep=None):
    columns = pieces[0][2].shape[1]
    positions = scaled.shape[2]
    tile = 640 if columns > 640 else columns
    spec = [(slot, first, block.shape[0]) for slot, first, block in pieces]

    def body(order_ref, scaled_ref, *refs):
        refs = list(refs)
        out_ref = refs.pop()
        value = None
        if total is not None:
            value = refs.pop(0)[...]
        if keep is not None:
            keep_ref = refs.pop(0)
        if extra is not None:
            value_part = lax.dot_general(
                refs.pop(0)[...],
                refs.pop(0)[...],
                (((0,), (0,)), ((), ())),
                preferred_element_type=jnp.float32,
            )
            value = value_part if value is None else value + value_part
        for (slot, first, count), ref in zip(spec, refs):
            value_part = lax.dot_general(
                ref[...],
                scaled_ref[order_ref[slot], pl.ds(first, count), :],
                (((0,), (0,)), ((), ())),
                preferred_element_type=jnp.float32,
            )
            value = value_part if value is None else value + value_part
        if keep is not None:
            value = jnp.where(keep_ref[...] > 0, value, 0.0)
        out_ref[...] = value.astype(out_ref.dtype)

    operands = [scaled]
    specs = [pl.BlockSpec(scaled.shape, lambda i, order_ref: (0, 0, 0))]
    if total is not None:
        operands.append(total)
        specs.append(pl.BlockSpec((tile, positions), lambda i, order_ref: (i, 0)))
    if keep is not None:
        operands.append(keep)
        specs.append(pl.BlockSpec(keep.shape, lambda i, order_ref: (0, 0)))
    if extra is not None:
        operands.extend(extra)
        specs.append(pl.BlockSpec((extra[0].shape[0], tile), lambda i, order_ref: (0, i)))
        specs.append(pl.BlockSpec(extra[1].shape, lambda i, order_ref: (0, 0)))
    for _, _, block in pieces:
        operands.append(block)
        specs.append(pl.BlockSpec((block.shape[0], tile), lambda i, order_ref: (0, i)))
    return pl.pallas_call(
        body,
        out_shape=jax.ShapeDtypeStruct(
            (columns, positions), jnp.float32 if keep is None else jnp.bfloat16
        ),
        grid_spec=pltpu.PrefetchScalarGridSpec(
            num_scalar_prefetch=1,
            grid=(pl.cdiv(columns, tile),),
            in_specs=specs,
            out_specs=pl.BlockSpec((tile, positions), lambda i, order_ref: (i, 0)),
        ),
        compiler_params=pltpu.CompilerParams(vmem_limit_bytes=VMEM),
        cost_estimate=LIGHT,
    )(order, *operands)


def merge(patches, row_mean, row_scale, ln_gain, ln_bias, merge_weight):
    rows, width = patches.shape
    window, _, features = merge_weight.shape
    tokens = rows // window

    def body(patches_ref, mean_ref, scale_ref, gain_ref, bias_ref, weight_ref, out_ref, normed_ref):
        step = pl.program_id(0)

        @pl.when(step == 0)
        def _():
            normed = (patches_ref[...].astype(jnp.float32) - mean_ref[...]) * scale_ref[
                ...
            ] * gain_ref[...].astype(jnp.float32) + bias_ref[...].astype(jnp.float32)
            normed_ref[...] = normed.astype(jnp.bfloat16)
            out_ref[...] = jnp.zeros_like(out_ref)

        wanted = lax.broadcasted_iota(jnp.int32, (tokens, rows), 0) * window + step
        chosen = (lax.broadcasted_iota(jnp.int32, (tokens, rows), 1) == wanted).astype(jnp.bfloat16)
        part = jnp.dot(chosen, normed_ref[...], preferred_element_type=jnp.float32)
        out_ref[...] += jnp.dot(
            part.astype(jnp.bfloat16), weight_ref[0], preferred_element_type=jnp.float32
        )

    def whole(shape):
        return pl.BlockSpec(shape, lambda i: (0, 0))

    return pl.pallas_call(
        body,
        out_shape=jax.ShapeDtypeStruct((tokens, features), jnp.float32),
        grid=(window,),
        in_specs=[
            whole((rows, width)),
            whole((rows, 1)),
            whole((rows, 1)),
            whole((1, width)),
            whole((1, width)),
            pl.BlockSpec((1, width, features), lambda i: (i, 0, 0)),
        ],
        out_specs=whole((tokens, features)),
        scratch_shapes=[pltpu.VMEM((rows, width), jnp.bfloat16)],
        compiler_params=pltpu.CompilerParams(vmem_limit_bytes=VMEM),
        cost_estimate=LIGHT,
    )(patches, row_mean, row_scale, ln_gain[None, :], ln_bias[None, :], merge_weight)


def combine(tp_index, texts, images, norm_gain):
    n_tp = len(texts)
    width, positions = texts[0].shape
    slots = images[0].shape[0]

    def body(index_ref, gain_ref, *refs):
        text_refs, image_refs = refs[:n_tp], refs[n_tp : 2 * n_tp]
        out_ref, value_ref = refs[2 * n_tp :]
        code = image_refs[0][:, width : width + 2].astype(jnp.float32)
        local = code[:, 0:1] * 256.0 + code[:, 1:2] - 1.0
        place = lax.broadcasted_iota(jnp.int32, (slots, positions), 1).astype(jnp.float32)
        hit = jnp.where(local == place, 1.0, 0.0)
        covered = jnp.max(hit, axis=0, keepdims=True)
        hit = hit.astype(jnp.bfloat16)
        squares = jnp.zeros((1, positions), jnp.float32)
        starts = []
        for distance in range(n_tp):
            start = pl.multiple_of(
                lax.rem(index_ref[0] + n_tp - distance, n_tp) * width, 16
            )
            starts.append(start)
            image = lax.dot_general(
                image_refs[distance][...],
                hit,
                (((0,), (0,)), ((), ())),
                preferred_element_type=jnp.float32,
            )[:width]
            value = jnp.where(covered > 0.0, image, text_refs[distance][...].astype(jnp.float32))
            squares += jnp.sum(value * value, axis=0, keepdims=True)
            value_ref[pl.ds(start, width), :] = value
        scale = lax.rsqrt(squares / (width * n_tp) + EPSILON)
        out_ref[...] = (
            value_ref[...] * scale * gain_ref[...].astype(jnp.float32)
        ).astype(out_ref.dtype)

    vmem = pl.BlockSpec(memory_space=pltpu.VMEM)
    return pl.pallas_call(
        body,
        out_shape=jax.ShapeDtypeStruct((width * n_tp, positions), jnp.bfloat16),
        in_specs=[pl.BlockSpec(memory_space=pltpu.SMEM)] + [vmem] * (1 + 2 * n_tp),
        out_specs=vmem,
        scratch_shapes=[pltpu.VMEM((width * n_tp, positions), jnp.float32)],
        compiler_params=pltpu.CompilerParams(vmem_limit_bytes=VMEM),
        cost_estimate=LIGHT,
    )(tp_index, norm_gain[:, None], *texts, *images)


def shards(
    n_req, n_tp,
    patches, ln_gain, ln_bias, merge_weight, text_rows, norm_gain, qkv_weight, token_pos, text_len,
):
    row_count, width = text_rows.shape
    me = lax.axis_index("req")
    lines, line_perm, table = ring_tables(n_req)
    x_perm = [(i, i ^ 1) for i in range(n_req)]
    y_perm = [(i, i ^ 2) for i in range(n_req)]
    rows = qkv_weight.shape[0]
    cut = rows // 32 * 16 or rows // 2
    order = lax.dynamic_slice_in_dim(jnp.asarray(table), me, 1, 0).reshape(-1)

    held, sides, corners = [qkv_weight], [], []
    for step in range(lines):
        if step < lines - 1:
            held.append(lax.ppermute(held[step], "req", line_perm))
        by_x = lax.ppermute(held[step], "req", x_perm)
        by_y = lax.ppermute(held[step], "req", y_perm)
        sides.append((by_x, by_y))
        corners.append(
            (lax.ppermute(by_y[:cut], "req", x_perm), lax.ppermute(by_x[cut:], "req", y_perm))
        )
    text_turned = text_rows.T
    texts = [text_turned] + [tp_shift(text_turned, n_tp, d) for d in range(1, n_tp)]

    token_count = token_pos.shape[0]
    target = lax.div(token_pos, row_count)
    same = target[:, None] == target[None, :]
    ids = jnp.arange(token_count, dtype=jnp.int32)
    before = jnp.sum((same & (ids[None, :] < ids[:, None])).astype(jnp.int32), axis=1)
    slot = target * IMG_CAP + before
    slot_count = n_req * IMG_CAP
    place = (
        jnp.arange(slot_count, dtype=jnp.int32)[:, None] == slot[None, :]
    ).astype(jnp.bfloat16)
    code = lax.rem(token_pos, row_count) + 1
    code_cols = jnp.stack([lax.div(code, 256), lax.rem(code, 256)], axis=1).astype(jnp.bfloat16)

    values = patches.astype(jnp.float32)
    sum_part = jnp.sum(values, axis=1)
    square_part = jnp.sum(values * values, axis=1)
    sum_total, square_total = lax.psum((sum_part, square_part), "tp")
    row_mean = (sum_total / DV)[:, None]
    second = (square_total / DV)[:, None]
    row_scale = lax.rsqrt(second - row_mean * row_mean + EPSILON)
    partial_value = merge(patches, row_mean, row_scale, ln_gain, ln_bias, merge_weight)
    merged = tp_scatter_sum(partial_value, n_tp, 1).astype(jnp.bfloat16)
    padding = (-width - 2) % 128
    payload = jnp.concatenate(
        [merged, code_cols, jnp.zeros((token_count, padding), jnp.bfloat16)], axis=1
    )
    outgoing = jnp.dot(place, payload, preferred_element_type=jnp.float32).astype(jnp.bfloat16)
    arrived = lax.all_to_all(
        outgoing.reshape(n_req, IMG_CAP, -1), "req", split_axis=0, concat_axis=0
    ).reshape(slot_count, -1)
    images = [arrived] + [tp_shift(arrived, n_tp, d) for d in range(1, n_tp)]
    tp_index = lax.axis_index("tp").reshape(1)
    scaled = combine(tp_index, texts, images, norm_gain)
    blocks = scaled.reshape(n_req, rows, row_count)

    def pieces_of(step):
        by_x, by_y = sides[step]
        return [(step * 4, 0, held[step]), (step * 4 + 1, 0, by_x), (step * 4 + 2, 0, by_y)]

    def corner_of(step):
        upper, lower = corners[step]
        return [(step * 4 + 3, 0, upper), (step * 4 + 3, cut, lower)]

    early, late = [], []
    for step in range(lines - 2):
        early += pieces_of(step) + corner_of(step)
    for step in range(lines - 2, lines - 1):
        late += pieces_of(step) + corner_of(step)
    total = multiply(order, blocks, early)
    total = multiply(order, blocks, late + pieces_of(lines - 1), total=total)

    position = me * row_count + jnp.arange(row_count, dtype=jnp.int32)
    request_ids = jnp.arange(text_len.shape[0], dtype=jnp.int32)
    limits = jnp.sum(
        jnp.where(
            lax.div(position, SEQ)[None, :] == request_ids[:, None], text_len[:, None], 0
        ),
        axis=0,
        keepdims=True,
    )
    keep = (lax.rem(position, SEQ)[None, :] < limits).astype(jnp.int32)
    return multiply(order, blocks, corner_of(lines - 1), total=total, keep=keep).T


def solution(mesh):
    placed = (
        P("req", "tp"),
        P("tp"),
        P("tp"),
        P(None, "tp", None),
        P("req", "tp"),
        P(),
        P("req", "tp"),
        P("req"),
        P(),
    )
    body = functools.partial(shards, mesh.shape["req"], mesh.shape["tp"])
    return jax.shard_map(
        body, mesh=mesh, in_specs=placed, out_specs=P("req", "tp"), check_vma=False
    )
```

```python
import functools

import jax
import jax.numpy as jnp
import numpy as np
from jax import lax
from jax.experimental import pallas as pl
from jax.experimental.pallas import tpu as pltpu
from jax.sharding import PartitionSpec as P

DV = 1664
SEQ = 4096
IMG_CAP = 16
EPSILON = 1e-06
VMEM = 56 << 20
LIGHT = pl.CostEstimate(flops=1000, bytes_accessed=1000, transcendentals=0)


def folded_ring(count):
    odd = list(range(1, count, 2))
    even = list(range(0, count, 2))
    return even[:1] + odd + even[:0:-1]


def tp_shift(value, n_tp, distance):
    return lax.ppermute(value, "tp", [(i, (i + distance) % n_tp) for i in range(n_tp)])


def tp_scatter_sum(value, n_tp, axis):
    me = lax.axis_index("tp")
    width = value.shape[axis] // n_tp
    total = lax.dynamic_slice_in_dim(value, me * width, width, axis)
    for distance in range(1, n_tp):
        block = lax.dynamic_slice_in_dim(value, (me + distance) % n_tp * width, width, axis)
        total = total + tp_shift(block, n_tp, distance)
    return total


def ring_tables(n_req):
    lines = n_req // 4
    order = folded_ring(lines)
    following = {order[i]: order[(i + 1) % lines] for i in range(lines)}
    line_perm = [(z * 4 + p, following[z] * 4 + p) for z in range(lines) for p in range(4)]
    table = np.zeros((n_req, n_req), np.int32)
    for index in range(n_req):
        for step in range(lines):
            z = order[(order.index(index // 4) - step) % lines]
            for flip in range(4):
                table[index, step * 4 + flip] = z * 4 + ((index % 4) ^ flip)
    return lines, line_perm, table


def tie(*values):
    return lax.optimization_barrier(values)


def column_tile(columns):
    return 640 if columns > 640 else columns


def column_cut(columns):
    tile = column_tile(columns)
    return pl.cdiv(columns, tile) // 2 * tile


def place_rows(scratch_ref, order_ref, step, rows, pieces):
    for flip, piece in enumerate(pieces):
        start = pl.multiple_of(lax.rem(order_ref[step * 4 + flip], 4) * rows, 8)
        if piece is None:
            piece = jnp.zeros((rows, scratch_ref.shape[1]), jnp.float32)
        scratch_ref[pl.ds(start, rows), :] = piece.astype(jnp.float32)


def piece_specs(blocks, rows, tile):
    if len(blocks) == 1:
        return [pl.BlockSpec((rows, tile), lambda i, order_ref: (0, i))]
    first = blocks[0].shape[1] // tile
    return [
        pl.BlockSpec((rows, tile), lambda i, order_ref: (0, jnp.minimum(i, first - 1))),
        pl.BlockSpec((rows, tile), lambda i, order_ref: (0, jnp.maximum(i - first, 0))),
    ]


def project(order, scaled, planes, last, columns, total=None, base=None, text_len=None):
    _, positions, depth = scaled.shape
    rows = depth // 4
    tile = column_tile(columns)
    operands = [scaled]
    specs = [pl.BlockSpec(scaled.shape, lambda i, order_ref: (0, 0, 0))]
    if last:
        operands += [base, text_len, total]
        specs += [
            pl.BlockSpec(memory_space=pltpu.SMEM),
            pl.BlockSpec(memory_space=pltpu.SMEM),
            pl.BlockSpec((positions, tile), lambda i, order_ref: (0, i)),
        ]
    for _, pieces in planes:
        for piece in pieces:
            if piece is not None:
                operands += list(piece)
                specs += piece_specs(piece, rows, tile)

    def body(order_ref, scaled_ref, *refs):
        refs, out_ref, scratch_ref = list(refs[:-2]), refs[-2], refs[-1]
        column = pl.program_id(0) * tile
        if last:
            base_ref, length_ref, total_ref = refs[:3]
            refs = refs[3:]
            value = total_ref[...]
        else:
            value = jnp.zeros((positions, tile), jnp.float32)
        for step, pieces in planes:
            taken = []
            for piece in pieces:
                if piece is None:
                    taken.append(None)
                    continue
                weight = refs.pop(0)[...]
                if len(piece) == 2:
                    weight = jnp.where(column < piece[0].shape[1], weight, refs.pop(0)[...])
                taken.append(weight)
            place_rows(scratch_ref, order_ref, step, rows, taken)
            value += jnp.dot(
                scaled_ref[lax.div(order_ref[step * 4], 4)],
                scratch_ref[...].astype(jnp.bfloat16),
                preferred_element_type=jnp.float32,
            )
        if not last:
            out_ref[...] = value
            return
        position = base_ref[0] + lax.broadcasted_iota(jnp.int32, (positions, tile), 0)
        limit = jnp.zeros((positions, tile), jnp.int32)
        for request in range(text_len.shape[0]):
            limit = jnp.where(lax.div(position, SEQ) == request, length_ref[request], limit)
        there = column + lax.broadcasted_iota(jnp.int32, (positions, tile), 1) < columns
        keep = (lax.rem(position, SEQ) < limit) & there
        value = jnp.where(keep, value, 0.0).astype(jnp.bfloat16)
        for first in range(0, tile, 128):
            side = min(128, tile - first)
            identity = (
                lax.broadcasted_iota(jnp.int32, (side, side), 0)
                == lax.broadcasted_iota(jnp.int32, (side, side), 1)
            ).astype(jnp.bfloat16)
            out_ref[pl.ds(first, side), :] = lax.dot_general(
                identity,
                value[:, first : first + side],
                (((1,), (1,)), ((), ())),
                preferred_element_type=jnp.float32,
            ).astype(jnp.bfloat16)

    if last:
        out_shape = jax.ShapeDtypeStruct((columns, positions), jnp.bfloat16)
        out_spec = pl.BlockSpec((tile, positions), lambda i, order_ref: (i, 0))
    else:
        out_shape = jax.ShapeDtypeStruct((positions, columns), jnp.float32)
        out_spec = pl.BlockSpec((positions, tile), lambda i, order_ref: (0, i))
    return pl.pallas_call(
        body,
        out_shape=out_shape,
        grid_spec=pltpu.PrefetchScalarGridSpec(
            num_scalar_prefetch=1,
            grid=(pl.cdiv(columns, tile),),
            in_specs=specs,
            out_specs=out_spec,
            scratch_shapes=[pltpu.VMEM((depth, tile), jnp.float32)],
        ),
        compiler_params=pltpu.CompilerParams(vmem_limit_bytes=VMEM),
        cost_estimate=pl.CostEstimate(
            flops=2 * len(planes) * depth * columns * positions,
            bytes_accessed=2 * len(planes) * depth * columns + 6 * columns * positions,
            transcendentals=0,
        ),
    )(order, *operands)


def project_plain(order, scaled, planes, last, columns, total=None, base=None, text_len=None):
    _, positions, depth = scaled.shape
    rows = depth // 4
    if total is None:
        total = jnp.zeros((positions, columns), jnp.float32)
    for step, pieces in planes:
        source = lax.dynamic_index_in_dim(scaled, lax.div(order[step * 4], 4), 0, keepdims=False)
        for flip, piece in enumerate(pieces):
            if piece is None:
                continue
            start = lax.rem(order[step * 4 + flip], 4) * rows
            total += jnp.dot(
                lax.dynamic_slice_in_dim(source, start, rows, 1),
                jnp.concatenate(piece, axis=1),
                preferred_element_type=jnp.float32,
            )
    if not last:
        return total
    position = base[0] + jnp.arange(positions, dtype=jnp.int32)
    limit = text_len[lax.div(position, SEQ)]
    keep = lax.rem(position, SEQ) < limit
    return jnp.where(keep[:, None], total, 0.0).astype(jnp.bfloat16).T


def row_stats(patches):
    rows, _ = patches.shape

    def body(patches_ref, out_ref):
        values = patches_ref[...].astype(jnp.float32)
        sums = jnp.sum(values, axis=1, keepdims=True)
        squares = jnp.sum(values * values, axis=1, keepdims=True)
        out_ref[:, :128] = jnp.broadcast_to(sums, (rows, 128))
        out_ref[:, 128:] = jnp.broadcast_to(squares, (rows, 128))

    vmem = pl.BlockSpec(memory_space=pltpu.VMEM)
    return pl.pallas_call(
        body,
        out_shape=jax.ShapeDtypeStruct((rows, 256), jnp.float32),
        in_specs=[vmem],
        out_specs=vmem,
        compiler_params=pltpu.CompilerParams(vmem_limit_bytes=VMEM),
        cost_estimate=LIGHT,
    )(patches)


def merge(patches, stats, gain_bias, merge_weight):
    rows, width = patches.shape
    window, _, features = merge_weight.shape
    tokens = rows // window
    tile = min(features, 256)
    count = len(stats)

    def body(patches_ref, gain_bias_ref, *refs):
        stats_refs, weight_ref, out_ref, parts_ref = refs[:count], *refs[count:]

        @pl.when(pl.program_id(0) == 0)
        def _():
            sums = sum(ref[...] for ref in stats_refs) / DV
            row_mean = sums[:, 0:1]
            row_scale = lax.rsqrt(sums[:, 128:129] - row_mean * row_mean + EPSILON)
            gain_bias = gain_bias_ref[...].astype(jnp.float32)
            normed = (
                (patches_ref[...].astype(jnp.float32) - row_mean) * row_scale * gain_bias[0:1]
                + gain_bias[1:2]
            ).astype(jnp.bfloat16)
            taken = lax.broadcasted_iota(jnp.int32, (tokens, rows), 1)
            first = lax.broadcasted_iota(jnp.int32, (tokens, rows), 0) * window
            for slot in range(window):
                chosen = (taken == first + slot).astype(jnp.bfloat16)
                parts_ref[slot] = jnp.dot(
                    chosen, normed, preferred_element_type=jnp.float32
                ).astype(jnp.bfloat16)

        value = jnp.zeros((tokens, tile), jnp.float32)
        for slot in range(window):
            value += jnp.dot(
                parts_ref[slot], weight_ref[slot], preferred_element_type=jnp.float32
            )
        out_ref[...] = value

    def whole(shape):
        return pl.BlockSpec(shape, lambda i: (0, 0))

    return pl.pallas_call(
        body,
        out_shape=jax.ShapeDtypeStruct((tokens, features), jnp.float32),
        grid=(pl.cdiv(features, tile),),
        in_specs=[whole((rows, width)), whole((2, width))]
        + [whole((rows, 256))] * count
        + [pl.BlockSpec((window, width, tile), lambda i: (0, 0, i))],
        out_specs=pl.BlockSpec((tokens, tile), lambda i: (0, i)),
        scratch_shapes=[pltpu.VMEM((window, tokens, width), jnp.bfloat16)],
        compiler_params=pltpu.CompilerParams(vmem_limit_bytes=VMEM),
        cost_estimate=LIGHT,
    )(patches, gain_bias, *stats, merge_weight)


def combine(tp_index, texts, images, gain_planes):
    n_tp = len(texts)
    positions, width = texts[0].shape
    slots = images[0].shape[0]
    lines, _, depth = gain_planes.shape
    share = lines // n_tp
    corner = width // 128 * 128

    def body(index_ref, gain_ref, *refs):
        text_refs, image_refs = refs[:n_tp], refs[n_tp : 2 * n_tp]
        out_ref, value_ref = refs[2 * n_tp :]
        code = image_refs[0][:, corner : corner + 128].astype(jnp.float32).T
        high = code[width - corner : width - corner + 1]
        low = code[width - corner + 1 : width - corner + 2]
        local = high * 256.0 + low - 1.0
        place = lax.broadcasted_iota(jnp.int32, (positions, slots), 0).astype(jnp.float32)
        hit = jnp.where(local == place, 1.0, 0.0)
        covered = jnp.max(hit, axis=1, keepdims=True)
        hit = hit.astype(jnp.bfloat16)
        squares = jnp.zeros((positions, 1), jnp.float32)
        for distance in range(n_tp):
            first = lax.rem(index_ref[0] + n_tp - distance, n_tp) * share
            image = jnp.dot(hit, image_refs[distance][...], preferred_element_type=jnp.float32)
            value = jnp.where(
                covered > 0.0, image[:, :width], text_refs[distance][...].astype(jnp.float32)
            )
            squares += jnp.sum(value * value, axis=1, keepdims=True)
            for piece in range(share):
                value_ref[first + piece] = value[:, piece * depth : (piece + 1) * depth]
        scale = lax.rsqrt(squares / (width * n_tp) + EPSILON)
        for line in range(lines):
            out_ref[line] = (
                value_ref[line] * scale * gain_ref[line].astype(jnp.float32)
            ).astype(out_ref.dtype)

    vmem = pl.BlockSpec(memory_space=pltpu.VMEM)
    return pl.pallas_call(
        body,
        out_shape=jax.ShapeDtypeStruct((lines, positions, depth), jnp.bfloat16),
        in_specs=[pl.BlockSpec(memory_space=pltpu.SMEM)] + [vmem] * (1 + 2 * n_tp),
        out_specs=vmem,
        scratch_shapes=[pltpu.VMEM((lines, positions, depth), jnp.float32)],
        compiler_params=pltpu.CompilerParams(vmem_limit_bytes=VMEM),
        cost_estimate=LIGHT,
    )(tp_index, gain_planes, *texts, *images)


def shards(
    n_req, n_tp,
    patches, ln_gain, ln_bias, merge_weight, text_rows, norm_gain, qkv_weight, token_pos, text_len,
):
    row_count, width = text_rows.shape
    me = lax.axis_index("req")
    tp_index = lax.axis_index("tp").reshape(1)
    lines, line_perm, table = ring_tables(n_req)
    x_perm = [(i, i ^ 1) for i in range(n_req)]
    y_perm = [(i, i ^ 2) for i in range(n_req)]
    rows, columns = qkv_weight.shape
    cut = column_cut(columns)
    order = lax.dynamic_slice_in_dim(jnp.asarray(table), me, 1, 0).reshape(-1)

    def along_line(block):
        return lax.ppermute(block, "req", line_perm)

    def to_sides(block):
        return lax.ppermute(block, "req", x_perm), lax.ppermute(block, "req", y_perm)

    def to_corner(step):
        by_x, by_y = sides[step]
        if step >= lines - 2 and cut:
            return (
                lax.ppermute(by_y[:, :cut], "req", x_perm),
                lax.ppermute(by_x[:, cut:], "req", y_perm),
            )
        if step % 2:
            return (lax.ppermute(by_x, "req", y_perm),)
        return (lax.ppermute(by_y, "req", x_perm),)

    held = [qkv_weight]
    held.append(along_line(held[0]))
    sides = [to_sides(held[0])]
    corners = []
    stats_own = row_stats(patches)
    stats = [stats_own] + [tp_shift(stats_own, n_tp, d) for d in range(1, n_tp)]
    gain_bias = jnp.stack([ln_gain, ln_bias])
    texts = [text_rows] + [tp_shift(text_rows, n_tp, d) for d in range(1, n_tp)]

    token_count = token_pos.shape[0]
    target = lax.div(token_pos, row_count)
    same = target[:, None] == target[None, :]
    ids = jnp.arange(token_count, dtype=jnp.int32)
    before = jnp.sum((same & (ids[None, :] < ids[:, None])).astype(jnp.int32), axis=1)
    slot = target * IMG_CAP + before
    slot_count = n_req * IMG_CAP
    place = (
        jnp.arange(slot_count, dtype=jnp.int32)[:, None] == slot[None, :]
    ).astype(jnp.bfloat16)
    code = lax.rem(token_pos, row_count) + 1
    code_cols = jnp.stack([lax.div(code, 256), lax.rem(code, 256)], axis=1).astype(jnp.bfloat16)
    gain_planes = norm_gain.reshape(lines, 1, 4 * rows)

    stats, held[1], sides[0], gain_bias, gain_planes = tie(
        stats, held[1], sides[0], gain_bias, gain_planes
    )
    held.append(along_line(held[1]))
    sides.append(to_sides(held[1]))
    corners.append(to_corner(0))
    partial_value = merge(patches, stats, gain_bias, merge_weight)

    partial_value, held[2], sides[1] = tie(partial_value, held[2], sides[1])
    held.append(along_line(held[2]))
    sides.append(to_sides(held[2]))
    corners.append(to_corner(1))
    merged = tp_scatter_sum(partial_value, n_tp, 1).astype(jnp.bfloat16)
    padding = (-width - 2) % 128
    payload = jnp.concatenate(
        [merged, code_cols, jnp.zeros((token_count, padding), jnp.bfloat16)], axis=1
    )
    outgoing = jnp.dot(place, payload, preferred_element_type=jnp.float32).astype(jnp.bfloat16)

    outgoing, held[3], sides[2], texts = tie(outgoing, held[3], sides[2], texts)
    sides.append(to_sides(held[3]))
    arrived = lax.all_to_all(
        outgoing.reshape(n_req, IMG_CAP, -1), "req", split_axis=0, concat_axis=0
    ).reshape(slot_count, -1)

    arrived, sides[3], corners = tie(arrived, sides[3], corners)
    for step in range(4, lines):
        held.append(along_line(held[step - 1]))
        sides.append(to_sides(held[step]))
    for step in range(2, lines):
        corners.append(to_corner(step))
    images = [arrived] + [tp_shift(arrived, n_tp, d) for d in range(1, n_tp)]
    scaled = combine(tp_index, texts, images, gain_planes)

    early, late = [], []
    for step in range(lines):
        pieces = [(held[step],), (sides[step][0],), (sides[step][1],)]
        if step < lines - 2:
            early.append((step, pieces + [corners[step]]))
        else:
            early.append((step, pieces + [None]))
            late.append((step, [None, None, None, corners[step]]))
    run = project if rows % 8 == 0 else project_plain
    total = run(order, scaled, early, False, columns)
    base = (me * row_count).reshape(1)
    return run(order, scaled, late, True, columns, total=total, base=base, text_len=text_len).T


def solution(mesh):
    placed = (
        P("req", "tp"),
        P("tp"),
        P("tp"),
        P(None, "tp", None),
        P("req", "tp"),
        P(),
        P("req", "tp"),
        P("req"),
        P(),
    )
    body = functools.partial(shards, mesh.shape["req"], mesh.shape["tp"])
    return jax.shard_map(
        body, mesh=mesh, in_specs=placed, out_specs=P("req", "tp"), check_vma=False
    )
```

```python
import functools

import jax
import jax.numpy as jnp
import numpy as np
from jax import lax
from jax.experimental import pallas as pl
from jax.experimental.pallas import tpu as pltpu
from jax.sharding import PartitionSpec as P

DV = 1664
SEQ = 4096
IMG_CAP = 16
EPSILON = 1e-06
VMEM = 32 << 20
LIGHT = pl.CostEstimate(flops=1000, bytes_accessed=1000, transcendentals=0)


def folded_ring(count):
    odd = list(range(1, count, 2))
    even = list(range(0, count, 2))
    return even[:1] + odd + even[:0:-1]


def tp_shift(value, n_tp, distance):
    return lax.ppermute(value, "tp", [(i, (i + distance) % n_tp) for i in range(n_tp)])


def tp_scatter_sum(value, n_tp, axis):
    me = lax.axis_index("tp")
    width = value.shape[axis] // n_tp
    total = lax.dynamic_slice_in_dim(value, me * width, width, axis)
    for distance in range(1, n_tp):
        block = lax.dynamic_slice_in_dim(value, (me + distance) % n_tp * width, width, axis)
        total = total + tp_shift(block, n_tp, distance)
    return total


def ring_tables(n_req):
    lines = n_req // 4
    order = folded_ring(lines)
    following = {order[i]: order[(i + 1) % lines] for i in range(lines)}
    line_perm = [(z * 4 + p, following[z] * 4 + p) for z in range(lines) for p in range(4)]
    table = np.zeros((n_req, n_req), np.int32)
    for index in range(n_req):
        for step in range(lines):
            z = order[(order.index(index // 4) - step) % lines]
            for flip in range(4):
                table[index, step * 4 + flip] = z * 4 + ((index % 4) ^ flip)
    return lines, line_perm, table


def tie(*values):
    return lax.optimization_barrier(values)


def row_stats(patches):
    rows, _ = patches.shape

    def body(patches_ref, out_ref):
        values = patches_ref[...].astype(jnp.float32)
        sums = jnp.sum(values, axis=1, keepdims=True)
        squares = jnp.sum(values * values, axis=1, keepdims=True)
        out_ref[:, :128] = jnp.broadcast_to(sums, (rows, 128))
        out_ref[:, 128:] = jnp.broadcast_to(squares, (rows, 128))

    vmem = pl.BlockSpec(memory_space=pltpu.VMEM)
    return pl.pallas_call(
        body,
        out_shape=jax.ShapeDtypeStruct((rows, 256), jnp.float32),
        in_specs=[vmem],
        out_specs=vmem,
        compiler_params=pltpu.CompilerParams(vmem_limit_bytes=VMEM),
        cost_estimate=LIGHT,
    )(patches)


def merge(patches, stats, gain_bias, merge_weight):
    rows, width = patches.shape
    window, _, features = merge_weight.shape
    tokens = rows // window
    count = len(stats)

    def body(patches_ref, gain_bias_ref, *refs):
        stats_refs, (weight_ref, out_ref, normed_ref) = refs[:count], refs[count:]
        step = pl.program_id(0)

        @pl.when(step == 0)
        def _():
            sums = sum(ref[...] for ref in stats_refs) / DV
            row_mean = sums[:, 0:1]
            row_scale = lax.rsqrt(sums[:, 128:129] - row_mean * row_mean + EPSILON)
            gain_bias = gain_bias_ref[...].astype(jnp.float32)
            normed_ref[...] = (
                (patches_ref[...].astype(jnp.float32) - row_mean) * row_scale * gain_bias[0:1]
                + gain_bias[1:2]
            ).astype(jnp.bfloat16)
            out_ref[...] = jnp.zeros_like(out_ref)

        wanted = lax.broadcasted_iota(jnp.int32, (tokens, rows), 0) * window + step
        chosen = (lax.broadcasted_iota(jnp.int32, (tokens, rows), 1) == wanted).astype(jnp.bfloat16)
        part = jnp.dot(chosen, normed_ref[...], preferred_element_type=jnp.float32)
        out_ref[...] += jnp.dot(
            part.astype(jnp.bfloat16), weight_ref[0], preferred_element_type=jnp.float32
        )

    def whole(shape):
        return pl.BlockSpec(shape, lambda i: (0, 0))

    return pl.pallas_call(
        body,
        out_shape=jax.ShapeDtypeStruct((tokens, features), jnp.float32),
        grid=(window,),
        in_specs=[whole((rows, width)), whole((2, width))]
        + [whole((rows, 256))] * count
        + [pl.BlockSpec((1, width, features), lambda i: (i, 0, 0))],
        out_specs=whole((tokens, features)),
        scratch_shapes=[pltpu.VMEM((rows, width), jnp.bfloat16)],
        compiler_params=pltpu.CompilerParams(vmem_limit_bytes=VMEM),
        cost_estimate=LIGHT,
    )(patches, gain_bias, *stats, merge_weight)


def combine(tp_index, texts, images, gain_column):
    n_tp = len(texts)
    width, positions = texts[0].shape
    slots = images[0].shape[0]

    def body(index_ref, gain_ref, *refs):
        text_refs, image_refs = refs[:n_tp], refs[n_tp : 2 * n_tp]
        out_ref, value_ref = refs[2 * n_tp :]
        code = image_refs[0][:, width : width + 2].astype(jnp.float32)
        local = code[:, 0:1] * 256.0 + code[:, 1:2] - 1.0
        place = lax.broadcasted_iota(jnp.int32, (slots, positions), 1).astype(jnp.float32)
        hit = jnp.where(local == place, 1.0, 0.0)
        covered = jnp.max(hit, axis=0, keepdims=True)
        hit = hit.astype(jnp.bfloat16)
        squares = jnp.zeros((1, positions), jnp.float32)
        starts = []
        for distance in range(n_tp):
            start = pl.multiple_of(
                lax.rem(index_ref[0] + n_tp - distance, n_tp) * width, 16
            )
            starts.append(start)
            image = lax.dot_general(
                image_refs[distance][...],
                hit,
                (((0,), (0,)), ((), ())),
                preferred_element_type=jnp.float32,
            )[:width]
            value = jnp.where(covered > 0.0, image, text_refs[distance][...].astype(jnp.float32))
            squares += jnp.sum(value * value, axis=0, keepdims=True)
            value_ref[pl.ds(start, width), :] = value
        scale = lax.rsqrt(squares / (width * n_tp) + EPSILON)
        out_ref[...] = (
            value_ref[...] * scale * gain_ref[...].astype(jnp.float32)
        ).astype(out_ref.dtype)

    vmem = pl.BlockSpec(memory_space=pltpu.VMEM)
    return pl.pallas_call(
        body,
        out_shape=jax.ShapeDtypeStruct((width * n_tp, positions), jnp.bfloat16),
        in_specs=[pl.BlockSpec(memory_space=pltpu.SMEM)] + [vmem] * (1 + 2 * n_tp),
        out_specs=vmem,
        scratch_shapes=[pltpu.VMEM((width * n_tp, positions), jnp.float32)],
        compiler_params=pltpu.CompilerParams(vmem_limit_bytes=VMEM),
        cost_estimate=LIGHT,
    )(tp_index, gain_column, *texts, *images)


def shards(
    n_req, n_tp,
    patches, ln_gain, ln_bias, merge_weight, text_rows, norm_gain, qkv_weight, token_pos, text_len,
):
    row_count, width = text_rows.shape
    me = lax.axis_index("req")
    tp_index = lax.axis_index("tp").reshape(1)
    lines, line_perm, table = ring_tables(n_req)
    x_perm = [(i, i ^ 1) for i in range(n_req)]
    y_perm = [(i, i ^ 2) for i in range(n_req)]
    rows, columns = qkv_weight.shape
    cut = (columns + 255) // 256 * 128
    order = lax.dynamic_slice_in_dim(jnp.asarray(table), me, 1, 0).reshape(-1)

    def along_line(block):
        return lax.ppermute(block, "req", line_perm)

    def to_sides(block):
        return lax.ppermute(block, "req", x_perm), lax.ppermute(block, "req", y_perm)

    def to_corner(by_x, by_y):
        left = lax.ppermute(by_y[:, :cut], "req", x_perm)
        right = lax.ppermute(by_x[:, cut:], "req", y_perm)
        return jnp.concatenate([left, right], axis=1)

    held = [qkv_weight]
    held.append(along_line(held[0]))
    sides = [to_sides(held[0])]
    corners = []
    stats_own = row_stats(patches)
    stats = [stats_own] + [tp_shift(stats_own, n_tp, d) for d in range(1, n_tp)]
    gain_bias = jnp.stack([ln_gain, ln_bias])
    text_turned = text_rows.T
    texts = [text_turned] + [tp_shift(text_turned, n_tp, d) for d in range(1, n_tp)]

    token_count = token_pos.shape[0]
    target = lax.div(token_pos, row_count)
    same = target[:, None] == target[None, :]
    ids = jnp.arange(token_count, dtype=jnp.int32)
    before = jnp.sum((same & (ids[None, :] < ids[:, None])).astype(jnp.int32), axis=1)
    slot = target * IMG_CAP + before
    slot_count = n_req * IMG_CAP
    place = (
        jnp.arange(slot_count, dtype=jnp.int32)[:, None] == slot[None, :]
    ).astype(jnp.bfloat16)
    code = lax.rem(token_pos, row_count) + 1
    code_cols = jnp.stack([lax.div(code, 256), lax.rem(code, 256)], axis=1).astype(jnp.bfloat16)
    gain_column = norm_gain[:, None]

    stats, held[1], sides[0], gain_bias, gain_column, order = tie(
        stats, held[1], sides[0], gain_bias, gain_column, order
    )
    held.append(along_line(held[1]))
    sides.append(to_sides(held[1]))
    corners.append(to_corner(*sides[0]))
    partial_value = merge(patches, stats, gain_bias, merge_weight)

    partial_value, held[2], sides[1] = tie(partial_value, held[2], sides[1])
    held.append(along_line(held[2]))
    sides.append(to_sides(held[2]))
    corners.append(along_line(corners[0]))
    merged = tp_scatter_sum(partial_value, n_tp, 1).astype(jnp.bfloat16)
    padding = (-width - 2) % 128
    payload = jnp.concatenate(
        [merged, code_cols, jnp.zeros((token_count, padding), jnp.bfloat16)], axis=1
    )
    outgoing = jnp.dot(place, payload, preferred_element_type=jnp.float32).astype(jnp.bfloat16)
    arrived = lax.all_to_all(
        outgoing.reshape(n_req, IMG_CAP, -1), "req", split_axis=0, concat_axis=0
    ).reshape(slot_count, -1)

    def group(step, corner=True):
        pieces = [held[step], *sides[step]] + ([corners[step]] if corner else [])
        return jnp.concatenate(pieces, axis=0)

    first_group = group(0)
    arrived, held[3], sides[2], texts, first_group = tie(
        arrived, held[3], sides[2], texts, first_group
    )
    sides.append(to_sides(held[3]))
    corners.append(along_line(corners[1]))
    images = [arrived] + [tp_shift(arrived, n_tp, d) for d in range(1, n_tp)]
    scaled = combine(tp_index, texts, images, gain_column)
    scaled, sides[3], corners[1] = tie(scaled, sides[3], corners[1])

    for step in range(4, lines):
        held.append(along_line(held[step - 1]))
        sides.append(to_sides(held[step]))
        corners.append(along_line(corners[step - 2]))
    corners.append(to_corner(*sides[-1]))

    blocks = scaled.reshape(n_req, rows, row_count)

    def rows_of(step, flips):
        return jnp.concatenate(
            [
                lax.dynamic_index_in_dim(blocks, order[step * 4 + flip], 0, keepdims=False)
                for flip in flips
            ],
            axis=0,
        )

    def product(source, weight):
        source, weight = tie(source, weight)
        return lax.dot_general(
            source, weight, (((0,), (0,)), ((), ())), preferred_element_type=jnp.float32
        )

    total = product(rows_of(0, range(4)), first_group)
    for step in range(1, lines - 1):
        total += product(rows_of(step, range(4)), group(step))
    total += product(rows_of(lines - 1, range(3)), group(lines - 1, False))
    total, corners[-1] = tie(total, corners[-1])

    position = me * row_count + jnp.arange(row_count, dtype=jnp.int32)
    request_ids = jnp.arange(text_len.shape[0], dtype=jnp.int32)
    limits = jnp.sum(
        jnp.where(
            lax.div(position, SEQ)[:, None] == request_ids[None, :], text_len[None, :], 0
        ),
        axis=1,
    )
    keep = lax.rem(position, SEQ) < limits
    total += product(rows_of(lines - 1, [3]), corners[lines - 1])
    return jnp.where(keep[:, None], total, 0.0).astype(jnp.bfloat16)


def solution(mesh):
    placed = (
        P("req", "tp"),
        P("tp"),
        P("tp"),
        P(None, "tp", None),
        P("req", "tp"),
        P(),
        P("req", "tp"),
        P("req"),
        P(),
    )
    body = functools.partial(shards, mesh.shape["req"], mesh.shape["tp"])
    return jax.shard_map(
        body, mesh=mesh, in_specs=placed, out_specs=P("req", "tp"), check_vma=False
    )
```

```python
import functools

import jax
import jax.numpy as jnp
import numpy as np
from jax import lax
from jax.experimental import pallas as pl
from jax.experimental.pallas import tpu as pltpu
from jax.sharding import PartitionSpec as P

DV = 1664
SEQ = 4096
IMG_CAP = 16
EPSILON = 1e-06
VMEM = 32 << 20
LIGHT = pl.CostEstimate(flops=1000, bytes_accessed=1000, transcendentals=0)


def folded_ring(count):
    odd = list(range(1, count, 2))
    even = list(range(0, count, 2))
    return even[:1] + odd + even[:0:-1]


def tp_shift(value, n_tp, distance):
    return lax.ppermute(value, "tp", [(i, (i + distance) % n_tp) for i in range(n_tp)])


def tp_scatter_sum(value, n_tp, axis):
    me = lax.axis_index("tp")
    width = value.shape[axis] // n_tp
    total = lax.dynamic_slice_in_dim(value, me * width, width, axis)
    for distance in range(1, n_tp):
        block = lax.dynamic_slice_in_dim(value, (me + distance) % n_tp * width, width, axis)
        total = total + tp_shift(block, n_tp, distance)
    return total


def ring_tables(n_req):
    lines = n_req // 4
    order = folded_ring(lines)
    following = {order[i]: order[(i + 1) % lines] for i in range(lines)}
    line_perm = [(z * 4 + p, following[z] * 4 + p) for z in range(lines) for p in range(4)]
    table = np.zeros((n_req, n_req), np.int32)
    for index in range(n_req):
        for step in range(lines):
            z = order[(order.index(index // 4) - step) % lines]
            for flip in range(4):
                table[index, step * 4 + flip] = z * 4 + ((index % 4) ^ flip)
    return lines, line_perm, table


def tie(*values):
    return lax.optimization_barrier(values)


def row_stats(patches):
    rows, _ = patches.shape

    def body(patches_ref, out_ref):
        values = patches_ref[...].astype(jnp.float32)
        sums = jnp.sum(values, axis=1, keepdims=True)
        squares = jnp.sum(values * values, axis=1, keepdims=True)
        out_ref[:, :128] = jnp.broadcast_to(sums, (rows, 128))
        out_ref[:, 128:] = jnp.broadcast_to(squares, (rows, 128))

    vmem = pl.BlockSpec(memory_space=pltpu.VMEM)
    return pl.pallas_call(
        body,
        out_shape=jax.ShapeDtypeStruct((rows, 256), jnp.float32),
        in_specs=[vmem],
        out_specs=vmem,
        compiler_params=pltpu.CompilerParams(vmem_limit_bytes=VMEM),
        cost_estimate=LIGHT,
    )(patches)


def merge(patches, stats, gain_bias, merge_weight):
    rows, width = patches.shape
    window, _, features = merge_weight.shape
    tokens = rows // window
    count = len(stats)

    def body(patches_ref, gain_bias_ref, *refs):
        stats_refs, (weight_ref, out_ref, normed_ref) = refs[:count], refs[count:]
        step = pl.program_id(0)

        @pl.when(step == 0)
        def _():
            sums = sum(ref[...] for ref in stats_refs) / DV
            row_mean = sums[:, 0:1]
            row_scale = lax.rsqrt(sums[:, 128:129] - row_mean * row_mean + EPSILON)
            gain_bias = gain_bias_ref[...].astype(jnp.float32)
            normed_ref[...] = (
                (patches_ref[...].astype(jnp.float32) - row_mean) * row_scale * gain_bias[0:1]
                + gain_bias[1:2]
            ).astype(jnp.bfloat16)
            out_ref[...] = jnp.zeros_like(out_ref)

        wanted = lax.broadcasted_iota(jnp.int32, (tokens, rows), 0) * window + step
        chosen = (lax.broadcasted_iota(jnp.int32, (tokens, rows), 1) == wanted).astype(jnp.bfloat16)
        part = jnp.dot(chosen, normed_ref[...], preferred_element_type=jnp.float32)
        out_ref[...] += jnp.dot(
            part.astype(jnp.bfloat16), weight_ref[0], preferred_element_type=jnp.float32
        )

    def whole(shape):
        return pl.BlockSpec(shape, lambda i: (0, 0))

    return pl.pallas_call(
        body,
        out_shape=jax.ShapeDtypeStruct((tokens, features), jnp.float32),
        grid=(window,),
        in_specs=[whole((rows, width)), whole((2, width))]
        + [whole((rows, 256))] * count
        + [pl.BlockSpec((1, width, features), lambda i: (i, 0, 0))],
        out_specs=whole((tokens, features)),
        scratch_shapes=[pltpu.VMEM((rows, width), jnp.bfloat16)],
        compiler_params=pltpu.CompilerParams(vmem_limit_bytes=VMEM),
        cost_estimate=LIGHT,
    )(patches, gain_bias, *stats, merge_weight)


def combine(tp_index, order, texts, images, gain_column):
    n_tp = len(texts)
    width, positions = texts[0].shape
    slots = images[0].shape[0]
    count = order.shape[0]
    rows = width * n_tp // count
    share = width // rows

    def body(index_ref, order_ref, gain_ref, *refs):
        text_refs, image_refs = refs[:n_tp], refs[n_tp : 2 * n_tp]
        out_ref, value_ref = refs[2 * n_tp :]
        code = image_refs[0][:, width : width + 2].astype(jnp.float32)
        local = code[:, 0:1] * 256.0 + code[:, 1:2] - 1.0
        place = lax.broadcasted_iota(jnp.int32, (slots, positions), 1).astype(jnp.float32)
        hit = jnp.where(local == place, 1.0, 0.0)
        covered = jnp.max(hit, axis=0, keepdims=True)
        hit = hit.astype(jnp.bfloat16)
        squares = jnp.zeros((1, positions), jnp.float32)
        for distance in range(n_tp):
            first = lax.rem(index_ref[0] + n_tp - distance, n_tp) * share
            image = lax.dot_general(
                image_refs[distance][...],
                hit,
                (((0,), (0,)), ((), ())),
                preferred_element_type=jnp.float32,
            )[:width]
            value = jnp.where(covered > 0.0, image, text_refs[distance][...].astype(jnp.float32))
            squares += jnp.sum(value * value, axis=0, keepdims=True)
            for block in range(share):
                value_ref[first + block] = value[block * rows : (block + 1) * rows]
        scale = lax.rsqrt(squares / (width * n_tp) + EPSILON)
        for block in range(count):
            source = order_ref[block]
            gain = gain_ref[source].astype(jnp.float32)
            out_ref[block] = (value_ref[source] * scale * gain).astype(out_ref.dtype)

    vmem = pl.BlockSpec(memory_space=pltpu.VMEM)
    smem = pl.BlockSpec(memory_space=pltpu.SMEM)
    return pl.pallas_call(
        body,
        out_shape=jax.ShapeDtypeStruct((count, rows, positions), jnp.bfloat16),
        in_specs=[smem, smem] + [vmem] * (1 + 2 * n_tp),
        out_specs=vmem,
        scratch_shapes=[pltpu.VMEM((count, rows, positions), jnp.float32)],
        compiler_params=pltpu.CompilerParams(vmem_limit_bytes=VMEM),
        cost_estimate=LIGHT,
    )(tp_index, order, gain_column, *texts, *images)


def shards(
    n_req, n_tp,
    patches, ln_gain, ln_bias, merge_weight, text_rows, norm_gain, qkv_weight, token_pos, text_len,
):
    row_count, width = text_rows.shape
    me = lax.axis_index("req")
    tp_index = lax.axis_index("tp").reshape(1)
    lines, line_perm, table = ring_tables(n_req)
    x_perm = [(i, i ^ 1) for i in range(n_req)]
    y_perm = [(i, i ^ 2) for i in range(n_req)]
    rows, columns = qkv_weight.shape
    cut = (columns + 255) // 256 * 128
    order = lax.dynamic_slice_in_dim(jnp.asarray(table), me, 1, 0).reshape(-1)

    def along_line(block):
        return lax.ppermute(block, "req", line_perm)

    def to_sides(block):
        return lax.ppermute(block, "req", x_perm), lax.ppermute(block, "req", y_perm)

    def to_corner(by_x, by_y):
        left = lax.ppermute(by_y[:, :cut], "req", x_perm)
        right = lax.ppermute(by_x[:, cut:], "req", y_perm)
        return jnp.concatenate([left, right], axis=1)

    held = [qkv_weight]
    held.append(along_line(held[0]))
    sides = [to_sides(held[0])]
    corners = []
    stats_own = row_stats(patches)
    stats = [stats_own] + [tp_shift(stats_own, n_tp, d) for d in range(1, n_tp)]
    gain_bias = jnp.stack([ln_gain, ln_bias])
    text_turned = text_rows.T
    texts = [text_turned] + [tp_shift(text_turned, n_tp, d) for d in range(1, n_tp)]

    token_count = token_pos.shape[0]
    target = lax.div(token_pos, row_count)
    same = target[:, None] == target[None, :]
    ids = jnp.arange(token_count, dtype=jnp.int32)
    before = jnp.sum((same & (ids[None, :] < ids[:, None])).astype(jnp.int32), axis=1)
    slot = target * IMG_CAP + before
    slot_count = n_req * IMG_CAP
    place = (
        jnp.arange(slot_count, dtype=jnp.int32)[:, None] == slot[None, :]
    ).astype(jnp.bfloat16)
    code = lax.rem(token_pos, row_count) + 1
    code_cols = jnp.stack([lax.div(code, 256), lax.rem(code, 256)], axis=1).astype(jnp.bfloat16)
    gain_column = norm_gain.reshape(n_req, rows, 1)

    stats, held[1], sides[0], gain_bias, gain_column, order = tie(
        stats, held[1], sides[0], gain_bias, gain_column, order
    )
    held.append(along_line(held[1]))
    sides.append(to_sides(held[1]))
    corners.append(to_corner(*sides[0]))
    partial_value = merge(patches, stats, gain_bias, merge_weight)

    partial_value, held[2], sides[1] = tie(partial_value, held[2], sides[1])
    held.append(along_line(held[2]))
    sides.append(to_sides(held[2]))
    merged = tp_scatter_sum(partial_value, n_tp, 1).astype(jnp.bfloat16)
    padding = (-width - 2) % 128
    payload = jnp.concatenate(
        [merged, code_cols, jnp.zeros((token_count, padding), jnp.bfloat16)], axis=1
    )
    outgoing = jnp.dot(place, payload, preferred_element_type=jnp.float32).astype(jnp.bfloat16)

    def group(step, corner=True):
        pieces = [held[step], *sides[step]] + ([corners[step]] if corner else [])
        return jnp.concatenate(pieces, axis=0)

    first_group = group(0)

    outgoing, held[3], sides[2], corners[0], texts, first_group = tie(
        outgoing, held[3], sides[2], corners[0], texts, first_group
    )
    sides.append(to_sides(held[3]))
    corners.append(along_line(corners[0]))
    corners.append(to_corner(*sides[2]))
    arrived = lax.all_to_all(
        outgoing.reshape(n_req, IMG_CAP, -1), "req", split_axis=0, concat_axis=0
    ).reshape(slot_count, -1)
    images = [arrived] + [tp_shift(arrived, n_tp, d) for d in range(1, n_tp)]
    blocks = combine(tp_index, order, texts, images, gain_column)

    def product(first, count, weight):
        source = blocks[first : first + count].reshape(count * rows, row_count)
        weight, source = tie(weight, source)
        return lax.dot_general(
            source, weight, (((0,), (0,)), ((), ())), preferred_element_type=jnp.float32
        )

    total = product(0, 4, first_group) + product(4, 4, group(1))

    total, sides[3] = tie(total, sides[3])
    for step in range(4, lines):
        held.append(along_line(held[step - 1]))
        sides.append(to_sides(held[step]))
        corners.append(to_corner(*sides[step - 1]))
    corners.append(to_corner(*sides[-1]))
    for step in range(2, lines - 1):
        total += product(step * 4, 4, group(step))
    total += product(lines * 4 - 4, 3, group(lines - 1, False))
    total, corners[-1] = tie(total, corners[-1])

    position = me * row_count + jnp.arange(row_count, dtype=jnp.int32)
    request_ids = jnp.arange(text_len.shape[0], dtype=jnp.int32)
    limits = jnp.sum(
        jnp.where(
            lax.div(position, SEQ)[:, None] == request_ids[None, :], text_len[None, :], 0
        ),
        axis=1,
    )
    keep = lax.rem(position, SEQ) < limits
    total += product(lines * 4 - 1, 1, corners[-1])
    return jnp.where(keep[:, None], total, 0.0).astype(jnp.bfloat16)


def solution(mesh):
    placed = (
        P("req", "tp"),
        P("tp"),
        P("tp"),
        P(None, "tp", None),
        P("req", "tp"),
        P(),
        P("req", "tp"),
        P("req"),
        P(),
    )
    body = functools.partial(shards, mesh.shape["req"], mesh.shape["tp"])
    return jax.shard_map(
        body, mesh=mesh, in_specs=placed, out_specs=P("req", "tp"), check_vma=False
    )
```

```python
import functools

import jax
import jax.numpy as jnp
import numpy as np
from jax import lax
from jax.experimental import pallas as pl
from jax.experimental.pallas import tpu as pltpu
from jax.sharding import PartitionSpec as P

DV = 1664
SEQ = 4096
IMG_CAP = 16
EPSILON = 1e-06
VMEM = 32 << 20
LIGHT = pl.CostEstimate(flops=1000, bytes_accessed=1000, transcendentals=0)


def folded_ring(count):
    odd = list(range(1, count, 2))
    even = list(range(0, count, 2))
    return even[:1] + odd + even[:0:-1]


def tp_shift(value, n_tp, distance):
    return lax.ppermute(value, "tp", [(i, (i + distance) % n_tp) for i in range(n_tp)])


def tp_scatter_sum(value, n_tp, axis):
    me = lax.axis_index("tp")
    width = value.shape[axis] // n_tp
    total = lax.dynamic_slice_in_dim(value, me * width, width, axis)
    for distance in range(1, n_tp):
        block = lax.dynamic_slice_in_dim(value, (me + distance) % n_tp * width, width, axis)
        total = total + tp_shift(block, n_tp, distance)
    return total


def ring_tables(n_req):
    lines = n_req // 4
    order = folded_ring(lines)
    following = {order[i]: order[(i + 1) % lines] for i in range(lines)}
    line_perm = [(z * 4 + p, following[z] * 4 + p) for z in range(lines) for p in range(4)]
    table = np.zeros((n_req, n_req), np.int32)
    for index in range(n_req):
        for step in range(lines):
            z = order[(order.index(index // 4) - step) % lines]
            for flip in range(4):
                table[index, step * 4 + flip] = z * 4 + ((index % 4) ^ flip)
    return lines, line_perm, table


def tie(*values):
    return lax.optimization_barrier(values)


def row_stats(patches):
    rows, _ = patches.shape

    def body(patches_ref, out_ref):
        values = patches_ref[...].astype(jnp.float32)
        sums = jnp.sum(values, axis=1, keepdims=True)
        squares = jnp.sum(values * values, axis=1, keepdims=True)
        out_ref[:, :128] = jnp.broadcast_to(sums, (rows, 128))
        out_ref[:, 128:] = jnp.broadcast_to(squares, (rows, 128))

    vmem = pl.BlockSpec(memory_space=pltpu.VMEM)
    return pl.pallas_call(
        body,
        out_shape=jax.ShapeDtypeStruct((rows, 256), jnp.float32),
        in_specs=[vmem],
        out_specs=vmem,
        compiler_params=pltpu.CompilerParams(vmem_limit_bytes=VMEM),
        cost_estimate=LIGHT,
    )(patches)


def merge(patches, stats, gain_bias, merge_weight):
    rows, width = patches.shape
    window, _, features = merge_weight.shape
    tokens = rows // window
    count = len(stats)

    def body(patches_ref, gain_bias_ref, *refs):
        stats_refs, (weight_ref, out_ref, normed_ref) = refs[:count], refs[count:]
        step = pl.program_id(0)

        @pl.when(step == 0)
        def _():
            sums = sum(ref[...] for ref in stats_refs) / DV
            row_mean = sums[:, 0:1]
            row_scale = lax.rsqrt(sums[:, 128:129] - row_mean * row_mean + EPSILON)
            gain_bias = gain_bias_ref[...].astype(jnp.float32)
            normed_ref[...] = (
                (patches_ref[...].astype(jnp.float32) - row_mean) * row_scale * gain_bias[0:1]
                + gain_bias[1:2]
            ).astype(jnp.bfloat16)
            out_ref[...] = jnp.zeros_like(out_ref)

        wanted = lax.broadcasted_iota(jnp.int32, (tokens, rows), 0) * window + step
        chosen = (lax.broadcasted_iota(jnp.int32, (tokens, rows), 1) == wanted).astype(jnp.bfloat16)
        part = jnp.dot(chosen, normed_ref[...], preferred_element_type=jnp.float32)
        out_ref[...] += jnp.dot(
            part.astype(jnp.bfloat16), weight_ref[0], preferred_element_type=jnp.float32
        )

    def whole(shape):
        return pl.BlockSpec(shape, lambda i: (0, 0))

    return pl.pallas_call(
        body,
        out_shape=jax.ShapeDtypeStruct((tokens, features), jnp.float32),
        grid=(window,),
        in_specs=[whole((rows, width)), whole((2, width))]
        + [whole((rows, 256))] * count
        + [pl.BlockSpec((1, width, features), lambda i: (i, 0, 0))],
        out_specs=whole((tokens, features)),
        scratch_shapes=[pltpu.VMEM((rows, width), jnp.bfloat16)],
        compiler_params=pltpu.CompilerParams(vmem_limit_bytes=VMEM),
        cost_estimate=LIGHT,
    )(patches, gain_bias, *stats, merge_weight)


def combine(tp_index, order, texts, images, gain_column):
    n_tp = len(texts)
    width, positions = texts[0].shape
    slots = images[0].shape[0]
    count = order.shape[0]
    rows = width * n_tp // count
    share = width // rows

    def body(index_ref, order_ref, gain_ref, *refs):
        text_refs, image_refs = refs[:n_tp], refs[n_tp : 2 * n_tp]
        out_ref, value_ref = refs[2 * n_tp :]
        code = image_refs[0][:, width : width + 2].astype(jnp.float32)
        local = code[:, 0:1] * 256.0 + code[:, 1:2] - 1.0
        place = lax.broadcasted_iota(jnp.int32, (slots, positions), 1).astype(jnp.float32)
        hit = jnp.where(local == place, 1.0, 0.0)
        covered = jnp.max(hit, axis=0, keepdims=True)
        hit = hit.astype(jnp.bfloat16)
        squares = jnp.zeros((1, positions), jnp.float32)
        for distance in range(n_tp):
            first = lax.rem(index_ref[0] + n_tp - distance, n_tp) * share
            image = lax.dot_general(
                image_refs[distance][...],
                hit,
                (((0,), (0,)), ((), ())),
                preferred_element_type=jnp.float32,
            )[:width]
            value = jnp.where(covered > 0.0, image, text_refs[distance][...].astype(jnp.float32))
            squares += jnp.sum(value * value, axis=0, keepdims=True)
            for block in range(share):
                value_ref[first + block] = value[block * rows : (block + 1) * rows]
        scale = lax.rsqrt(squares / (width * n_tp) + EPSILON)
        for block in range(count):
            source = order_ref[block]
            gain = gain_ref[source].astype(jnp.float32)
            out_ref[block] = (value_ref[source] * scale * gain).astype(out_ref.dtype)

    vmem = pl.BlockSpec(memory_space=pltpu.VMEM)
    smem = pl.BlockSpec(memory_space=pltpu.SMEM)
    return pl.pallas_call(
        body,
        out_shape=jax.ShapeDtypeStruct((count, rows, positions), jnp.bfloat16),
        in_specs=[smem, smem] + [vmem] * (1 + 2 * n_tp),
        out_specs=vmem,
        scratch_shapes=[pltpu.VMEM((count, rows, positions), jnp.float32)],
        compiler_params=pltpu.CompilerParams(vmem_limit_bytes=VMEM),
        cost_estimate=LIGHT,
    )(tp_index, order, gain_column, *texts, *images)


def shards(
    n_req, n_tp,
    patches, ln_gain, ln_bias, merge_weight, text_rows, norm_gain, qkv_weight, token_pos, text_len,
):
    row_count, width = text_rows.shape
    me = lax.axis_index("req")
    tp_index = lax.axis_index("tp").reshape(1)
    lines, line_perm, table = ring_tables(n_req)
    x_perm = [(i, i ^ 1) for i in range(n_req)]
    y_perm = [(i, i ^ 2) for i in range(n_req)]
    rows, columns = qkv_weight.shape
    cut = (columns + 255) // 256 * 128
    order = lax.dynamic_slice_in_dim(jnp.asarray(table), me, 1, 0).reshape(-1)

    def along_line(block):
        return lax.ppermute(block, "req", line_perm)

    def to_sides(block):
        return lax.ppermute(block, "req", x_perm), lax.ppermute(block, "req", y_perm)

    def to_corner(by_x, by_y):
        left = lax.ppermute(by_y[:, :cut], "req", x_perm)
        right = lax.ppermute(by_x[:, cut:], "req", y_perm)
        return jnp.concatenate([left, right], axis=1)

    held = [qkv_weight]
    held.append(along_line(held[0]))
    sides = [to_sides(held[0])]
    corners = []
    stats_own = row_stats(patches)
    stats = [stats_own] + [tp_shift(stats_own, n_tp, d) for d in range(1, n_tp)]
    gain_bias = jnp.stack([ln_gain, ln_bias])
    text_turned = text_rows.T
    texts = [text_turned] + [tp_shift(text_turned, n_tp, d) for d in range(1, n_tp)]

    token_count = token_pos.shape[0]
    target = lax.div(token_pos, row_count)
    same = target[:, None] == target[None, :]
    ids = jnp.arange(token_count, dtype=jnp.int32)
    before = jnp.sum((same & (ids[None, :] < ids[:, None])).astype(jnp.int32), axis=1)
    slot = target * IMG_CAP + before
    slot_count = n_req * IMG_CAP
    place = (
        jnp.arange(slot_count, dtype=jnp.int32)[:, None] == slot[None, :]
    ).astype(jnp.bfloat16)
    code = lax.rem(token_pos, row_count) + 1
    code_cols = jnp.stack([lax.div(code, 256), lax.rem(code, 256)], axis=1).astype(jnp.bfloat16)
    gain_column = norm_gain.reshape(n_req, rows, 1)

    stats, held[1], sides[0], gain_bias, gain_column, order = tie(
        stats, held[1], sides[0], gain_bias, gain_column, order
    )
    held.append(along_line(held[1]))
    sides.append(to_sides(held[1]))
    corners.append(to_corner(*sides[0]))
    partial_value = merge(patches, stats, gain_bias, merge_weight)

    partial_value, held[2], sides[1] = tie(partial_value, held[2], sides[1])
    held.append(along_line(held[2]))
    sides.append(to_sides(held[2]))
    merged = tp_scatter_sum(partial_value, n_tp, 1).astype(jnp.bfloat16)
    merged, corners[0] = tie(merged, corners[0])
    corners.append(along_line(corners[0]))
    padding = (-width - 2) % 128
    payload = jnp.concatenate(
        [merged, code_cols, jnp.zeros((token_count, padding), jnp.bfloat16)], axis=1
    )
    outgoing = jnp.dot(place, payload, preferred_element_type=jnp.float32).astype(jnp.bfloat16)

    def group(step, corner=True):
        pieces = [held[step], *sides[step]] + ([corners[step]] if corner else [])
        return jnp.concatenate(pieces, axis=0)

    first_group = group(0)

    outgoing, held[3], sides[2], texts, first_group = tie(
        outgoing, held[3], sides[2], texts, first_group
    )
    sides.append(to_sides(held[3]))
    arrived = lax.all_to_all(
        outgoing.reshape(n_req, IMG_CAP, -1), "req", split_axis=0, concat_axis=0
    ).reshape(slot_count, -1)
    arrived, corners[1] = tie(arrived, corners[1])
    corners.append(along_line(corners[1]))
    images = [arrived] + [tp_shift(arrived, n_tp, d) for d in range(1, n_tp)]
    blocks = combine(tp_index, order, texts, images, gain_column)
    second_group = group(1)
    blocks, sides[3], second_group = tie(blocks, sides[3], second_group)

    def product(first, count, weight):
        source = blocks[first : first + count].reshape(count * rows, row_count)
        weight, source = tie(weight, source)
        return lax.dot_general(
            source, weight, (((0,), (0,)), ((), ())), preferred_element_type=jnp.float32
        )

    total = product(0, 4, first_group)
    (total,) = tie(total + product(4, 4, second_group))

    for step in range(4, lines):
        held.append(along_line(held[step - 1]))
        sides.append(to_sides(held[step]))
        corners.append(along_line(corners[step - 2]))
    corners.append(to_corner(*sides[-1]))
    (total,) = tie(total + product(lines * 4 - 4, 3, group(lines - 1, False)))
    for step in range(2, lines - 1):
        (total,) = tie(total + product(step * 4, 4, group(step)))
    total, corners[-1] = tie(total, corners[-1])

    position = me * row_count + jnp.arange(row_count, dtype=jnp.int32)
    request_ids = jnp.arange(text_len.shape[0], dtype=jnp.int32)
    limits = jnp.sum(
        jnp.where(
            lax.div(position, SEQ)[:, None] == request_ids[None, :], text_len[None, :], 0
        ),
        axis=1,
    )
    keep = lax.rem(position, SEQ) < limits
    total += product(lines * 4 - 1, 1, corners[-1])
    return jnp.where(keep[:, None], total, 0.0).astype(jnp.bfloat16)


def solution(mesh):
    placed = (
        P("req", "tp"),
        P("tp"),
        P("tp"),
        P(None, "tp", None),
        P("req", "tp"),
        P(),
        P("req", "tp"),
        P("req"),
        P(),
    )
    body = functools.partial(shards, mesh.shape["req"], mesh.shape["tp"])
    return jax.shard_map(
        body, mesh=mesh, in_specs=placed, out_specs=P("req", "tp"), check_vma=False
    )
```

```python
import functools

import jax
import jax.numpy as jnp
import numpy as np
from jax import lax
from jax.experimental import pallas as pl
from jax.experimental.pallas import tpu as pltpu
from jax.sharding import PartitionSpec as P

DV = 1664
SEQ = 4096
IMG_CAP = 16
EPSILON = 1e-06
VMEM = 32 << 20
LIGHT = pl.CostEstimate(flops=1000, bytes_accessed=1000, transcendentals=0)


def folded_ring(count):
    odd = list(range(1, count, 2))
    even = list(range(0, count, 2))
    return even[:1] + odd + even[:0:-1]


def tp_shift(value, n_tp, distance):
    return lax.ppermute(value, "tp", [(i, (i + distance) % n_tp) for i in range(n_tp)])


def tp_scatter_sum(value, n_tp, axis):
    me = lax.axis_index("tp")
    width = value.shape[axis] // n_tp
    total = lax.dynamic_slice_in_dim(value, me * width, width, axis)
    for distance in range(1, n_tp):
        block = lax.dynamic_slice_in_dim(value, (me + distance) % n_tp * width, width, axis)
        total = total + tp_shift(block, n_tp, distance)
    return total


def ring_tables(n_req):
    lines = n_req // 4
    order = folded_ring(lines)
    following = {order[i]: order[(i + 1) % lines] for i in range(lines)}
    line_perm = [(z * 4 + p, following[z] * 4 + p) for z in range(lines) for p in range(4)]
    arrivals = [(0, flip) for flip in range(4)]
    arrivals += [(step, flip) for step in range(1, lines) for flip in range(3)]
    arrivals += [(step, 3) for step in range(1, lines)]
    table = np.zeros((n_req, n_req), np.int32)
    for index in range(n_req):
        for place, (step, flip) in enumerate(arrivals):
            z = order[(order.index(index // 4) - step) % lines]
            table[index, place] = z * 4 + ((index % 4) ^ flip)
    return lines, line_perm, table


def tie(*values):
    return lax.optimization_barrier(values)


def row_stats(patches):
    rows, _ = patches.shape

    def body(patches_ref, out_ref):
        values = patches_ref[...].astype(jnp.float32)
        sums = jnp.sum(values, axis=1, keepdims=True)
        squares = jnp.sum(values * values, axis=1, keepdims=True)
        out_ref[:, :128] = jnp.broadcast_to(sums, (rows, 128))
        out_ref[:, 128:] = jnp.broadcast_to(squares, (rows, 128))

    vmem = pl.BlockSpec(memory_space=pltpu.VMEM)
    return pl.pallas_call(
        body,
        out_shape=jax.ShapeDtypeStruct((rows, 256), jnp.float32),
        in_specs=[vmem],
        out_specs=vmem,
        compiler_params=pltpu.CompilerParams(vmem_limit_bytes=VMEM),
        cost_estimate=LIGHT,
    )(patches)


def merge(patches, stats, gain_bias, merge_weight):
    rows, width = patches.shape
    window, _, features = merge_weight.shape
    tokens = rows // window
    count = len(stats)

    def body(patches_ref, gain_bias_ref, *refs):
        stats_refs, (weight_ref, out_ref, normed_ref) = refs[:count], refs[count:]
        step = pl.program_id(0)

        @pl.when(step == 0)
        def _():
            sums = sum(ref[...] for ref in stats_refs) / DV
            row_mean = sums[:, 0:1]
            row_scale = lax.rsqrt(sums[:, 128:129] - row_mean * row_mean + EPSILON)
            gain_bias = gain_bias_ref[...].astype(jnp.float32)
            normed_ref[...] = (
                (patches_ref[...].astype(jnp.float32) - row_mean) * row_scale * gain_bias[0:1]
                + gain_bias[1:2]
            ).astype(jnp.bfloat16)
            out_ref[...] = jnp.zeros_like(out_ref)

        wanted = lax.broadcasted_iota(jnp.int32, (tokens, rows), 0) * window + step
        chosen = (lax.broadcasted_iota(jnp.int32, (tokens, rows), 1) == wanted).astype(jnp.bfloat16)
        part = jnp.dot(chosen, normed_ref[...], preferred_element_type=jnp.float32)
        out_ref[...] += jnp.dot(
            part.astype(jnp.bfloat16), weight_ref[0], preferred_element_type=jnp.float32
        )

    def whole(shape):
        return pl.BlockSpec(shape, lambda i: (0, 0))

    return pl.pallas_call(
        body,
        out_shape=jax.ShapeDtypeStruct((tokens, features), jnp.float32),
        grid=(window,),
        in_specs=[whole((rows, width)), whole((2, width))]
        + [whole((rows, 256))] * count
        + [pl.BlockSpec((1, width, features), lambda i: (i, 0, 0))],
        out_specs=whole((tokens, features)),
        scratch_shapes=[pltpu.VMEM((rows, width), jnp.bfloat16)],
        compiler_params=pltpu.CompilerParams(vmem_limit_bytes=VMEM),
        cost_estimate=LIGHT,
    )(patches, gain_bias, *stats, merge_weight)


def combine(tp_index, order, texts, images, gain_column):
    n_tp = len(texts)
    width, positions = texts[0].shape
    slots = images[0].shape[0]
    count = order.shape[0]
    rows = width * n_tp // count
    share = width // rows

    def body(index_ref, order_ref, gain_ref, *refs):
        text_refs, image_refs = refs[:n_tp], refs[n_tp : 2 * n_tp]
        out_ref, value_ref = refs[2 * n_tp :]
        code = image_refs[0][:, width : width + 2].astype(jnp.float32)
        local = code[:, 0:1] * 256.0 + code[:, 1:2] - 1.0
        place = lax.broadcasted_iota(jnp.int32, (slots, positions), 1).astype(jnp.float32)
        hit = jnp.where(local == place, 1.0, 0.0)
        covered = jnp.max(hit, axis=0, keepdims=True)
        hit = hit.astype(jnp.bfloat16)
        squares = jnp.zeros((1, positions), jnp.float32)
        for distance in range(n_tp):
            first = lax.rem(index_ref[0] + n_tp - distance, n_tp) * share
            image = lax.dot_general(
                image_refs[distance][...],
                hit,
                (((0,), (0,)), ((), ())),
                preferred_element_type=jnp.float32,
            )[:width]
            value = jnp.where(covered > 0.0, image, text_refs[distance][...].astype(jnp.float32))
            squares += jnp.sum(value * value, axis=0, keepdims=True)
            for block in range(share):
                value_ref[first + block] = value[block * rows : (block + 1) * rows]
        scale = lax.rsqrt(squares / (width * n_tp) + EPSILON)
        for block in range(count):
            source = order_ref[block]
            gain = gain_ref[source].astype(jnp.float32)
            out_ref[block] = (value_ref[source] * scale * gain).astype(out_ref.dtype)

    vmem = pl.BlockSpec(memory_space=pltpu.VMEM)
    smem = pl.BlockSpec(memory_space=pltpu.SMEM)
    return pl.pallas_call(
        body,
        out_shape=jax.ShapeDtypeStruct((count, rows, positions), jnp.bfloat16),
        in_specs=[smem, smem] + [vmem] * (1 + 2 * n_tp),
        out_specs=vmem,
        scratch_shapes=[pltpu.VMEM((count, rows, positions), jnp.float32)],
        compiler_params=pltpu.CompilerParams(vmem_limit_bytes=VMEM),
        cost_estimate=LIGHT,
    )(tp_index, order, gain_column, *texts, *images)


def shards(
    n_req, n_tp,
    patches, ln_gain, ln_bias, merge_weight, text_rows, norm_gain, qkv_weight, token_pos, text_len,
):
    row_count, width = text_rows.shape
    me = lax.axis_index("req")
    tp_index = lax.axis_index("tp").reshape(1)
    lines, line_perm, table = ring_tables(n_req)
    x_perm = [(i, i ^ 1) for i in range(n_req)]
    y_perm = [(i, i ^ 2) for i in range(n_req)]
    rows, columns = qkv_weight.shape
    cut = (columns + 255) // 256 * 128
    order = lax.dynamic_slice_in_dim(jnp.asarray(table), me, 1, 0).reshape(-1)

    def along_line(block):
        return lax.ppermute(block, "req", line_perm)

    def to_sides(block):
        return lax.ppermute(block, "req", x_perm), lax.ppermute(block, "req", y_perm)

    def to_corner(by_x, by_y):
        left = lax.ppermute(by_y[:, :cut], "req", x_perm)
        right = lax.ppermute(by_x[:, cut:], "req", y_perm)
        return jnp.concatenate([left, right], axis=1)

    held = [qkv_weight]
    held.append(along_line(held[0]))
    sides = [to_sides(held[0])]
    corners = []
    stats_own = row_stats(patches)
    stats = [stats_own] + [tp_shift(stats_own, n_tp, d) for d in range(1, n_tp)]
    gain_bias = jnp.stack([ln_gain, ln_bias])
    text_turned = text_rows.T
    texts = [text_turned] + [tp_shift(text_turned, n_tp, d) for d in range(1, n_tp)]

    token_count = token_pos.shape[0]
    target = lax.div(token_pos, row_count)
    same = target[:, None] == target[None, :]
    ids = jnp.arange(token_count, dtype=jnp.int32)
    before = jnp.sum((same & (ids[None, :] < ids[:, None])).astype(jnp.int32), axis=1)
    slot = target * IMG_CAP + before
    slot_count = n_req * IMG_CAP
    place = (
        jnp.arange(slot_count, dtype=jnp.int32)[:, None] == slot[None, :]
    ).astype(jnp.bfloat16)
    code = lax.rem(token_pos, row_count) + 1
    code_cols = jnp.stack([lax.div(code, 256), lax.rem(code, 256)], axis=1).astype(jnp.bfloat16)
    gain_column = norm_gain.reshape(n_req, rows, 1)

    stats, held[1], sides[0], gain_bias, gain_column, order = tie(
        stats, held[1], sides[0], gain_bias, gain_column, order
    )
    held.append(along_line(held[1]))
    sides.append(to_sides(held[1]))
    corners.append(to_corner(*sides[0]))
    partial_value = merge(patches, stats, gain_bias, merge_weight)

    partial_value, held[2], sides[1], corners[0] = tie(
        partial_value, held[2], sides[1], corners[0]
    )
    held.append(along_line(held[2]))
    sides.append(to_sides(held[2]))
    merged = tp_scatter_sum(partial_value, n_tp, 1).astype(jnp.bfloat16)
    padding = (-width - 2) % 128
    payload = jnp.concatenate(
        [merged, code_cols, jnp.zeros((token_count, padding), jnp.bfloat16)], axis=1
    )
    outgoing = jnp.dot(place, payload, preferred_element_type=jnp.float32).astype(jnp.bfloat16)
    arrived = lax.all_to_all(
        outgoing.reshape(n_req, IMG_CAP, -1), "req", split_axis=0, concat_axis=0
    ).reshape(slot_count, -1)

    held[3], sides[2], behind = tie(held[3], sides[2], corners[0])
    sides.append(to_sides(held[3]))
    corners.append(along_line(behind))
    images = [arrived] + [tp_shift(arrived, n_tp, d) for d in range(1, n_tp)]
    blocks = combine(tp_index, order, texts, images, gain_column)
    for step in range(4, lines):
        held.append(along_line(held[step - 1]))
        sides.append(to_sides(held[step]))
    early = [held[0], *sides[0], corners[0]]
    for step in range(1, lines - 1):
        early += [held[step], *sides[step]]
    early = jnp.concatenate(early, axis=0)
    blocks, sides[-1], early = tie(blocks, sides[-1], early)

    def product(first, weight):
        count = weight.shape[0]
        source = blocks[first : first + count // rows].reshape(count, row_count)
        weight, source = tie(weight, source)
        return lax.dot_general(
            source, weight, (((0,), (0,)), ((), ())), preferred_element_type=jnp.float32
        )

    for step in range(2, lines - 1):
        corners.append(along_line(corners[step - 1]))
    corners.append(to_corner(*sides[-1]))
    (total,) = tie(product(0, early))
    late = jnp.concatenate([held[-1], *sides[-1]], axis=0)
    (total,) = tie(total + product(lines * 3 - 2, late))
    last = jnp.concatenate(corners[1:], axis=0)

    position = me * row_count + jnp.arange(row_count, dtype=jnp.int32)
    request_ids = jnp.arange(text_len.shape[0], dtype=jnp.int32)
    limits = jnp.sum(
        jnp.where(
            lax.div(position, SEQ)[:, None] == request_ids[None, :], text_len[None, :], 0
        ),
        axis=1,
    )
    keep = lax.rem(position, SEQ) < limits
    total += product(lines * 3 + 1, last)
    return jnp.where(keep[:, None], total, 0.0).astype(jnp.bfloat16)


def solution(mesh):
    placed = (
        P("req", "tp"),
        P("tp"),
        P("tp"),
        P(None, "tp", None),
        P("req", "tp"),
        P(),
        P("req", "tp"),
        P("req"),
        P(),
    )
    body = functools.partial(shards, mesh.shape["req"], mesh.shape["tp"])
    return jax.shard_map(
        body, mesh=mesh, in_specs=placed, out_specs=P("req", "tp"), check_vma=False
    )
```

```python
import functools

import jax
import jax.numpy as jnp
import numpy as np
from jax import lax
from jax.experimental import pallas as pl
from jax.experimental.pallas import tpu as pltpu
from jax.sharding import PartitionSpec as P

DV = 1664
SEQ = 4096
IMG_CAP = 16
EPSILON = 1e-06
VMEM = 32 << 20
LIGHT = pl.CostEstimate(flops=1000, bytes_accessed=1000, transcendentals=0)


def folded_ring(count):
    odd = list(range(1, count, 2))
    even = list(range(0, count, 2))
    return even[:1] + odd + even[:0:-1]


def tp_shift(value, n_tp, distance):
    return lax.ppermute(value, "tp", [(i, (i + distance) % n_tp) for i in range(n_tp)])


def tp_scatter_sum(value, n_tp, axis):
    me = lax.axis_index("tp")
    width = value.shape[axis] // n_tp
    total = lax.dynamic_slice_in_dim(value, me * width, width, axis)
    for distance in range(1, n_tp):
        block = lax.dynamic_slice_in_dim(value, (me + distance) % n_tp * width, width, axis)
        total = total + tp_shift(block, n_tp, distance)
    return total


def ring_tables(n_req):
    lines = n_req // 4
    order = folded_ring(lines)
    following = {order[i]: order[(i + 1) % lines] for i in range(lines)}
    line_perm = [(z * 4 + p, following[z] * 4 + p) for z in range(lines) for p in range(4)]
    arrivals = [(0, flip) for flip in range(4)]
    arrivals += [(step, flip) for step in range(1, lines) for flip in range(3)]
    arrivals += [(step, 3) for step in range(1, lines)]
    table = np.zeros((n_req, n_req), np.int32)
    for index in range(n_req):
        for place, (step, flip) in enumerate(arrivals):
            z = order[(order.index(index // 4) - step) % lines]
            table[index, place] = z * 4 + ((index % 4) ^ flip)
    return lines, line_perm, table


def tie(*values):
    return lax.optimization_barrier(values)


def row_stats(patches):
    rows, _ = patches.shape

    def body(patches_ref, out_ref):
        values = patches_ref[...].astype(jnp.float32)
        sums = jnp.sum(values, axis=1, keepdims=True)
        squares = jnp.sum(values * values, axis=1, keepdims=True)
        out_ref[:, :128] = jnp.broadcast_to(sums, (rows, 128))
        out_ref[:, 128:] = jnp.broadcast_to(squares, (rows, 128))

    vmem = pl.BlockSpec(memory_space=pltpu.VMEM)
    return pl.pallas_call(
        body,
        out_shape=jax.ShapeDtypeStruct((rows, 256), jnp.float32),
        in_specs=[vmem],
        out_specs=vmem,
        compiler_params=pltpu.CompilerParams(vmem_limit_bytes=VMEM),
        cost_estimate=LIGHT,
    )(patches)


def merge(patches, stats, gain_bias, merge_weight):
    rows, width = patches.shape
    window, _, features = merge_weight.shape
    tokens = rows // window
    count = len(stats)

    def body(patches_ref, gain_bias_ref, *refs):
        stats_refs, (weight_ref, out_ref, normed_ref) = refs[:count], refs[count:]
        step = pl.program_id(0)

        @pl.when(step == 0)
        def _():
            sums = sum(ref[...] for ref in stats_refs) / DV
            row_mean = sums[:, 0:1]
            row_scale = lax.rsqrt(sums[:, 128:129] - row_mean * row_mean + EPSILON)
            gain_bias = gain_bias_ref[...].astype(jnp.float32)
            normed_ref[...] = (
                (patches_ref[...].astype(jnp.float32) - row_mean) * row_scale * gain_bias[0:1]
                + gain_bias[1:2]
            ).astype(jnp.bfloat16)
            out_ref[...] = jnp.zeros_like(out_ref)

        wanted = lax.broadcasted_iota(jnp.int32, (tokens, rows), 0) * window + step
        chosen = (lax.broadcasted_iota(jnp.int32, (tokens, rows), 1) == wanted).astype(jnp.bfloat16)
        part = jnp.dot(chosen, normed_ref[...], preferred_element_type=jnp.float32)
        out_ref[...] += jnp.dot(
            part.astype(jnp.bfloat16), weight_ref[0], preferred_element_type=jnp.float32
        )

    def whole(shape):
        return pl.BlockSpec(shape, lambda i: (0, 0))

    return pl.pallas_call(
        body,
        out_shape=jax.ShapeDtypeStruct((tokens, features), jnp.float32),
        grid=(window,),
        in_specs=[whole((rows, width)), whole((2, width))]
        + [whole((rows, 256))] * count
        + [pl.BlockSpec((1, width, features), lambda i: (i, 0, 0))],
        out_specs=whole((tokens, features)),
        scratch_shapes=[pltpu.VMEM((rows, width), jnp.bfloat16)],
        compiler_params=pltpu.CompilerParams(vmem_limit_bytes=VMEM),
        cost_estimate=LIGHT,
    )(patches, gain_bias, *stats, merge_weight)


def combine(tp_index, order, texts, images, gain_column):
    n_tp = len(texts)
    width, positions = texts[0].shape
    slots = images[0].shape[0]
    count = order.shape[0]
    rows = width * n_tp // count
    share = width // rows

    def body(index_ref, order_ref, gain_ref, *refs):
        text_refs, image_refs = refs[:n_tp], refs[n_tp : 2 * n_tp]
        out_ref, value_ref = refs[2 * n_tp :]
        code = image_refs[0][:, width : width + 2].astype(jnp.float32)
        local = code[:, 0:1] * 256.0 + code[:, 1:2] - 1.0
        place = lax.broadcasted_iota(jnp.int32, (slots, positions), 1).astype(jnp.float32)
        hit = jnp.where(local == place, 1.0, 0.0)
        covered = jnp.max(hit, axis=0, keepdims=True)
        hit = hit.astype(jnp.bfloat16)
        squares = jnp.zeros((1, positions), jnp.float32)
        for distance in range(n_tp):
            first = lax.rem(index_ref[0] + n_tp - distance, n_tp) * share
            image = lax.dot_general(
                image_refs[distance][...],
                hit,
                (((0,), (0,)), ((), ())),
                preferred_element_type=jnp.float32,
            )[:width]
            value = jnp.where(covered > 0.0, image, text_refs[distance][...].astype(jnp.float32))
            squares += jnp.sum(value * value, axis=0, keepdims=True)
            for block in range(share):
                value_ref[first + block] = value[block * rows : (block + 1) * rows]
        scale = lax.rsqrt(squares / (width * n_tp) + EPSILON)
        for block in range(count):
            source = order_ref[block]
            gain = gain_ref[source].astype(jnp.float32)
            out_ref[block] = (value_ref[source] * scale * gain).astype(out_ref.dtype)

    vmem = pl.BlockSpec(memory_space=pltpu.VMEM)
    smem = pl.BlockSpec(memory_space=pltpu.SMEM)
    return pl.pallas_call(
        body,
        out_shape=jax.ShapeDtypeStruct((count, rows, positions), jnp.bfloat16),
        in_specs=[smem, smem] + [vmem] * (1 + 2 * n_tp),
        out_specs=vmem,
        scratch_shapes=[pltpu.VMEM((count, rows, positions), jnp.float32)],
        compiler_params=pltpu.CompilerParams(vmem_limit_bytes=VMEM),
        cost_estimate=LIGHT,
    )(tp_index, order, gain_column, *texts, *images)


def shards(
    n_req, n_tp,
    patches, ln_gain, ln_bias, merge_weight, text_rows, norm_gain, qkv_weight, token_pos, text_len,
):
    row_count, width = text_rows.shape
    me = lax.axis_index("req")
    tp_index = lax.axis_index("tp").reshape(1)
    lines, line_perm, table = ring_tables(n_req)
    x_perm = [(i, i ^ 1) for i in range(n_req)]
    y_perm = [(i, i ^ 2) for i in range(n_req)]
    rows, columns = qkv_weight.shape
    cut = (columns + 255) // 256 * 128
    order = lax.dynamic_slice_in_dim(jnp.asarray(table), me, 1, 0).reshape(-1)

    def along_line(block):
        return lax.ppermute(block, "req", line_perm)

    def to_sides(block):
        return lax.ppermute(block, "req", x_perm), lax.ppermute(block, "req", y_perm)

    def to_corner(by_x, by_y):
        left = lax.ppermute(by_y[:, :cut], "req", x_perm)
        right = lax.ppermute(by_x[:, cut:], "req", y_perm)
        return jnp.concatenate([left, right], axis=1)

    held = [qkv_weight]
    held.append(along_line(held[0]))
    sides = [to_sides(held[0])]
    corners = []
    stats_own = row_stats(patches)
    stats = [stats_own] + [tp_shift(stats_own, n_tp, d) for d in range(1, n_tp)]
    gain_bias = jnp.stack([ln_gain, ln_bias])
    text_turned = text_rows.T
    texts = [text_turned] + [tp_shift(text_turned, n_tp, d) for d in range(1, n_tp)]

    token_count = token_pos.shape[0]
    target = lax.div(token_pos, row_count)
    same = target[:, None] == target[None, :]
    ids = jnp.arange(token_count, dtype=jnp.int32)
    before = jnp.sum((same & (ids[None, :] < ids[:, None])).astype(jnp.int32), axis=1)
    slot = target * IMG_CAP + before
    slot_count = n_req * IMG_CAP
    code = lax.rem(token_pos, row_count) + 1
    code_cols = jnp.stack([lax.div(code, 256), lax.rem(code, 256)], axis=1).astype(jnp.bfloat16)
    gain_column = norm_gain.reshape(n_req, rows, 1)

    partial_value = merge(patches, stats, gain_bias, merge_weight)

    partial_value, held[1], sides[0], gain_column, order, slot, code_cols = tie(
        partial_value, held[1], sides[0], gain_column, order, slot, code_cols
    )
    held.append(along_line(held[1]))
    sides.append(to_sides(held[1]))
    corners.append(to_corner(*sides[0]))
    merged = tp_scatter_sum(partial_value, n_tp, 1).astype(jnp.bfloat16)
    padding = (-width - 2) % 128
    payload = jnp.concatenate(
        [merged, code_cols, jnp.zeros((token_count, padding), jnp.bfloat16)], axis=1
    )
    place = (
        jnp.arange(slot_count, dtype=jnp.int32)[:, None] == slot[None, :]
    ).astype(jnp.bfloat16)
    outgoing = jnp.dot(place, payload, preferred_element_type=jnp.float32).astype(jnp.bfloat16)
    arrived = lax.all_to_all(
        outgoing.reshape(n_req, IMG_CAP, -1), "req", split_axis=0, concat_axis=0
    ).reshape(slot_count, -1)

    held[2], sides[1] = tie(held[2], sides[1])
    held.append(along_line(held[2]))
    sides.append(to_sides(held[2]))
    corners.append(along_line(corners[0]))
    images = [arrived] + [tp_shift(arrived, n_tp, d) for d in range(1, n_tp)]
    blocks = combine(tp_index, order, texts, images, gain_column)

    held[3], sides[2] = tie(held[3], sides[2])
    sides.append(to_sides(held[3]))
    for step in range(4, lines):
        held.append(along_line(held[step - 1]))
        sides.append(to_sides(held[step]))
    blocks, corners[1] = tie(blocks, corners[1])
    for step in range(2, lines - 1):
        corners.append(along_line(corners[step - 1]))

    def product(first, weights):
        weight = jnp.concatenate(weights, axis=0)
        count = weight.shape[0]
        source = blocks[first : first + count // rows].reshape(count, row_count)
        weight, source = tie(weight, source)
        return lax.dot_general(
            source, weight, (((0,), (0,)), ((), ())), preferred_element_type=jnp.float32
        )

    total = product(0, [held[0], *sides[0], corners[0]])
    for step in range(1, lines - 1):
        (total,) = tie(total + product(step * 3 + 1, [held[step], *sides[step]]))

    total, sides[-1] = tie(total, sides[-1])
    corners.append(to_corner(*sides[-1]))
    (total,) = tie(total + product(lines * 3 - 2, [held[-1], *sides[-1]]))

    position = me * row_count + jnp.arange(row_count, dtype=jnp.int32)
    request_ids = jnp.arange(text_len.shape[0], dtype=jnp.int32)
    limits = jnp.sum(
        jnp.where(
            lax.div(position, SEQ)[:, None] == request_ids[None, :], text_len[None, :], 0
        ),
        axis=1,
    )
    keep = lax.rem(position, SEQ) < limits
    total += product(lines * 3 + 1, corners[1:])
    return jnp.where(keep[:, None], total, 0.0).astype(jnp.bfloat16)


def solution(mesh):
    placed = (
        P("req", "tp"),
        P("tp"),
        P("tp"),
        P(None, "tp", None),
        P("req", "tp"),
        P(),
        P("req", "tp"),
        P("req"),
        P(),
    )
    body = functools.partial(shards, mesh.shape["req"], mesh.shape["tp"])
    return jax.shard_map(
        body, mesh=mesh, in_specs=placed, out_specs=P("req", "tp"), check_vma=False
    )
```

```python
import functools

import jax
import jax.numpy as jnp
import numpy as np
from jax import lax
from jax.experimental import pallas as pl
from jax.experimental.pallas import tpu as pltpu
from jax.sharding import PartitionSpec as P

DV = 1664
SEQ = 4096
IMG_CAP = 16
EPSILON = 1e-06
VMEM = 32 << 20
LIGHT = pl.CostEstimate(flops=1000, bytes_accessed=1000, transcendentals=0)


def folded_ring(count):
    odd = list(range(1, count, 2))
    even = list(range(0, count, 2))
    return even[:1] + odd + even[:0:-1]


def tp_shift(value, n_tp, distance):
    return lax.ppermute(value, "tp", [(i, (i + distance) % n_tp) for i in range(n_tp)])


def tp_scatter_sum(value, n_tp, axis):
    me = lax.axis_index("tp")
    width = value.shape[axis] // n_tp
    total = lax.dynamic_slice_in_dim(value, me * width, width, axis)
    for distance in range(1, n_tp):
        block = lax.dynamic_slice_in_dim(value, (me + distance) % n_tp * width, width, axis)
        total = total + tp_shift(block, n_tp, distance)
    return total


def ring_tables(n_req):
    lines = n_req // 4
    order = folded_ring(lines)
    following = {order[i]: order[(i + 1) % lines] for i in range(lines)}
    line_perm = [(z * 4 + p, following[z] * 4 + p) for z in range(lines) for p in range(4)]
    arrivals = [(0, flip) for flip in range(4)]
    arrivals += [(step, flip) for step in range(1, lines) for flip in range(3)]
    arrivals += [(step, 3) for step in range(1, lines)]
    table = np.zeros((n_req, n_req), np.int32)
    for index in range(n_req):
        for place, (step, flip) in enumerate(arrivals):
            z = order[(order.index(index // 4) - step) % lines]
            table[index, place] = z * 4 + ((index % 4) ^ flip)
    return lines, line_perm, table


def tie(*values):
    return lax.optimization_barrier(values)


def row_stats(patches):
    rows, _ = patches.shape

    def body(patches_ref, out_ref):
        values = patches_ref[...].astype(jnp.float32)
        sums = jnp.sum(values, axis=1, keepdims=True)
        squares = jnp.sum(values * values, axis=1, keepdims=True)
        out_ref[:, :128] = jnp.broadcast_to(sums, (rows, 128))
        out_ref[:, 128:] = jnp.broadcast_to(squares, (rows, 128))

    vmem = pl.BlockSpec(memory_space=pltpu.VMEM)
    return pl.pallas_call(
        body,
        out_shape=jax.ShapeDtypeStruct((rows, 256), jnp.float32),
        in_specs=[vmem],
        out_specs=vmem,
        compiler_params=pltpu.CompilerParams(vmem_limit_bytes=VMEM),
        cost_estimate=pl.CostEstimate(flops=1000, bytes_accessed=16 << 20, transcendentals=0),
    )(patches)


def merge(patches, stats, gain_bias, merge_weight):
    rows, width = patches.shape
    window, _, features = merge_weight.shape
    tokens = rows // window
    count = len(stats)

    def body(patches_ref, gain_bias_ref, *refs):
        stats_refs, (weight_ref, out_ref, normed_ref) = refs[:count], refs[count:]
        step = pl.program_id(0)

        @pl.when(step == 0)
        def _():
            sums = sum(ref[...] for ref in stats_refs) / DV
            row_mean = sums[:, 0:1]
            row_scale = lax.rsqrt(sums[:, 128:129] - row_mean * row_mean + EPSILON)
            gain_bias = gain_bias_ref[...].astype(jnp.float32)
            normed_ref[...] = (
                (patches_ref[...].astype(jnp.float32) - row_mean) * row_scale * gain_bias[0:1]
                + gain_bias[1:2]
            ).astype(jnp.bfloat16)
            out_ref[...] = jnp.zeros_like(out_ref)

        wanted = lax.broadcasted_iota(jnp.int32, (tokens, rows), 0) * window + step
        chosen = (lax.broadcasted_iota(jnp.int32, (tokens, rows), 1) == wanted).astype(jnp.bfloat16)
        part = jnp.dot(chosen, normed_ref[...], preferred_element_type=jnp.float32)
        out_ref[...] += jnp.dot(
            part.astype(jnp.bfloat16), weight_ref[0], preferred_element_type=jnp.float32
        )

    def whole(shape):
        return pl.BlockSpec(shape, lambda i: (0, 0))

    return pl.pallas_call(
        body,
        out_shape=jax.ShapeDtypeStruct((tokens, features), jnp.float32),
        grid=(window,),
        in_specs=[whole((rows, width)), whole((2, width))]
        + [whole((rows, 256))] * count
        + [pl.BlockSpec((1, width, features), lambda i: (i, 0, 0))],
        out_specs=whole((tokens, features)),
        scratch_shapes=[pltpu.VMEM((rows, width), jnp.bfloat16)],
        compiler_params=pltpu.CompilerParams(vmem_limit_bytes=VMEM),
        cost_estimate=LIGHT,
    )(patches, gain_bias, *stats, merge_weight)


def combine(tp_index, order, texts, images, gain_column):
    n_tp = len(texts)
    width, positions = texts[0].shape
    slots = images[0].shape[0]
    count = order.shape[0]
    rows = width * n_tp // count
    share = width // rows

    def body(index_ref, order_ref, gain_ref, *refs):
        text_refs, image_refs = refs[:n_tp], refs[n_tp : 2 * n_tp]
        out_ref, value_ref = refs[2 * n_tp :]
        code = image_refs[0][:, width : width + 2].astype(jnp.float32)
        local = code[:, 0:1] * 256.0 + code[:, 1:2] - 1.0
        place = lax.broadcasted_iota(jnp.int32, (slots, positions), 1).astype(jnp.float32)
        hit = jnp.where(local == place, 1.0, 0.0)
        covered = jnp.max(hit, axis=0, keepdims=True)
        hit = hit.astype(jnp.bfloat16)
        squares = jnp.zeros((1, positions), jnp.float32)
        for distance in range(n_tp):
            first = lax.rem(index_ref[0] + n_tp - distance, n_tp) * share
            image = lax.dot_general(
                image_refs[distance][...],
                hit,
                (((0,), (0,)), ((), ())),
                preferred_element_type=jnp.float32,
            )[:width]
            value = jnp.where(covered > 0.0, image, text_refs[distance][...].astype(jnp.float32))
            squares += jnp.sum(value * value, axis=0, keepdims=True)
            for block in range(share):
                value_ref[first + block] = value[block * rows : (block + 1) * rows]
        scale = lax.rsqrt(squares / (width * n_tp) + EPSILON)
        for block in range(count):
            source = order_ref[block]
            gain = gain_ref[source].astype(jnp.float32)
            out_ref[block] = (value_ref[source] * scale * gain).astype(out_ref.dtype)

    vmem = pl.BlockSpec(memory_space=pltpu.VMEM)
    smem = pl.BlockSpec(memory_space=pltpu.SMEM)
    return pl.pallas_call(
        body,
        out_shape=jax.ShapeDtypeStruct((count, rows, positions), jnp.bfloat16),
        in_specs=[smem, smem] + [vmem] * (1 + 2 * n_tp),
        out_specs=vmem,
        scratch_shapes=[pltpu.VMEM((count, rows, positions), jnp.float32)],
        compiler_params=pltpu.CompilerParams(vmem_limit_bytes=VMEM),
        cost_estimate=LIGHT,
    )(tp_index, order, gain_column, *texts, *images)


def shards(
    n_req, n_tp,
    patches, ln_gain, ln_bias, merge_weight, text_rows, norm_gain, qkv_weight, token_pos, text_len,
):
    row_count, width = text_rows.shape
    me = lax.axis_index("req")
    tp_index = lax.axis_index("tp").reshape(1)
    lines, line_perm, table = ring_tables(n_req)
    x_perm = [(i, i ^ 1) for i in range(n_req)]
    y_perm = [(i, i ^ 2) for i in range(n_req)]
    rows, columns = qkv_weight.shape
    cut = (columns + 255) // 256 * 128
    order = lax.dynamic_slice_in_dim(jnp.asarray(table), me, 1, 0).reshape(-1)

    def along_line(block):
        return lax.ppermute(block, "req", line_perm)

    def to_sides(block):
        return lax.ppermute(block, "req", x_perm), lax.ppermute(block, "req", y_perm)

    def to_corner(by_x, by_y):
        left = lax.ppermute(by_y[:, :cut], "req", x_perm)
        right = lax.ppermute(by_x[:, cut:], "req", y_perm)
        return jnp.concatenate([left, right], axis=1)

    held = [qkv_weight]
    held.append(along_line(held[0]))
    sides = [to_sides(held[0])]
    corners = []
    stats_own = row_stats(patches)
    stats = [stats_own] + [tp_shift(stats_own, n_tp, d) for d in range(1, n_tp)]
    gain_bias = jnp.stack([ln_gain, ln_bias])
    text_turned = text_rows.T
    texts = [text_turned] + [tp_shift(text_turned, n_tp, d) for d in range(1, n_tp)]

    token_count = token_pos.shape[0]
    target = lax.div(token_pos, row_count)
    same = target[:, None] == target[None, :]
    ids = jnp.arange(token_count, dtype=jnp.int32)
    before = jnp.sum((same & (ids[None, :] < ids[:, None])).astype(jnp.int32), axis=1)
    slot = target * IMG_CAP + before
    slot_count = n_req * IMG_CAP
    code = lax.rem(token_pos, row_count) + 1
    code_cols = jnp.stack([lax.div(code, 256), lax.rem(code, 256)], axis=1).astype(jnp.bfloat16)
    gain_column = norm_gain.reshape(n_req, rows, 1)

    partial_value = merge(patches, stats, gain_bias, merge_weight)

    partial_value, held[1], sides[0], gain_column, order, slot, code_cols = tie(
        partial_value, held[1], sides[0], gain_column, order, slot, code_cols
    )
    held.append(along_line(held[1]))
    sides.append(to_sides(held[1]))
    corners.append(to_corner(*sides[0]))
    merged = tp_scatter_sum(partial_value, n_tp, 1).astype(jnp.bfloat16)
    padding = (-width - 2) % 128
    payload = jnp.concatenate(
        [merged, code_cols, jnp.zeros((token_count, padding), jnp.bfloat16)], axis=1
    )
    place = (
        jnp.arange(slot_count, dtype=jnp.int32)[:, None] == slot[None, :]
    ).astype(jnp.bfloat16)
    outgoing = jnp.dot(place, payload, preferred_element_type=jnp.float32).astype(jnp.bfloat16)
    arrived = lax.all_to_all(
        outgoing.reshape(n_req, IMG_CAP, -1), "req", split_axis=0, concat_axis=0
    ).reshape(slot_count, -1)

    held[2], sides[1] = tie(held[2], sides[1])
    held.append(along_line(held[2]))
    sides.append(to_sides(held[2]))
    images = [arrived] + [tp_shift(arrived, n_tp, d) for d in range(1, n_tp)]
    blocks = combine(tp_index, order, texts, images, gain_column)

    held[3], corners[0] = tie(held[3], corners[0])
    corners.append(along_line(corners[0]))
    held[3], sides[2] = tie(held[3], sides[2])
    sides.append(to_sides(held[3]))
    for step in range(4, lines):
        held.append(along_line(held[step - 1]))
        sides.append(to_sides(held[step]))
    def product(first, weights):
        weight = jnp.concatenate(weights, axis=0)
        count = weight.shape[0]
        source = blocks[first : first + count // rows].reshape(count, row_count)
        weight, source = tie(weight, source)
        return lax.dot_general(
            source, weight, (((0,), (0,)), ((), ())), preferred_element_type=jnp.float32
        )

    total = product(0, [held[0], *sides[0], corners[0]])
    for step in range(1, lines - 1):
        (total,) = tie(total + product(step * 3 + 1, [held[step], *sides[step]]))
        if step == 1:
            total, corners[1] = tie(total, corners[1])
            for other in range(2, lines - 1):
                corners.append(along_line(corners[other - 1]))

    total, sides[-1] = tie(total, sides[-1])
    corners.append(to_corner(*sides[-1]))
    (total,) = tie(total + product(lines * 3 - 2, [held[-1], *sides[-1]]))

    position = me * row_count + jnp.arange(row_count, dtype=jnp.int32)
    request_ids = jnp.arange(text_len.shape[0], dtype=jnp.int32)
    limits = jnp.sum(
        jnp.where(
            lax.div(position, SEQ)[:, None] == request_ids[None, :], text_len[None, :], 0
        ),
        axis=1,
    )
    keep = lax.rem(position, SEQ) < limits
    total += product(lines * 3 + 1, corners[1:])
    return jnp.where(keep[:, None], total, 0.0).astype(jnp.bfloat16)


def solution(mesh):
    placed = (
        P("req", "tp"),
        P("tp"),
        P("tp"),
        P(None, "tp", None),
        P("req", "tp"),
        P(),
        P("req", "tp"),
        P("req"),
        P(),
    )
    body = functools.partial(shards, mesh.shape["req"], mesh.shape["tp"])
    return jax.shard_map(
        body, mesh=mesh, in_specs=placed, out_specs=P("req", "tp"), check_vma=False
    )
```

```python
import functools

import jax
import jax.numpy as jnp
import numpy as np
from jax import lax
from jax.experimental import pallas as pl
from jax.experimental.pallas import tpu as pltpu
from jax.sharding import PartitionSpec as P

DV = 1664
SEQ = 4096
IMG_CAP = 16
EPSILON = 1e-06
VMEM = 32 << 20
LIGHT = pl.CostEstimate(flops=1000, bytes_accessed=1000, transcendentals=0)


def folded_ring(count):
    odd = list(range(1, count, 2))
    even = list(range(0, count, 2))
    return even[:1] + odd + even[:0:-1]


def tp_shift(value, n_tp, distance):
    return lax.ppermute(value, "tp", [(i, (i + distance) % n_tp) for i in range(n_tp)])


def tp_scatter_sum(value, n_tp, axis):
    me = lax.axis_index("tp")
    width = value.shape[axis] // n_tp
    total = lax.dynamic_slice_in_dim(value, me * width, width, axis)
    for distance in range(1, n_tp):
        block = lax.dynamic_slice_in_dim(value, (me + distance) % n_tp * width, width, axis)
        total = total + tp_shift(block, n_tp, distance)
    return total


def ring_tables(n_req):
    lines = n_req // 4
    order = folded_ring(lines)
    following = {order[i]: order[(i + 1) % lines] for i in range(lines)}
    line_perm = [(z * 4 + p, following[z] * 4 + p) for z in range(lines) for p in range(4)]
    arrivals = [(0, flip) for flip in range(4)]
    arrivals += [(step, flip) for step in range(1, lines) for flip in range(3)]
    arrivals += [(step, 3) for step in range(1, lines)]
    table = np.zeros((n_req, n_req), np.int32)
    for index in range(n_req):
        for place, (step, flip) in enumerate(arrivals):
            z = order[(order.index(index // 4) - step) % lines]
            table[index, place] = z * 4 + ((index % 4) ^ flip)
    return lines, line_perm, table


def tie(*values):
    return lax.optimization_barrier(values)


def row_stats(patches):
    rows, _ = patches.shape

    def body(patches_ref, out_ref):
        values = patches_ref[...].astype(jnp.float32)
        sums = jnp.sum(values, axis=1, keepdims=True)
        squares = jnp.sum(values * values, axis=1, keepdims=True)
        out_ref[:, :128] = jnp.broadcast_to(sums, (rows, 128))
        out_ref[:, 128:] = jnp.broadcast_to(squares, (rows, 128))

    vmem = pl.BlockSpec(memory_space=pltpu.VMEM)
    return pl.pallas_call(
        body,
        out_shape=jax.ShapeDtypeStruct((rows, 256), jnp.float32),
        in_specs=[vmem],
        out_specs=vmem,
        compiler_params=pltpu.CompilerParams(vmem_limit_bytes=VMEM),
        cost_estimate=pl.CostEstimate(flops=1000, bytes_accessed=16 << 20, transcendentals=0),
    )(patches)


def merge(patches, stats, gain_bias, merge_weight):
    rows, width = patches.shape
    window, _, features = merge_weight.shape
    tokens = rows // window
    count = len(stats)

    def body(patches_ref, gain_bias_ref, *refs):
        stats_refs, (weight_ref, out_ref, normed_ref) = refs[:count], refs[count:]
        step = pl.program_id(0)

        @pl.when(step == 0)
        def _():
            sums = sum(ref[...] for ref in stats_refs) / DV
            row_mean = sums[:, 0:1]
            row_scale = lax.rsqrt(sums[:, 128:129] - row_mean * row_mean + EPSILON)
            gain_bias = gain_bias_ref[...].astype(jnp.float32)
            normed_ref[...] = (
                (patches_ref[...].astype(jnp.float32) - row_mean) * row_scale * gain_bias[0:1]
                + gain_bias[1:2]
            ).astype(jnp.bfloat16)
            out_ref[...] = jnp.zeros_like(out_ref)

        wanted = lax.broadcasted_iota(jnp.int32, (tokens, rows), 0) * window + step
        chosen = (lax.broadcasted_iota(jnp.int32, (tokens, rows), 1) == wanted).astype(jnp.bfloat16)
        part = jnp.dot(chosen, normed_ref[...], preferred_element_type=jnp.float32)
        out_ref[...] += jnp.dot(
            part.astype(jnp.bfloat16), weight_ref[0], preferred_element_type=jnp.float32
        )

    def whole(shape):
        return pl.BlockSpec(shape, lambda i: (0, 0))

    return pl.pallas_call(
        body,
        out_shape=jax.ShapeDtypeStruct((tokens, features), jnp.float32),
        grid=(window,),
        in_specs=[whole((rows, width)), whole((2, width))]
        + [whole((rows, 256))] * count
        + [pl.BlockSpec((1, width, features), lambda i: (i, 0, 0))],
        out_specs=whole((tokens, features)),
        scratch_shapes=[pltpu.VMEM((rows, width), jnp.bfloat16)],
        compiler_params=pltpu.CompilerParams(vmem_limit_bytes=VMEM),
        cost_estimate=LIGHT,
    )(patches, gain_bias, *stats, merge_weight)


def combine(tp_index, order, texts, images, gain_column):
    n_tp = len(texts)
    width, positions = texts[0].shape
    slots = images[0].shape[0]
    count = order.shape[0]
    rows = width * n_tp // count
    share = width // rows

    def body(index_ref, order_ref, gain_ref, *refs):
        text_refs, image_refs = refs[:n_tp], refs[n_tp : 2 * n_tp]
        out_ref, value_ref = refs[2 * n_tp :]
        code = image_refs[0][:, width : width + 2].astype(jnp.float32)
        local = code[:, 0:1] * 256.0 + code[:, 1:2] - 1.0
        place = lax.broadcasted_iota(jnp.int32, (slots, positions), 1).astype(jnp.float32)
        hit = jnp.where(local == place, 1.0, 0.0)
        covered = jnp.max(hit, axis=0, keepdims=True)
        hit = hit.astype(jnp.bfloat16)
        squares = jnp.zeros((1, positions), jnp.float32)
        for distance in range(n_tp):
            first = lax.rem(index_ref[0] + n_tp - distance, n_tp) * share
            image = lax.dot_general(
                image_refs[distance][...],
                hit,
                (((0,), (0,)), ((), ())),
                preferred_element_type=jnp.float32,
            )[:width]
            value = jnp.where(covered > 0.0, image, text_refs[distance][...].astype(jnp.float32))
            squares += jnp.sum(value * value, axis=0, keepdims=True)
            for block in range(share):
                value_ref[first + block] = value[block * rows : (block + 1) * rows]
        scale = lax.rsqrt(squares / (width * n_tp) + EPSILON)
        for block in range(count):
            source = order_ref[block]
            gain = gain_ref[source].astype(jnp.float32)
            out_ref[block] = (value_ref[source] * scale * gain).astype(out_ref.dtype)

    vmem = pl.BlockSpec(memory_space=pltpu.VMEM)
    smem = pl.BlockSpec(memory_space=pltpu.SMEM)
    return pl.pallas_call(
        body,
        out_shape=jax.ShapeDtypeStruct((count, rows, positions), jnp.bfloat16),
        in_specs=[smem, smem] + [vmem] * (1 + 2 * n_tp),
        out_specs=vmem,
        scratch_shapes=[pltpu.VMEM((count, rows, positions), jnp.float32)],
        compiler_params=pltpu.CompilerParams(vmem_limit_bytes=VMEM),
        cost_estimate=LIGHT,
    )(tp_index, order, gain_column, *texts, *images)


def shards(
    n_req, n_tp,
    patches, ln_gain, ln_bias, merge_weight, text_rows, norm_gain, qkv_weight, token_pos, text_len,
):
    row_count, width = text_rows.shape
    me = lax.axis_index("req")
    tp_index = lax.axis_index("tp").reshape(1)
    lines, line_perm, table = ring_tables(n_req)
    x_perm = [(i, i ^ 1) for i in range(n_req)]
    y_perm = [(i, i ^ 2) for i in range(n_req)]
    rows, columns = qkv_weight.shape
    cut = (columns + 255) // 256 * 128
    order = lax.dynamic_slice_in_dim(jnp.asarray(table), me, 1, 0).reshape(-1)

    def along_line(block):
        return lax.ppermute(block, "req", line_perm)

    def to_sides(block):
        return lax.ppermute(block, "req", x_perm), lax.ppermute(block, "req", y_perm)

    def to_corner(by_x, by_y):
        left = lax.ppermute(by_y[:, :cut], "req", x_perm)
        right = lax.ppermute(by_x[:, cut:], "req", y_perm)
        return left, right

    stats_own, qkv_weight = tie(row_stats(patches), qkv_weight)
    held = [qkv_weight]
    held.append(along_line(held[0]))
    sides = [to_sides(held[0])]
    stats = [stats_own] + [tp_shift(stats_own, n_tp, d) for d in range(1, n_tp)]
    gain_bias = jnp.stack([ln_gain, ln_bias])
    text_turned = text_rows.T
    texts = [text_turned] + [tp_shift(text_turned, n_tp, d) for d in range(1, n_tp)]

    token_count = token_pos.shape[0]
    target = lax.div(token_pos, row_count)
    same = target[:, None] == target[None, :]
    ids = jnp.arange(token_count, dtype=jnp.int32)
    before = jnp.sum((same & (ids[None, :] < ids[:, None])).astype(jnp.int32), axis=1)
    slot = target * IMG_CAP + before
    slot_count = n_req * IMG_CAP
    code = lax.rem(token_pos, row_count) + 1
    code_cols = jnp.stack([lax.div(code, 256), lax.rem(code, 256)], axis=1).astype(jnp.bfloat16)
    gain_column = norm_gain.reshape(n_req, rows, 1)

    partial_value = merge(patches, stats, gain_bias, merge_weight)

    partial_value, held[1], sides[0], gain_column, order, slot, code_cols = tie(
        partial_value, held[1], sides[0], gain_column, order, slot, code_cols
    )
    held.append(along_line(held[1]))
    sides.append(to_sides(held[1]))
    halves = to_corner(*sides[0])
    merged = tp_scatter_sum(partial_value, n_tp, 1).astype(jnp.bfloat16)
    padding = (-width - 2) % 128
    payload = jnp.concatenate(
        [merged, code_cols, jnp.zeros((token_count, padding), jnp.bfloat16)], axis=1
    )
    place = (
        jnp.arange(slot_count, dtype=jnp.int32)[:, None] == slot[None, :]
    ).astype(jnp.bfloat16)
    outgoing = jnp.dot(place, payload, preferred_element_type=jnp.float32).astype(jnp.bfloat16)
    arrived = lax.all_to_all(
        outgoing.reshape(n_req, IMG_CAP, -1), "req", split_axis=0, concat_axis=0
    ).reshape(slot_count, -1)

    held[2], sides[1], halves = tie(held[2], sides[1], halves)
    held.append(along_line(held[2]))
    sides.append(to_sides(held[2]))
    arrived, halves = tie(arrived, halves)
    corners = [jnp.concatenate(halves, axis=1)]
    corners.append(along_line(corners[0]))
    images = [arrived] + [tp_shift(arrived, n_tp, d) for d in range(1, n_tp)]
    blocks = combine(tp_index, order, texts, images, gain_column)

    held[3], sides[2] = tie(held[3], sides[2])
    sides.append(to_sides(held[3]))
    for step in range(4, lines):
        held.append(along_line(held[step - 1]))
        sides.append(to_sides(held[step]))

    def product(first, weights):
        weight = jnp.concatenate(weights, axis=0)
        count = weight.shape[0]
        source = blocks[first : first + count // rows].reshape(count, row_count)
        weight, source = tie(weight, source)
        return lax.dot_general(
            source, weight, (((0,), (0,)), ((), ())), preferred_element_type=jnp.float32
        )

    total = product(0, [held[0], *sides[0], corners[0]])
    total, corners[1] = tie(total, corners[1])
    for step in range(2, lines - 1):
        corners.append(along_line(corners[step - 1]))
    for step in range(1, lines - 1):
        (total,) = tie(total + product(step * 3 + 1, [held[step], *sides[step]]))

    total, sides[-1] = tie(total, sides[-1])
    corners.append(jnp.concatenate(to_corner(*sides[-1]), axis=1))
    (total,) = tie(total + product(lines * 3 - 2, [held[-1], *sides[-1]]))

    position = me * row_count + jnp.arange(row_count, dtype=jnp.int32)
    request_ids = jnp.arange(text_len.shape[0], dtype=jnp.int32)
    limits = jnp.sum(
        jnp.where(
            lax.div(position, SEQ)[:, None] == request_ids[None, :], text_len[None, :], 0
        ),
        axis=1,
    )
    keep = lax.rem(position, SEQ) < limits
    total += product(lines * 3 + 1, corners[1:])
    return jnp.where(keep[:, None], total, 0.0).astype(jnp.bfloat16)


def solution(mesh):
    placed = (
        P("req", "tp"),
        P("tp"),
        P("tp"),
        P(None, "tp", None),
        P("req", "tp"),
        P(),
        P("req", "tp"),
        P("req"),
        P(),
    )
    body = functools.partial(shards, mesh.shape["req"], mesh.shape["tp"])
    return jax.shard_map(
        body, mesh=mesh, in_specs=placed, out_specs=P("req", "tp"), check_vma=False
    )
```

```python
import functools

import jax
import jax.numpy as jnp
import numpy as np
from jax import lax
from jax.experimental import pallas as pl
from jax.experimental.pallas import tpu as pltpu
from jax.sharding import PartitionSpec as P

DV = 1664
SEQ = 4096
IMG_CAP = 16
EPSILON = 1e-06
VMEM = 32 << 20
LIGHT = pl.CostEstimate(flops=1000, bytes_accessed=1000, transcendentals=0)


def folded_ring(count):
    odd = list(range(1, count, 2))
    even = list(range(0, count, 2))
    return even[:1] + odd + even[:0:-1]


def tp_shift(value, n_tp, distance):
    return lax.ppermute(value, "tp", [(i, (i + distance) % n_tp) for i in range(n_tp)])


def tp_scatter_sum(value, n_tp, axis):
    me = lax.axis_index("tp")
    width = value.shape[axis] // n_tp
    total = lax.dynamic_slice_in_dim(value, me * width, width, axis)
    for distance in range(1, n_tp):
        block = lax.dynamic_slice_in_dim(value, (me + distance) % n_tp * width, width, axis)
        total = total + tp_shift(block, n_tp, distance)
    return total


def ring_tables(n_req):
    lines = n_req // 4
    order = folded_ring(lines)
    following = {order[i]: order[(i + 1) % lines] for i in range(lines)}
    line_perm = [(z * 4 + p, following[z] * 4 + p) for z in range(lines) for p in range(4)]
    arrivals = [(0, flip) for flip in range(4)]
    arrivals += [(step, flip) for step in range(1, lines) for flip in range(3)]
    arrivals += [(step, 3) for step in range(1, lines)]
    table = np.zeros((n_req, n_req), np.int32)
    for index in range(n_req):
        for place, (step, flip) in enumerate(arrivals):
            z = order[(order.index(index // 4) - step) % lines]
            table[index, place] = z * 4 + ((index % 4) ^ flip)
    return lines, line_perm, table


def tie(*values):
    return lax.optimization_barrier(values)


def row_stats(patches):
    rows, _ = patches.shape

    def body(patches_ref, out_ref):
        values = patches_ref[...].astype(jnp.float32)
        sums = jnp.sum(values, axis=1, keepdims=True)
        squares = jnp.sum(values * values, axis=1, keepdims=True)
        out_ref[:, :128] = jnp.broadcast_to(sums, (rows, 128))
        out_ref[:, 128:] = jnp.broadcast_to(squares, (rows, 128))

    vmem = pl.BlockSpec(memory_space=pltpu.VMEM)
    return pl.pallas_call(
        body,
        out_shape=jax.ShapeDtypeStruct((rows, 256), jnp.float32),
        in_specs=[vmem],
        out_specs=vmem,
        compiler_params=pltpu.CompilerParams(vmem_limit_bytes=VMEM),
        cost_estimate=pl.CostEstimate(flops=1000, bytes_accessed=16 << 20, transcendentals=0),
    )(patches)


def merge(patches, stats, gain_bias, merge_weight):
    rows, width = patches.shape
    window, _, features = merge_weight.shape
    tokens = rows // window
    count = len(stats)

    def body(patches_ref, gain_bias_ref, *refs):
        stats_refs, (weight_ref, out_ref, normed_ref) = refs[:count], refs[count:]
        step = pl.program_id(0)

        @pl.when(step == 0)
        def _():
            sums = sum(ref[...] for ref in stats_refs) / DV
            row_mean = sums[:, 0:1]
            row_scale = lax.rsqrt(sums[:, 128:129] - row_mean * row_mean + EPSILON)
            gain_bias = gain_bias_ref[...].astype(jnp.float32)
            normed_ref[...] = (
                (patches_ref[...].astype(jnp.float32) - row_mean) * row_scale * gain_bias[0:1]
                + gain_bias[1:2]
            ).astype(jnp.bfloat16)
            out_ref[...] = jnp.zeros_like(out_ref)

        wanted = lax.broadcasted_iota(jnp.int32, (tokens, rows), 0) * window + step
        chosen = (lax.broadcasted_iota(jnp.int32, (tokens, rows), 1) == wanted).astype(jnp.bfloat16)
        part = jnp.dot(chosen, normed_ref[...], preferred_element_type=jnp.float32)
        out_ref[...] += jnp.dot(
            part.astype(jnp.bfloat16), weight_ref[0], preferred_element_type=jnp.float32
        )

    def whole(shape):
        return pl.BlockSpec(shape, lambda i: (0, 0))

    return pl.pallas_call(
        body,
        out_shape=jax.ShapeDtypeStruct((tokens, features), jnp.float32),
        grid=(window,),
        in_specs=[whole((rows, width)), whole((2, width))]
        + [whole((rows, 256))] * count
        + [pl.BlockSpec((1, width, features), lambda i: (i, 0, 0))],
        out_specs=whole((tokens, features)),
        scratch_shapes=[pltpu.VMEM((rows, width), jnp.bfloat16)],
        compiler_params=pltpu.CompilerParams(vmem_limit_bytes=VMEM),
        cost_estimate=LIGHT,
    )(patches, gain_bias, *stats, merge_weight)


def combine(tp_index, order, texts, images, gain_column):
    n_tp = len(texts)
    width, positions = texts[0].shape
    slots = images[0].shape[0]
    count = order.shape[0]
    rows = width * n_tp // count
    share = width // rows

    def body(index_ref, order_ref, gain_ref, *refs):
        text_refs, image_refs = refs[:n_tp], refs[n_tp : 2 * n_tp]
        out_ref, value_ref = refs[2 * n_tp :]
        code = image_refs[0][:, width : width + 2].astype(jnp.float32)
        local = code[:, 0:1] * 256.0 + code[:, 1:2] - 1.0
        place = lax.broadcasted_iota(jnp.int32, (slots, positions), 1).astype(jnp.float32)
        hit = jnp.where(local == place, 1.0, 0.0)
        covered = jnp.max(hit, axis=0, keepdims=True)
        hit = hit.astype(jnp.bfloat16)
        squares = jnp.zeros((1, positions), jnp.float32)
        for distance in range(n_tp):
            first = lax.rem(index_ref[0] + n_tp - distance, n_tp) * share
            image = lax.dot_general(
                image_refs[distance][...],
                hit,
                (((0,), (0,)), ((), ())),
                preferred_element_type=jnp.float32,
            )[:width]
            value = jnp.where(covered > 0.0, image, text_refs[distance][...].astype(jnp.float32))
            squares += jnp.sum(value * value, axis=0, keepdims=True)
            for block in range(share):
                value_ref[first + block] = value[block * rows : (block + 1) * rows]
        scale = lax.rsqrt(squares / (width * n_tp) + EPSILON)
        for block in range(count):
            source = order_ref[block]
            gain = gain_ref[source].astype(jnp.float32)
            out_ref[block] = (value_ref[source] * scale * gain).astype(out_ref.dtype)

    vmem = pl.BlockSpec(memory_space=pltpu.VMEM)
    smem = pl.BlockSpec(memory_space=pltpu.SMEM)
    return pl.pallas_call(
        body,
        out_shape=jax.ShapeDtypeStruct((count, rows, positions), jnp.bfloat16),
        in_specs=[smem, smem] + [vmem] * (1 + 2 * n_tp),
        out_specs=vmem,
        scratch_shapes=[pltpu.VMEM((count, rows, positions), jnp.float32)],
        compiler_params=pltpu.CompilerParams(vmem_limit_bytes=VMEM),
        cost_estimate=LIGHT,
    )(tp_index, order, gain_column, *texts, *images)


def shards(
    n_req, n_tp,
    patches, ln_gain, ln_bias, merge_weight, text_rows, norm_gain, qkv_weight, token_pos, text_len,
):
    row_count, width = text_rows.shape
    me = lax.axis_index("req")
    tp_index = lax.axis_index("tp").reshape(1)
    lines, line_perm, table = ring_tables(n_req)
    x_perm = [(i, i ^ 1) for i in range(n_req)]
    y_perm = [(i, i ^ 2) for i in range(n_req)]
    rows, columns = qkv_weight.shape
    cut = (columns + 255) // 256 * 128
    order = lax.dynamic_slice_in_dim(jnp.asarray(table), me, 1, 0).reshape(-1)

    def along_line(block):
        return lax.ppermute(block, "req", line_perm)

    def to_sides(block):
        return lax.ppermute(block, "req", x_perm), lax.ppermute(block, "req", y_perm)

    def to_corner(by_x, by_y):
        left = lax.ppermute(by_y[:, :cut], "req", x_perm)
        right = lax.ppermute(by_x[:, cut:], "req", y_perm)
        return left, right

    stats_own = row_stats(patches)
    held = [qkv_weight]
    held.append(along_line(held[0]))
    sides = [to_sides(held[0])]
    stats = [stats_own] + [tp_shift(stats_own, n_tp, d) for d in range(1, n_tp)]
    gain_bias = jnp.stack([ln_gain, ln_bias])
    text_turned = text_rows.T
    texts = [text_turned] + [tp_shift(text_turned, n_tp, d) for d in range(1, n_tp)]

    token_count = token_pos.shape[0]
    target = lax.div(token_pos, row_count)
    same = target[:, None] == target[None, :]
    ids = jnp.arange(token_count, dtype=jnp.int32)
    before = jnp.sum((same & (ids[None, :] < ids[:, None])).astype(jnp.int32), axis=1)
    slot = target * IMG_CAP + before
    slot_count = n_req * IMG_CAP
    code = lax.rem(token_pos, row_count) + 1
    code_cols = jnp.stack([lax.div(code, 256), lax.rem(code, 256)], axis=1).astype(jnp.bfloat16)
    gain_column = norm_gain.reshape(n_req, rows, 1)


    stats, held[1], sides[0], gain_bias, gain_column, order, slot, code_cols = tie(
        stats, held[1], sides[0], gain_bias, gain_column, order, slot, code_cols
    )
    held.append(along_line(held[1]))
    sides.append(to_sides(held[1]))
    halves = to_corner(*sides[0])
    partial_value = merge(patches, stats, gain_bias, merge_weight)

    partial_value, held[2], sides[1] = tie(partial_value, held[2], sides[1])
    held.append(along_line(held[2]))
    sides.append(to_sides(held[2]))
    merged = tp_scatter_sum(partial_value, n_tp, 1).astype(jnp.bfloat16)
    merged, halves = tie(merged, halves)
    corners = [jnp.concatenate(halves, axis=1)]
    corners.append(along_line(corners[0]))
    padding = (-width - 2) % 128
    payload = jnp.concatenate(
        [merged, code_cols, jnp.zeros((token_count, padding), jnp.bfloat16)], axis=1
    )
    place = (
        jnp.arange(slot_count, dtype=jnp.int32)[:, None] == slot[None, :]
    ).astype(jnp.bfloat16)
    outgoing = jnp.dot(place, payload, preferred_element_type=jnp.float32).astype(jnp.bfloat16)
    arrived = lax.all_to_all(
        outgoing.reshape(n_req, IMG_CAP, -1), "req", split_axis=0, concat_axis=0
    ).reshape(slot_count, -1)

    held[3], sides[2] = tie(held[3], sides[2])
    sides.append(to_sides(held[3]))
    images = [arrived] + [tp_shift(arrived, n_tp, d) for d in range(1, n_tp)]
    blocks = combine(tp_index, order, texts, images, gain_column)
    blocks, corners[1] = tie(blocks, corners[1])
    for step in range(4, lines):
        held.append(along_line(held[step - 1]))
        sides.append(to_sides(held[step]))
    for step in range(2, lines - 1):
        corners.append(along_line(corners[step - 1]))

    def add_product(total, first, weights):
        weight = jnp.concatenate(weights, axis=0)
        count = weight.shape[0]
        source = blocks[first : first + count // rows].reshape(count, row_count)
        if total is None:
            weight, source = tie(weight, source)
        else:
            weight, source, total = tie(weight, source, total)
        part = lax.dot_general(
            source, weight, (((0,), (0,)), ((), ())), preferred_element_type=jnp.float32
        )
        return part if total is None else total + part

    total = add_product(None, 0, [held[0], *sides[0], corners[0]])
    total = add_product(total, 4, [held[1], *sides[1]])

    total, sides[-1] = tie(total, sides[-1])
    corners.append(jnp.concatenate(to_corner(*sides[-1]), axis=1))
    for step in range(2, lines):
        total = add_product(total, step * 3 + 1, [held[step], *sides[step]])

    position = me * row_count + jnp.arange(row_count, dtype=jnp.int32)
    request_ids = jnp.arange(text_len.shape[0], dtype=jnp.int32)
    limits = jnp.sum(
        jnp.where(
            lax.div(position, SEQ)[:, None] == request_ids[None, :], text_len[None, :], 0
        ),
        axis=1,
    )
    keep = lax.rem(position, SEQ) < limits
    total = add_product(total, lines * 3 + 1, corners[1:])
    return jnp.where(keep[:, None], total, 0.0).astype(jnp.bfloat16)


def solution(mesh):
    placed = (
        P("req", "tp"),
        P("tp"),
        P("tp"),
        P(None, "tp", None),
        P("req", "tp"),
        P(),
        P("req", "tp"),
        P("req"),
        P(),
    )
    body = functools.partial(shards, mesh.shape["req"], mesh.shape["tp"])
    return jax.shard_map(
        body, mesh=mesh, in_specs=placed, out_specs=P("req", "tp"), check_vma=False
    )
```

```python
import functools

import jax
import jax.numpy as jnp
import numpy as np
from jax import lax
from jax.experimental import pallas as pl
from jax.experimental.pallas import tpu as pltpu
from jax.sharding import PartitionSpec as P

DV = 1664
SEQ = 4096
IMG_CAP = 16
EPSILON = 1e-06
VMEM = 32 << 20
LIGHT = pl.CostEstimate(flops=1000, bytes_accessed=1000, transcendentals=0)


def folded_ring(count):
    odd = list(range(1, count, 2))
    even = list(range(0, count, 2))
    return even[:1] + odd + even[:0:-1]


def tp_shift(value, n_tp, distance):
    return lax.ppermute(value, "tp", [(i, (i + distance) % n_tp) for i in range(n_tp)])


def tp_scatter_sum(value, n_tp, axis):
    me = lax.axis_index("tp")
    width = value.shape[axis] // n_tp
    total = lax.dynamic_slice_in_dim(value, me * width, width, axis)
    for distance in range(1, n_tp):
        block = lax.dynamic_slice_in_dim(value, (me + distance) % n_tp * width, width, axis)
        total = total + tp_shift(block, n_tp, distance)
    return total


def ring_tables(n_req):
    lines = n_req // 4
    order = folded_ring(lines)
    following = {order[i]: order[(i + 1) % lines] for i in range(lines)}
    line_perm = [(z * 4 + p, following[z] * 4 + p) for z in range(lines) for p in range(4)]
    arrivals = [(0, flip) for flip in range(4)]
    arrivals += [(step, flip) for step in range(1, lines) for flip in range(3)]
    arrivals += [(step, 3) for step in range(1, lines)]
    table = np.zeros((n_req, n_req), np.int32)
    for index in range(n_req):
        for place, (step, flip) in enumerate(arrivals):
            z = order[(order.index(index // 4) - step) % lines]
            table[index, place] = z * 4 + ((index % 4) ^ flip)
    return lines, line_perm, table


def tie(*values):
    return lax.optimization_barrier(values)


def row_stats(patches):
    rows, _ = patches.shape

    def body(patches_ref, out_ref):
        values = patches_ref[...].astype(jnp.float32)
        sums = jnp.sum(values, axis=1, keepdims=True)
        squares = jnp.sum(values * values, axis=1, keepdims=True)
        out_ref[:, :128] = jnp.broadcast_to(sums, (rows, 128))
        out_ref[:, 128:] = jnp.broadcast_to(squares, (rows, 128))

    vmem = pl.BlockSpec(memory_space=pltpu.VMEM)
    return pl.pallas_call(
        body,
        out_shape=jax.ShapeDtypeStruct((rows, 256), jnp.float32),
        in_specs=[vmem],
        out_specs=vmem,
        compiler_params=pltpu.CompilerParams(vmem_limit_bytes=VMEM),
        cost_estimate=pl.CostEstimate(flops=1000, bytes_accessed=16 << 20, transcendentals=0),
    )(patches)


def merge(patches, stats, gain_bias, merge_weight):
    rows, width = patches.shape
    window, _, features = merge_weight.shape
    tokens = rows // window
    count = len(stats)

    def body(patches_ref, gain_bias_ref, *refs):
        stats_refs, (weight_ref, out_ref, normed_ref) = refs[:count], refs[count:]
        step = pl.program_id(0)

        @pl.when(step == 0)
        def _():
            sums = sum(ref[...] for ref in stats_refs) / DV
            row_mean = sums[:, 0:1]
            row_scale = lax.rsqrt(sums[:, 128:129] - row_mean * row_mean + EPSILON)
            gain_bias = gain_bias_ref[...].astype(jnp.float32)
            normed_ref[...] = (
                (patches_ref[...].astype(jnp.float32) - row_mean) * row_scale * gain_bias[0:1]
                + gain_bias[1:2]
            ).astype(jnp.bfloat16)
            out_ref[...] = jnp.zeros_like(out_ref)

        wanted = lax.broadcasted_iota(jnp.int32, (tokens, rows), 0) * window + step
        chosen = (lax.broadcasted_iota(jnp.int32, (tokens, rows), 1) == wanted).astype(jnp.bfloat16)
        part = jnp.dot(chosen, normed_ref[...], preferred_element_type=jnp.float32)
        out_ref[...] += jnp.dot(
            part.astype(jnp.bfloat16), weight_ref[0], preferred_element_type=jnp.float32
        )

    def whole(shape):
        return pl.BlockSpec(shape, lambda i: (0, 0))

    return pl.pallas_call(
        body,
        out_shape=jax.ShapeDtypeStruct((tokens, features), jnp.float32),
        grid=(window,),
        in_specs=[whole((rows, width)), whole((2, width))]
        + [whole((rows, 256))] * count
        + [pl.BlockSpec((1, width, features), lambda i: (i, 0, 0))],
        out_specs=whole((tokens, features)),
        scratch_shapes=[pltpu.VMEM((rows, width), jnp.bfloat16)],
        compiler_params=pltpu.CompilerParams(vmem_limit_bytes=VMEM),
        cost_estimate=LIGHT,
    )(patches, gain_bias, *stats, merge_weight)


def combine(tp_index, order, texts, images, gain_column):
    n_tp = len(texts)
    width, positions = texts[0].shape
    slots = images[0].shape[0]
    count = order.shape[0]
    rows = width * n_tp // count
    share = width // rows

    def body(index_ref, order_ref, gain_ref, *refs):
        text_refs, image_refs = refs[:n_tp], refs[n_tp : 2 * n_tp]
        out_ref, value_ref = refs[2 * n_tp :]
        code = image_refs[0][:, width : width + 2].astype(jnp.float32)
        local = code[:, 0:1] * 256.0 + code[:, 1:2] - 1.0
        place = lax.broadcasted_iota(jnp.int32, (slots, positions), 1).astype(jnp.float32)
        hit = jnp.where(local == place, 1.0, 0.0)
        covered = jnp.max(hit, axis=0, keepdims=True)
        hit = hit.astype(jnp.bfloat16)
        squares = jnp.zeros((1, positions), jnp.float32)
        for distance in range(n_tp):
            first = lax.rem(index_ref[0] + n_tp - distance, n_tp) * share
            image = lax.dot_general(
                image_refs[distance][...],
                hit,
                (((0,), (0,)), ((), ())),
                preferred_element_type=jnp.float32,
            )[:width]
            value = jnp.where(covered > 0.0, image, text_refs[distance][...].astype(jnp.float32))
            squares += jnp.sum(value * value, axis=0, keepdims=True)
            for block in range(share):
                value_ref[first + block] = value[block * rows : (block + 1) * rows]
        scale = lax.rsqrt(squares / (width * n_tp) + EPSILON)
        for block in range(count):
            source = order_ref[block]
            gain = gain_ref[source].astype(jnp.float32)
            out_ref[block] = (value_ref[source] * scale * gain).astype(out_ref.dtype)

    vmem = pl.BlockSpec(memory_space=pltpu.VMEM)
    smem = pl.BlockSpec(memory_space=pltpu.SMEM)
    return pl.pallas_call(
        body,
        out_shape=jax.ShapeDtypeStruct((count, rows, positions), jnp.bfloat16),
        in_specs=[smem, smem] + [vmem] * (1 + 2 * n_tp),
        out_specs=vmem,
        scratch_shapes=[pltpu.VMEM((count, rows, positions), jnp.float32)],
        compiler_params=pltpu.CompilerParams(vmem_limit_bytes=VMEM),
        cost_estimate=LIGHT,
    )(tp_index, order, gain_column, *texts, *images)


def shards(
    n_req, n_tp,
    patches, ln_gain, ln_bias, merge_weight, text_rows, norm_gain, qkv_weight, token_pos, text_len,
):
    row_count, width = text_rows.shape
    me = lax.axis_index("req")
    tp_index = lax.axis_index("tp").reshape(1)
    lines, line_perm, table = ring_tables(n_req)
    x_perm = [(i, i ^ 1) for i in range(n_req)]
    y_perm = [(i, i ^ 2) for i in range(n_req)]
    corner_perm = [(i, i ^ 3) for i in range(n_req)]
    rows, columns = qkv_weight.shape
    order = lax.dynamic_slice_in_dim(jnp.asarray(table), me, 1, 0).reshape(-1)

    def along_line(block):
        return lax.ppermute(block, "req", line_perm)

    def to_sides(block):
        return lax.ppermute(block, "req", x_perm), lax.ppermute(block, "req", y_perm)

    def to_corner(block):
        return lax.ppermute(block, "req", corner_perm)

    held = [qkv_weight]
    held.append(along_line(held[0]))
    sides = [to_sides(held[0])]
    corners = [to_corner(held[0])]
    stats_own = row_stats(patches)
    stats = [stats_own] + [tp_shift(stats_own, n_tp, d) for d in range(1, n_tp)]
    gain_bias = jnp.stack([ln_gain, ln_bias])
    text_turned = text_rows.T
    texts = [text_turned] + [tp_shift(text_turned, n_tp, d) for d in range(1, n_tp)]

    token_count = token_pos.shape[0]
    target = lax.div(token_pos, row_count)
    same = target[:, None] == target[None, :]
    ids = jnp.arange(token_count, dtype=jnp.int32)
    before = jnp.sum((same & (ids[None, :] < ids[:, None])).astype(jnp.int32), axis=1)
    slot = target * IMG_CAP + before
    slot_count = n_req * IMG_CAP
    code = lax.rem(token_pos, row_count) + 1
    code_cols = jnp.stack([lax.div(code, 256), lax.rem(code, 256)], axis=1).astype(jnp.bfloat16)
    gain_column = norm_gain.reshape(n_req, rows, 1)

    partial_value = merge(patches, stats, gain_bias, merge_weight)

    partial_value, held[1], sides[0], gain_column, order, slot, code_cols = tie(
        partial_value, held[1], sides[0], gain_column, order, slot, code_cols
    )
    held.append(along_line(held[1]))
    sides.append(to_sides(held[1]))
    merged = tp_scatter_sum(partial_value, n_tp, 1).astype(jnp.bfloat16)
    padding = (-width - 2) % 128
    payload = jnp.concatenate(
        [merged, code_cols, jnp.zeros((token_count, padding), jnp.bfloat16)], axis=1
    )
    place = (
        jnp.arange(slot_count, dtype=jnp.int32)[:, None] == slot[None, :]
    ).astype(jnp.bfloat16)
    outgoing = jnp.dot(place, payload, preferred_element_type=jnp.float32).astype(jnp.bfloat16)
    outgoing, corners[0] = tie(outgoing, corners[0])
    arrived = lax.all_to_all(
        outgoing.reshape(n_req, IMG_CAP, -1), "req", split_axis=0, concat_axis=0
    ).reshape(slot_count, -1)

    held[2], sides[1], corners[0] = tie(held[2], sides[1], corners[0])
    held.append(along_line(held[2]))
    sides.append(to_sides(held[2]))
    images = [arrived] + [tp_shift(arrived, n_tp, d) for d in range(1, n_tp)]
    blocks = combine(tp_index, order, texts, images, gain_column)

    corners.append(along_line(corners[0]))
    held[3], sides[2] = tie(held[3], sides[2])
    sides.append(to_sides(held[3]))
    for step in range(4, lines):
        held.append(along_line(held[step - 1]))
        sides.append(to_sides(held[step]))
    corner_last = to_corner(held[-1])

    def add_product(total, first, weights):
        weight = jnp.concatenate(weights, axis=0)
        count = weight.shape[0]
        source = blocks[first : first + count // rows].reshape(count, row_count)
        if total is None:
            weight, source = tie(weight, source)
        else:
            weight, source, total = tie(weight, source, total)
        part = lax.dot_general(
            source, weight, (((0,), (0,)), ((), ())), preferred_element_type=jnp.float32
        )
        return part if total is None else total + part

    total = add_product(None, 0, [held[0], *sides[0], corners[0]])
    total, corners[1] = tie(total, corners[1])
    for step in range(2, lines - 1):
        corners.append(along_line(corners[step - 1]))
    corners.append(corner_last)
    for step in range(1, lines):
        total = add_product(total, step * 3 + 1, [held[step], *sides[step]])

    position = me * row_count + jnp.arange(row_count, dtype=jnp.int32)
    request_ids = jnp.arange(text_len.shape[0], dtype=jnp.int32)
    limits = jnp.sum(
        jnp.where(
            lax.div(position, SEQ)[:, None] == request_ids[None, :], text_len[None, :], 0
        ),
        axis=1,
    )
    keep = lax.rem(position, SEQ) < limits
    total = add_product(total, lines * 3 + 1, corners[1:])
    return jnp.where(keep[:, None], total, 0.0).astype(jnp.bfloat16)


def solution(mesh):
    placed = (
        P("req", "tp"),
        P("tp"),
        P("tp"),
        P(None, "tp", None),
        P("req", "tp"),
        P(),
        P("req", "tp"),
        P("req"),
        P(),
    )
    body = functools.partial(shards, mesh.shape["req"], mesh.shape["tp"])
    return jax.shard_map(
        body, mesh=mesh, in_specs=placed, out_specs=P("req", "tp"), check_vma=False
    )
```

```python
import functools

import jax
import jax.numpy as jnp
import numpy as np
from jax import lax
from jax.experimental import pallas as pl
from jax.experimental.pallas import tpu as pltpu
from jax.sharding import PartitionSpec as P

DV = 1664
SEQ = 4096
IMG_CAP = 16
EPSILON = 1e-06
VMEM = 32 << 20
LIGHT = pl.CostEstimate(flops=1000, bytes_accessed=1000, transcendentals=0)


def folded_ring(count):
    odd = list(range(1, count, 2))
    even = list(range(0, count, 2))
    return even[:1] + odd + even[:0:-1]


def tp_shift(value, n_tp, distance):
    return lax.ppermute(value, "tp", [(i, (i + distance) % n_tp) for i in range(n_tp)])


def tp_scatter_sum(value, n_tp, axis):
    me = lax.axis_index("tp")
    width = value.shape[axis] // n_tp
    total = lax.dynamic_slice_in_dim(value, me * width, width, axis)
    for distance in range(1, n_tp):
        block = lax.dynamic_slice_in_dim(value, (me + distance) % n_tp * width, width, axis)
        total = total + tp_shift(block, n_tp, distance)
    return total


def ring_tables(n_req):
    lines = n_req // 4
    order = folded_ring(lines)
    following = {order[i]: order[(i + 1) % lines] for i in range(lines)}
    line_perm = [(z * 4 + p, following[z] * 4 + p) for z in range(lines) for p in range(4)]
    arrivals = [(0, flip) for flip in range(4)]
    arrivals += [(step, flip) for step in range(1, lines) for flip in range(3)]
    arrivals += [(step, 3) for step in range(1, lines)]
    table = np.zeros((n_req, n_req), np.int32)
    for index in range(n_req):
        for place, (step, flip) in enumerate(arrivals):
            z = order[(order.index(index // 4) - step) % lines]
            table[index, place] = z * 4 + ((index % 4) ^ flip)
    return lines, line_perm, table


def tie(*values):
    return lax.optimization_barrier(values)


def row_stats(patches):
    rows, _ = patches.shape

    def body(patches_ref, out_ref):
        values = patches_ref[...].astype(jnp.float32)
        sums = jnp.sum(values, axis=1, keepdims=True)
        squares = jnp.sum(values * values, axis=1, keepdims=True)
        out_ref[:, :128] = jnp.broadcast_to(sums, (rows, 128))
        out_ref[:, 128:] = jnp.broadcast_to(squares, (rows, 128))

    vmem = pl.BlockSpec(memory_space=pltpu.VMEM)
    return pl.pallas_call(
        body,
        out_shape=jax.ShapeDtypeStruct((rows, 256), jnp.float32),
        in_specs=[vmem],
        out_specs=vmem,
        compiler_params=pltpu.CompilerParams(vmem_limit_bytes=VMEM),
        cost_estimate=pl.CostEstimate(flops=1000, bytes_accessed=16 << 20, transcendentals=0),
    )(patches)


def merge(patches, stats, gain_bias, merge_weight):
    rows, width = patches.shape
    window, _, features = merge_weight.shape
    tokens = rows // window
    count = len(stats)

    def body(patches_ref, gain_bias_ref, *refs):
        stats_refs, (weight_ref, out_ref, normed_ref) = refs[:count], refs[count:]
        step = pl.program_id(0)

        @pl.when(step == 0)
        def _():
            sums = sum(ref[...] for ref in stats_refs) / DV
            row_mean = sums[:, 0:1]
            row_scale = lax.rsqrt(sums[:, 128:129] - row_mean * row_mean + EPSILON)
            gain_bias = gain_bias_ref[...].astype(jnp.float32)
            normed_ref[...] = (
                (patches_ref[...].astype(jnp.float32) - row_mean) * row_scale * gain_bias[0:1]
                + gain_bias[1:2]
            ).astype(jnp.bfloat16)
            out_ref[...] = jnp.zeros_like(out_ref)

        wanted = lax.broadcasted_iota(jnp.int32, (tokens, rows), 0) * window + step
        chosen = (lax.broadcasted_iota(jnp.int32, (tokens, rows), 1) == wanted).astype(jnp.bfloat16)
        part = jnp.dot(chosen, normed_ref[...], preferred_element_type=jnp.float32)
        out_ref[...] += jnp.dot(
            part.astype(jnp.bfloat16), weight_ref[0], preferred_element_type=jnp.float32
        )

    def whole(shape):
        return pl.BlockSpec(shape, lambda i: (0, 0))

    return pl.pallas_call(
        body,
        out_shape=jax.ShapeDtypeStruct((tokens, features), jnp.float32),
        grid=(window,),
        in_specs=[whole((rows, width)), whole((2, width))]
        + [whole((rows, 256))] * count
        + [pl.BlockSpec((1, width, features), lambda i: (i, 0, 0))],
        out_specs=whole((tokens, features)),
        scratch_shapes=[pltpu.VMEM((rows, width), jnp.bfloat16)],
        compiler_params=pltpu.CompilerParams(vmem_limit_bytes=VMEM),
        cost_estimate=LIGHT,
    )(patches, gain_bias, *stats, merge_weight)


def combine(tp_index, order, texts, images, gain_column):
    n_tp = len(texts)
    width, positions = texts[0].shape
    slots = images[0].shape[0]
    count = order.shape[0]
    rows = width * n_tp // count
    share = width // rows

    def body(index_ref, order_ref, gain_ref, *refs):
        text_refs, image_refs = refs[:n_tp], refs[n_tp : 2 * n_tp]
        out_ref, value_ref = refs[2 * n_tp :]
        code = image_refs[0][:, width : width + 2].astype(jnp.float32)
        local = code[:, 0:1] * 256.0 + code[:, 1:2] - 1.0
        place = lax.broadcasted_iota(jnp.int32, (slots, positions), 1).astype(jnp.float32)
        hit = jnp.where(local == place, 1.0, 0.0)
        covered = jnp.max(hit, axis=0, keepdims=True)
        hit = hit.astype(jnp.bfloat16)
        squares = jnp.zeros((1, positions), jnp.float32)
        for distance in range(n_tp):
            first = lax.rem(index_ref[0] + n_tp - distance, n_tp) * share
            image = lax.dot_general(
                image_refs[distance][...],
                hit,
                (((0,), (0,)), ((), ())),
                preferred_element_type=jnp.float32,
            )[:width]
            value = jnp.where(covered > 0.0, image, text_refs[distance][...].astype(jnp.float32))
            squares += jnp.sum(value * value, axis=0, keepdims=True)
            for block in range(share):
                value_ref[first + block] = value[block * rows : (block + 1) * rows]
        scale = lax.rsqrt(squares / (width * n_tp) + EPSILON)
        for block in range(count):
            source = order_ref[block]
            gain = gain_ref[source].astype(jnp.float32)
            out_ref[block] = (value_ref[source] * scale * gain).astype(out_ref.dtype)

    vmem = pl.BlockSpec(memory_space=pltpu.VMEM)
    smem = pl.BlockSpec(memory_space=pltpu.SMEM)
    return pl.pallas_call(
        body,
        out_shape=jax.ShapeDtypeStruct((count, rows, positions), jnp.bfloat16),
        in_specs=[smem, smem] + [vmem] * (1 + 2 * n_tp),
        out_specs=vmem,
        scratch_shapes=[pltpu.VMEM((count, rows, positions), jnp.float32)],
        compiler_params=pltpu.CompilerParams(vmem_limit_bytes=VMEM),
        cost_estimate=LIGHT,
    )(tp_index, order, gain_column, *texts, *images)


def shards(
    n_req, n_tp,
    patches, ln_gain, ln_bias, merge_weight, text_rows, norm_gain, qkv_weight, token_pos, text_len,
):
    row_count, width = text_rows.shape
    me = lax.axis_index("req")
    tp_index = lax.axis_index("tp").reshape(1)
    lines, line_perm, table = ring_tables(n_req)
    x_perm = [(i, i ^ 1) for i in range(n_req)]
    y_perm = [(i, i ^ 2) for i in range(n_req)]
    rows, columns = qkv_weight.shape
    cut = (columns + 255) // 256 * 128
    order = lax.dynamic_slice_in_dim(jnp.asarray(table), me, 1, 0).reshape(-1)

    def along_line(block):
        return lax.ppermute(block, "req", line_perm)

    def to_sides(block):
        return lax.ppermute(block, "req", x_perm), lax.ppermute(block, "req", y_perm)

    def to_corner(by_x, by_y):
        left = lax.ppermute(by_y[:, :cut], "req", x_perm)
        right = lax.ppermute(by_x[:, cut:], "req", y_perm)
        return jnp.concatenate([left, right], axis=1)

    held = [qkv_weight]
    held.append(along_line(held[0]))
    sides = [to_sides(held[0])]
    corners = []
    stats_own = row_stats(patches)
    stats = [stats_own] + [tp_shift(stats_own, n_tp, d) for d in range(1, n_tp)]
    gain_bias = jnp.stack([ln_gain, ln_bias])
    text_turned = text_rows.T
    texts = [text_turned] + [tp_shift(text_turned, n_tp, d) for d in range(1, n_tp)]

    token_count = token_pos.shape[0]
    target = lax.div(token_pos, row_count)
    same = target[:, None] == target[None, :]
    ids = jnp.arange(token_count, dtype=jnp.int32)
    before = jnp.sum((same & (ids[None, :] < ids[:, None])).astype(jnp.int32), axis=1)
    slot = target * IMG_CAP + before
    slot_count = n_req * IMG_CAP
    code = lax.rem(token_pos, row_count) + 1
    code_cols = jnp.stack([lax.div(code, 256), lax.rem(code, 256)], axis=1).astype(jnp.bfloat16)
    gain_column = norm_gain.reshape(n_req, rows, 1)

    partial_value = merge(patches, stats, gain_bias, merge_weight)

    partial_value, held[1], sides[0], gain_column, order, slot, code_cols = tie(
        partial_value, held[1], sides[0], gain_column, order, slot, code_cols
    )
    held.append(along_line(held[1]))
    sides.append(to_sides(held[1]))
    corners.append(to_corner(*sides[0]))
    merged = tp_scatter_sum(partial_value, n_tp, 1).astype(jnp.bfloat16)
    padding = (-width - 2) % 128
    payload = jnp.concatenate(
        [merged, code_cols, jnp.zeros((token_count, padding), jnp.bfloat16)], axis=1
    )
    place = (
        jnp.arange(slot_count, dtype=jnp.int32)[:, None] == slot[None, :]
    ).astype(jnp.bfloat16)
    outgoing = jnp.dot(place, payload, preferred_element_type=jnp.float32).astype(jnp.bfloat16)
    arrived = lax.all_to_all(
        outgoing.reshape(n_req, IMG_CAP, -1), "req", split_axis=0, concat_axis=0
    ).reshape(slot_count, -1)

    held[2], sides[1] = tie(held[2], sides[1])
    held.append(along_line(held[2]))
    sides.append(to_sides(held[2]))
    images = [arrived] + [tp_shift(arrived, n_tp, d) for d in range(1, n_tp)]
    blocks = combine(tp_index, order, texts, images, gain_column)

    corners.append(along_line(corners[0]))
    blocks, corners[1] = tie(blocks, corners[1])
    held[3], sides[2] = tie(held[3], sides[2])
    sides.append(to_sides(held[3]))
    for step in range(4, lines):
        held.append(along_line(held[step - 1]))
        sides.append(to_sides(held[step]))
    for step in range(2, lines - 1):
        corners.append(along_line(corners[step - 1]))

    def add_product(total, first, weights):
        weight = jnp.concatenate(weights, axis=0)
        count = weight.shape[0]
        source = blocks[first : first + count // rows].reshape(count, row_count)
        if total is None:
            weight, source = tie(weight, source)
        else:
            weight, source, total = tie(weight, source, total)
        part = lax.dot_general(
            source, weight, (((0,), (0,)), ((), ())), preferred_element_type=jnp.float32
        )
        return part if total is None else total + part

    total = add_product(None, 0, [held[0], *sides[0], corners[0]])
    total = add_product(total, 4, [held[1], *sides[1]])

    total, sides[-1] = tie(total, sides[-1])
    corners.append(to_corner(*sides[-1]))
    for step in range(2, lines):
        total = add_product(total, step * 3 + 1, [held[step], *sides[step]])

    position = me * row_count + jnp.arange(row_count, dtype=jnp.int32)
    request_ids = jnp.arange(text_len.shape[0], dtype=jnp.int32)
    limits = jnp.sum(
        jnp.where(
            lax.div(position, SEQ)[:, None] == request_ids[None, :], text_len[None, :], 0
        ),
        axis=1,
    )
    keep = lax.rem(position, SEQ) < limits
    total = add_product(total, lines * 3 + 1, corners[1:])
    return jnp.where(keep[:, None], total, 0.0).astype(jnp.bfloat16)


def solution(mesh):
    placed = (
        P("req", "tp"),
        P("tp"),
        P("tp"),
        P(None, "tp", None),
        P("req", "tp"),
        P(),
        P("req", "tp"),
        P("req"),
        P(),
    )
    body = functools.partial(shards, mesh.shape["req"], mesh.shape["tp"])
    return jax.shard_map(
        body, mesh=mesh, in_specs=placed, out_specs=P("req", "tp"), check_vma=False
    )
```

```python
import functools

import jax
import jax.numpy as jnp
import numpy as np
from jax import lax
from jax.experimental import pallas as pl
from jax.experimental.pallas import tpu as pltpu
from jax.sharding import PartitionSpec as P

DV = 1664
SEQ = 4096
IMG_CAP = 16
EPSILON = 1e-06
VMEM = 32 << 20
LIGHT = pl.CostEstimate(flops=1000, bytes_accessed=1000, transcendentals=0)


def folded_ring(count):
    odd = list(range(1, count, 2))
    even = list(range(0, count, 2))
    return even[:1] + odd + even[:0:-1]


def tp_shift(value, n_tp, distance):
    return lax.ppermute(value, "tp", [(i, (i + distance) % n_tp) for i in range(n_tp)])


def tp_scatter_sum(value, n_tp, axis):
    me = lax.axis_index("tp")
    width = value.shape[axis] // n_tp
    total = lax.dynamic_slice_in_dim(value, me * width, width, axis)
    for distance in range(1, n_tp):
        block = lax.dynamic_slice_in_dim(value, (me + distance) % n_tp * width, width, axis)
        total = total + tp_shift(block, n_tp, distance)
    return total


def ring_tables(n_req):
    lines = n_req // 4
    order = folded_ring(lines)
    following = {order[i]: order[(i + 1) % lines] for i in range(lines)}
    line_perm = [(z * 4 + p, following[z] * 4 + p) for z in range(lines) for p in range(4)]
    arrivals = [(0, flip) for flip in range(4)]
    arrivals += [(step, flip) for step in range(1, lines) for flip in range(3)]
    arrivals += [(step, 3) for step in range(1, lines)]
    table = np.zeros((n_req, n_req), np.int32)
    for index in range(n_req):
        for place, (step, flip) in enumerate(arrivals):
            z = order[(order.index(index // 4) - step) % lines]
            table[index, place] = z * 4 + ((index % 4) ^ flip)
    return lines, line_perm, table


def tie(*values):
    return lax.optimization_barrier(values)


def row_stats(patches):
    rows, _ = patches.shape

    def body(patches_ref, out_ref):
        values = patches_ref[...].astype(jnp.float32)
        sums = jnp.sum(values, axis=1, keepdims=True)
        squares = jnp.sum(values * values, axis=1, keepdims=True)
        out_ref[:, :128] = jnp.broadcast_to(sums, (rows, 128))
        out_ref[:, 128:] = jnp.broadcast_to(squares, (rows, 128))

    vmem = pl.BlockSpec(memory_space=pltpu.VMEM)
    return pl.pallas_call(
        body,
        out_shape=jax.ShapeDtypeStruct((rows, 256), jnp.float32),
        in_specs=[vmem],
        out_specs=vmem,
        compiler_params=pltpu.CompilerParams(vmem_limit_bytes=VMEM),
        cost_estimate=pl.CostEstimate(flops=1000, bytes_accessed=16 << 20, transcendentals=0),
    )(patches)


def merge(patches, stats, gain_bias, merge_weight):
    rows, width = patches.shape
    window, _, features = merge_weight.shape
    tokens = rows // window
    count = len(stats)

    def body(patches_ref, gain_bias_ref, *refs):
        stats_refs, (weight_ref, out_ref, normed_ref) = refs[:count], refs[count:]
        step = pl.program_id(0)

        @pl.when(step == 0)
        def _():
            sums = sum(ref[...] for ref in stats_refs) / DV
            row_mean = sums[:, 0:1]
            row_scale = lax.rsqrt(sums[:, 128:129] - row_mean * row_mean + EPSILON)
            gain_bias = gain_bias_ref[...].astype(jnp.float32)
            normed_ref[...] = (
                (patches_ref[...].astype(jnp.float32) - row_mean) * row_scale * gain_bias[0:1]
                + gain_bias[1:2]
            ).astype(jnp.bfloat16)
            out_ref[...] = jnp.zeros_like(out_ref)

        wanted = lax.broadcasted_iota(jnp.int32, (tokens, rows), 0) * window + step
        chosen = (lax.broadcasted_iota(jnp.int32, (tokens, rows), 1) == wanted).astype(jnp.bfloat16)
        part = jnp.dot(chosen, normed_ref[...], preferred_element_type=jnp.float32)
        out_ref[...] += jnp.dot(
            part.astype(jnp.bfloat16), weight_ref[0], preferred_element_type=jnp.float32
        )

    def whole(shape):
        return pl.BlockSpec(shape, lambda i: (0, 0))

    return pl.pallas_call(
        body,
        out_shape=jax.ShapeDtypeStruct((tokens, features), jnp.float32),
        grid=(window,),
        in_specs=[whole((rows, width)), whole((2, width))]
        + [whole((rows, 256))] * count
        + [pl.BlockSpec((1, width, features), lambda i: (i, 0, 0))],
        out_specs=whole((tokens, features)),
        scratch_shapes=[pltpu.VMEM((rows, width), jnp.bfloat16)],
        compiler_params=pltpu.CompilerParams(vmem_limit_bytes=VMEM),
        cost_estimate=LIGHT,
    )(patches, gain_bias, *stats, merge_weight)


def combine(tp_index, order, texts, images, gain_column):
    n_tp = len(texts)
    width, positions = texts[0].shape
    slots = images[0].shape[0]
    count = order.shape[0]
    rows = width * n_tp // count
    share = width // rows

    def body(index_ref, order_ref, gain_ref, *refs):
        text_refs, image_refs = refs[:n_tp], refs[n_tp : 2 * n_tp]
        out_ref, value_ref = refs[2 * n_tp :]
        code = image_refs[0][:, width : width + 2].astype(jnp.float32)
        local = code[:, 0:1] * 256.0 + code[:, 1:2] - 1.0
        place = lax.broadcasted_iota(jnp.int32, (slots, positions), 1).astype(jnp.float32)
        hit = jnp.where(local == place, 1.0, 0.0)
        covered = jnp.max(hit, axis=0, keepdims=True)
        hit = hit.astype(jnp.bfloat16)
        squares = jnp.zeros((1, positions), jnp.float32)
        for distance in range(n_tp):
            first = lax.rem(index_ref[0] + n_tp - distance, n_tp) * share
            image = lax.dot_general(
                image_refs[distance][...],
                hit,
                (((0,), (0,)), ((), ())),
                preferred_element_type=jnp.float32,
            )[:width]
            value = jnp.where(covered > 0.0, image, text_refs[distance][...].astype(jnp.float32))
            squares += jnp.sum(value * value, axis=0, keepdims=True)
            for block in range(share):
                value_ref[first + block] = value[block * rows : (block + 1) * rows]
        scale = lax.rsqrt(squares / (width * n_tp) + EPSILON)
        for block in range(count):
            source = order_ref[block]
            gain = gain_ref[source].astype(jnp.float32)
            out_ref[block] = (value_ref[source] * scale * gain).astype(out_ref.dtype)

    vmem = pl.BlockSpec(memory_space=pltpu.VMEM)
    smem = pl.BlockSpec(memory_space=pltpu.SMEM)
    return pl.pallas_call(
        body,
        out_shape=jax.ShapeDtypeStruct((count, rows, positions), jnp.bfloat16),
        in_specs=[smem, smem] + [vmem] * (1 + 2 * n_tp),
        out_specs=vmem,
        scratch_shapes=[pltpu.VMEM((count, rows, positions), jnp.float32)],
        compiler_params=pltpu.CompilerParams(vmem_limit_bytes=VMEM),
        cost_estimate=LIGHT,
    )(tp_index, order, gain_column, *texts, *images)


def shards(
    n_req, n_tp,
    patches, ln_gain, ln_bias, merge_weight, text_rows, norm_gain, qkv_weight, token_pos, text_len,
):
    row_count, width = text_rows.shape
    me = lax.axis_index("req")
    tp_index = lax.axis_index("tp").reshape(1)
    lines, line_perm, table = ring_tables(n_req)
    x_perm = [(i, i ^ 1) for i in range(n_req)]
    y_perm = [(i, i ^ 2) for i in range(n_req)]
    rows, columns = qkv_weight.shape
    cut = (columns + 255) // 256 * 128
    order = lax.dynamic_slice_in_dim(jnp.asarray(table), me, 1, 0).reshape(-1)

    def along_line(block):
        return lax.ppermute(block, "req", line_perm)

    def to_sides(block):
        return lax.ppermute(block, "req", x_perm), lax.ppermute(block, "req", y_perm)

    def to_corner(by_x, by_y):
        left = lax.ppermute(by_y[:, :cut], "req", x_perm)
        right = lax.ppermute(by_x[:, cut:], "req", y_perm)
        return jnp.concatenate([left, right], axis=1)

    held = [qkv_weight]
    held.append(along_line(held[0]))
    sides = [to_sides(held[0])]
    corners = []
    stats_own = row_stats(patches)
    stats = [stats_own] + [tp_shift(stats_own, n_tp, d) for d in range(1, n_tp)]
    gain_bias = jnp.stack([ln_gain, ln_bias])
    text_turned = text_rows.T
    texts = [text_turned] + [tp_shift(text_turned, n_tp, d) for d in range(1, n_tp)]

    token_count = token_pos.shape[0]
    target = lax.div(token_pos, row_count)
    same = target[:, None] == target[None, :]
    ids = jnp.arange(token_count, dtype=jnp.int32)
    before = jnp.sum((same & (ids[None, :] < ids[:, None])).astype(jnp.int32), axis=1)
    slot = target * IMG_CAP + before
    slot_count = n_req * IMG_CAP
    code = lax.rem(token_pos, row_count) + 1
    code_cols = jnp.stack([lax.div(code, 256), lax.rem(code, 256)], axis=1).astype(jnp.bfloat16)
    gain_column = norm_gain.reshape(n_req, rows, 1)

    partial_value = merge(patches, stats, gain_bias, merge_weight)

    partial_value, held[1], sides[0], gain_column, order, slot, code_cols = tie(
        partial_value, held[1], sides[0], gain_column, order, slot, code_cols
    )
    held.append(along_line(held[1]))
    sides.append(to_sides(held[1]))
    corners.append(to_corner(*sides[0]))
    merged = tp_scatter_sum(partial_value, n_tp, 1).astype(jnp.bfloat16)
    padding = (-width - 2) % 128
    payload = jnp.concatenate(
        [merged, code_cols, jnp.zeros((token_count, padding), jnp.bfloat16)], axis=1
    )
    place = (
        jnp.arange(slot_count, dtype=jnp.int32)[:, None] == slot[None, :]
    ).astype(jnp.bfloat16)
    outgoing = jnp.dot(place, payload, preferred_element_type=jnp.float32).astype(jnp.bfloat16)
    arrived = lax.all_to_all(
        outgoing.reshape(n_req, IMG_CAP, -1), "req", split_axis=0, concat_axis=0
    ).reshape(slot_count, -1)

    held[2], sides[1] = tie(held[2], sides[1])
    held.append(along_line(held[2]))
    sides.append(to_sides(held[2]))
    images = [arrived] + [tp_shift(arrived, n_tp, d) for d in range(1, n_tp)]
    blocks = combine(tp_index, order, texts, images, gain_column)

    held[3], corners[0] = tie(held[3], corners[0])
    corners.append(along_line(corners[0]))
    held[3], sides[2] = tie(held[3], sides[2])
    sides.append(to_sides(held[3]))
    for step in range(4, lines):
        held.append(along_line(held[step - 1]))
        sides.append(to_sides(held[step]))
    for step in range(2, lines - 2):
        corners.append(along_line(corners[step - 1]))
    corners.append(to_corner(*sides[-2]))

    def add_product(total, first, weights):
        weight = jnp.concatenate(weights, axis=0)
        count = weight.shape[0]
        source = blocks[first : first + count // rows].reshape(count, row_count)
        if total is None:
            weight, source = tie(weight, source)
        else:
            weight, source, total = tie(weight, source, total)
        part = lax.dot_general(
            source, weight, (((0,), (0,)), ((), ())), preferred_element_type=jnp.float32
        )
        return part if total is None else total + part

    total = add_product(None, 0, [held[0], *sides[0], corners[0]])
    total = add_product(total, 4, [held[1], *sides[1]])

    total, sides[-1] = tie(total, sides[-1])
    corners.append(to_corner(*sides[-1]))
    for step in range(2, lines):
        total = add_product(total, step * 3 + 1, [held[step], *sides[step]])

    position = me * row_count + jnp.arange(row_count, dtype=jnp.int32)
    request_ids = jnp.arange(text_len.shape[0], dtype=jnp.int32)
    limits = jnp.sum(
        jnp.where(
            lax.div(position, SEQ)[:, None] == request_ids[None, :], text_len[None, :], 0
        ),
        axis=1,
    )
    keep = lax.rem(position, SEQ) < limits
    total = add_product(total, lines * 3 + 1, corners[1:])
    return jnp.where(keep[:, None], total, 0.0).astype(jnp.bfloat16)


def solution(mesh):
    placed = (
        P("req", "tp"),
        P("tp"),
        P("tp"),
        P(None, "tp", None),
        P("req", "tp"),
        P(),
        P("req", "tp"),
        P("req"),
        P(),
    )
    body = functools.partial(shards, mesh.shape["req"], mesh.shape["tp"])
    return jax.shard_map(
        body, mesh=mesh, in_specs=placed, out_specs=P("req", "tp"), check_vma=False
    )
```

```python
import functools

import jax
import jax.numpy as jnp
import numpy as np
from jax import lax
from jax.experimental import pallas as pl
from jax.experimental.pallas import tpu as pltpu
from jax.sharding import PartitionSpec as P

DV = 1664
SEQ = 4096
IMG_CAP = 16
EPSILON = 1e-06
VMEM = 32 << 20
LIGHT = pl.CostEstimate(flops=1000, bytes_accessed=1000, transcendentals=0)


def folded_ring(count):
    odd = list(range(1, count, 2))
    even = list(range(0, count, 2))
    return even[:1] + odd + even[:0:-1]


def tp_shift(value, n_tp, distance):
    return lax.ppermute(value, "tp", [(i, (i + distance) % n_tp) for i in range(n_tp)])


def tp_scatter_sum(value, n_tp, axis):
    me = lax.axis_index("tp")
    width = value.shape[axis] // n_tp
    total = lax.dynamic_slice_in_dim(value, me * width, width, axis)
    for distance in range(1, n_tp):
        block = lax.dynamic_slice_in_dim(value, (me + distance) % n_tp * width, width, axis)
        total = total + tp_shift(block, n_tp, distance)
    return total


def ring_tables(n_req):
    lines = n_req // 4
    order = folded_ring(lines)
    following = {order[i]: order[(i + 1) % lines] for i in range(lines)}
    line_perm = [(z * 4 + p, following[z] * 4 + p) for z in range(lines) for p in range(4)]
    arrivals = [(0, flip) for flip in range(4)]
    arrivals += [(step, flip) for step in range(1, lines) for flip in range(3)]
    arrivals += [(step, 3) for step in range(1, lines)]
    table = np.zeros((n_req, n_req), np.int32)
    for index in range(n_req):
        for place, (step, flip) in enumerate(arrivals):
            z = order[(order.index(index // 4) - step) % lines]
            table[index, place] = z * 4 + ((index % 4) ^ flip)
    return lines, line_perm, table


def tie(*values):
    return lax.optimization_barrier(values)


def row_stats(patches):
    rows, _ = patches.shape

    def body(patches_ref, out_ref):
        values = patches_ref[...].astype(jnp.float32)
        sums = jnp.sum(values, axis=1, keepdims=True)
        squares = jnp.sum(values * values, axis=1, keepdims=True)
        out_ref[:, :128] = jnp.broadcast_to(sums, (rows, 128))
        out_ref[:, 128:] = jnp.broadcast_to(squares, (rows, 128))

    vmem = pl.BlockSpec(memory_space=pltpu.VMEM)
    return pl.pallas_call(
        body,
        out_shape=jax.ShapeDtypeStruct((rows, 256), jnp.float32),
        in_specs=[vmem],
        out_specs=vmem,
        compiler_params=pltpu.CompilerParams(vmem_limit_bytes=VMEM),
        cost_estimate=pl.CostEstimate(flops=1000, bytes_accessed=16 << 20, transcendentals=0),
    )(patches)


def row_chunks(width):
    chunks = [(first, 256) for first in range(0, width - 255, 256)]
    rest = width % 256
    if rest:
        chunks.append((width - rest, rest))
    if any(first % size for first, size in chunks):
        return [(0, width)]
    return chunks


def merge(patches, stats, gain_bias, merge_weight):
    rows, width = patches.shape
    window, _, features = merge_weight.shape
    tokens = rows // window
    count = len(stats)
    chunks = row_chunks(width)

    def body(patches_ref, gain_bias_ref, *refs):
        stats_refs, (*weight_refs, out_ref, normed_ref) = refs[:count], refs[count:]
        step = pl.program_id(0)

        @pl.when(step == 0)
        def _():
            sums = sum(ref[...] for ref in stats_refs) / DV
            row_mean = sums[:, 0:1]
            row_scale = lax.rsqrt(sums[:, 128:129] - row_mean * row_mean + EPSILON)
            gain_bias = gain_bias_ref[...].astype(jnp.float32)
            normed_ref[...] = (
                (patches_ref[...].astype(jnp.float32) - row_mean) * row_scale * gain_bias[0:1]
                + gain_bias[1:2]
            ).astype(jnp.bfloat16)
            out_ref[...] = jnp.zeros_like(out_ref)

        wanted = lax.broadcasted_iota(jnp.int32, (tokens, rows), 0) * window + step
        chosen = (lax.broadcasted_iota(jnp.int32, (tokens, rows), 1) == wanted).astype(jnp.bfloat16)
        part = jnp.dot(chosen, normed_ref[...], preferred_element_type=jnp.float32).astype(
            jnp.bfloat16
        )
        value = out_ref[...]
        for (first, size), ref in zip(chunks, weight_refs):
            value += jnp.dot(
                part[:, first : first + size], ref[0], preferred_element_type=jnp.float32
            )
        out_ref[...] = value

    def whole(shape):
        return pl.BlockSpec(shape, lambda i: (0, 0))

    def chunk(first, size):
        return pl.BlockSpec((1, size, features), lambda i: (i, first // size, 0))

    return pl.pallas_call(
        body,
        out_shape=jax.ShapeDtypeStruct((tokens, features), jnp.float32),
        grid=(window,),
        in_specs=[whole((rows, width)), whole((2, width))]
        + [whole((rows, 256))] * count
        + [chunk(first, size) for first, size in chunks],
        out_specs=whole((tokens, features)),
        scratch_shapes=[pltpu.VMEM((rows, width), jnp.bfloat16)],
        compiler_params=pltpu.CompilerParams(vmem_limit_bytes=56 << 20),
        cost_estimate=LIGHT,
    )(patches, gain_bias, *stats, *([merge_weight] * len(chunks)))


def combine(tp_index, order, texts, images, gain_column):
    n_tp = len(texts)
    width, positions = texts[0].shape
    slots = images[0].shape[0]
    count = order.shape[0]
    rows = width * n_tp // count
    share = width // rows

    def body(index_ref, order_ref, gain_ref, *refs):
        text_refs, image_refs = refs[:n_tp], refs[n_tp : 2 * n_tp]
        out_ref, value_ref = refs[2 * n_tp :]
        code = image_refs[0][:, width : width + 2].astype(jnp.float32)
        local = code[:, 0:1] * 256.0 + code[:, 1:2] - 1.0
        place = lax.broadcasted_iota(jnp.int32, (slots, positions), 1).astype(jnp.float32)
        hit = jnp.where(local == place, 1.0, 0.0)
        covered = jnp.max(hit, axis=0, keepdims=True)
        hit = hit.astype(jnp.bfloat16)
        squares = jnp.zeros((1, positions), jnp.float32)
        for distance in range(n_tp):
            first = lax.rem(index_ref[0] + n_tp - distance, n_tp) * share
            image = lax.dot_general(
                image_refs[distance][...],
                hit,
                (((0,), (0,)), ((), ())),
                preferred_element_type=jnp.float32,
            )[:width]
            value = jnp.where(covered > 0.0, image, text_refs[distance][...].astype(jnp.float32))
            squares += jnp.sum(value * value, axis=0, keepdims=True)
            for block in range(share):
                value_ref[first + block] = value[block * rows : (block + 1) * rows]
        scale = lax.rsqrt(squares / (width * n_tp) + EPSILON)
        for block in range(count):
            source = order_ref[block]
            gain = gain_ref[source].astype(jnp.float32)
            out_ref[block] = (value_ref[source] * scale * gain).astype(out_ref.dtype)

    vmem = pl.BlockSpec(memory_space=pltpu.VMEM)
    smem = pl.BlockSpec(memory_space=pltpu.SMEM)
    return pl.pallas_call(
        body,
        out_shape=jax.ShapeDtypeStruct((count, rows, positions), jnp.bfloat16),
        in_specs=[smem, smem] + [vmem] * (1 + 2 * n_tp),
        out_specs=vmem,
        scratch_shapes=[pltpu.VMEM((count, rows, positions), jnp.float32)],
        compiler_params=pltpu.CompilerParams(vmem_limit_bytes=VMEM),
        cost_estimate=LIGHT,
    )(tp_index, order, gain_column, *texts, *images)


def shards(
    n_req, n_tp,
    patches, ln_gain, ln_bias, merge_weight, text_rows, norm_gain, qkv_weight, token_pos, text_len,
):
    row_count, width = text_rows.shape
    me = lax.axis_index("req")
    tp_index = lax.axis_index("tp").reshape(1)
    lines, line_perm, table = ring_tables(n_req)
    x_perm = [(i, i ^ 1) for i in range(n_req)]
    y_perm = [(i, i ^ 2) for i in range(n_req)]
    rows, columns = qkv_weight.shape
    cut = (columns + 255) // 256 * 128
    order = lax.dynamic_slice_in_dim(jnp.asarray(table), me, 1, 0).reshape(-1)

    def along_line(block):
        return lax.ppermute(block, "req", line_perm)

    def to_sides(block):
        return lax.ppermute(block, "req", x_perm), lax.ppermute(block, "req", y_perm)

    def to_corner(by_x, by_y):
        left = lax.ppermute(by_y[:, :cut], "req", x_perm)
        right = lax.ppermute(by_x[:, cut:], "req", y_perm)
        return jnp.concatenate([left, right], axis=1)

    held = [qkv_weight]
    held.append(along_line(held[0]))
    sides = [to_sides(held[0])]
    corners = []
    stats_own = row_stats(patches)
    stats = [stats_own] + [tp_shift(stats_own, n_tp, d) for d in range(1, n_tp)]
    gain_bias = jnp.stack([ln_gain, ln_bias])
    text_turned = text_rows.T
    texts = [text_turned] + [tp_shift(text_turned, n_tp, d) for d in range(1, n_tp)]

    token_count = token_pos.shape[0]
    target = lax.div(token_pos, row_count)
    same = target[:, None] == target[None, :]
    ids = jnp.arange(token_count, dtype=jnp.int32)
    before = jnp.sum((same & (ids[None, :] < ids[:, None])).astype(jnp.int32), axis=1)
    slot = target * IMG_CAP + before
    slot_count = n_req * IMG_CAP
    code = lax.rem(token_pos, row_count) + 1
    code_cols = jnp.stack([lax.div(code, 256), lax.rem(code, 256)], axis=1).astype(jnp.bfloat16)
    gain_column = norm_gain.reshape(n_req, rows, 1)

    partial_value = merge(patches, stats, gain_bias, merge_weight)

    partial_value, held[1], sides[0], gain_column, order, slot, code_cols = tie(
        partial_value, held[1], sides[0], gain_column, order, slot, code_cols
    )
    held.append(along_line(held[1]))
    sides.append(to_sides(held[1]))
    corners.append(to_corner(*sides[0]))
    merged = tp_scatter_sum(partial_value, n_tp, 1).astype(jnp.bfloat16)
    padding = (-width - 2) % 128
    payload = jnp.concatenate(
        [merged, code_cols, jnp.zeros((token_count, padding), jnp.bfloat16)], axis=1
    )
    place = (
        jnp.arange(slot_count, dtype=jnp.int32)[:, None] == slot[None, :]
    ).astype(jnp.bfloat16)
    outgoing = jnp.dot(place, payload, preferred_element_type=jnp.float32).astype(jnp.bfloat16)
    arrived = lax.all_to_all(
        outgoing.reshape(n_req, IMG_CAP, -1), "req", split_axis=0, concat_axis=0
    ).reshape(slot_count, -1)

    held[2], sides[1] = tie(held[2], sides[1])
    held.append(along_line(held[2]))
    sides.append(to_sides(held[2]))
    images = [arrived] + [tp_shift(arrived, n_tp, d) for d in range(1, n_tp)]
    blocks = combine(tp_index, order, texts, images, gain_column)

    held[3], corners[0] = tie(held[3], corners[0])
    corners.append(along_line(corners[0]))
    held[3], sides[2] = tie(held[3], sides[2])
    sides.append(to_sides(held[3]))
    for step in range(4, lines):
        held.append(along_line(held[step - 1]))
        sides.append(to_sides(held[step]))
    for step in range(2, lines - 2):
        corners.append(along_line(corners[step - 1]))
    corners.append(to_corner(*sides[-2]))

    def add_product(total, first, weights):
        weight = jnp.concatenate(weights, axis=0)
        count = weight.shape[0]
        source = blocks[first : first + count // rows].reshape(count, row_count)
        if total is None:
            weight, source = tie(weight, source)
        else:
            weight, source, total = tie(weight, source, total)
        part = lax.dot_general(
            source, weight, (((0,), (0,)), ((), ())), preferred_element_type=jnp.float32
        )
        return part if total is None else total + part

    total = add_product(None, 0, [held[0], *sides[0], corners[0]])
    total = add_product(total, 4, [held[1], *sides[1]])

    total, sides[-1] = tie(total, sides[-1])
    corners.append(to_corner(*sides[-1]))
    for step in range(2, lines - 1):
        total = add_product(total, step * 3 + 1, [held[step], *sides[step]])
    total, late = tie(total, [held[-1], *sides[-1]])
    total = add_product(total, lines * 3 - 2, late)

    position = me * row_count + jnp.arange(row_count, dtype=jnp.int32)
    request_ids = jnp.arange(text_len.shape[0], dtype=jnp.int32)
    limits = jnp.sum(
        jnp.where(
            lax.div(position, SEQ)[:, None] == request_ids[None, :], text_len[None, :], 0
        ),
        axis=1,
    )
    keep = lax.rem(position, SEQ) < limits
    total = add_product(total, lines * 3 + 1, corners[1:])
    return jnp.where(keep[:, None], total, 0.0).astype(jnp.bfloat16)


def solution(mesh):
    placed = (
        P("req", "tp"),
        P("tp"),
        P("tp"),
        P(None, "tp", None),
        P("req", "tp"),
        P(),
        P("req", "tp"),
        P("req"),
        P(),
    )
    body = functools.partial(shards, mesh.shape["req"], mesh.shape["tp"])
    return jax.shard_map(
        body, mesh=mesh, in_specs=placed, out_specs=P("req", "tp"), check_vma=False
    )
```

```python
import functools

import jax
import jax.numpy as jnp
import numpy as np
from jax import lax
from jax.experimental import pallas as pl
from jax.experimental.pallas import tpu as pltpu
from jax.sharding import PartitionSpec as P

DV = 1664
SEQ = 4096
IMG_CAP = 16
EPSILON = 1e-06
VMEM = 32 << 20
LIGHT = pl.CostEstimate(flops=1000, bytes_accessed=1000, transcendentals=0)


def folded_ring(count):
    odd = list(range(1, count, 2))
    even = list(range(0, count, 2))
    return even[:1] + odd + even[:0:-1]


def tp_shift(value, n_tp, distance):
    return lax.ppermute(value, "tp", [(i, (i + distance) % n_tp) for i in range(n_tp)])


def tp_scatter_sum(value, n_tp, axis):
    me = lax.axis_index("tp")
    width = value.shape[axis] // n_tp
    total = lax.dynamic_slice_in_dim(value, me * width, width, axis)
    for distance in range(1, n_tp):
        block = lax.dynamic_slice_in_dim(value, (me + distance) % n_tp * width, width, axis)
        total = total + tp_shift(block, n_tp, distance)
    return total


def ring_tables(n_req):
    lines = n_req // 4
    order = folded_ring(lines)
    following = {order[i]: order[(i + 1) % lines] for i in range(lines)}
    line_perm = [(z * 4 + p, following[z] * 4 + p) for z in range(lines) for p in range(4)]
    arrivals = [(0, flip) for flip in range(4)]
    arrivals += [(step, flip) for step in range(1, lines) for flip in range(3)]
    arrivals += [(step, 3) for step in range(1, lines)]
    table = np.zeros((n_req, n_req), np.int32)
    for index in range(n_req):
        for place, (step, flip) in enumerate(arrivals):
            z = order[(order.index(index // 4) - step) % lines]
            table[index, place] = z * 4 + ((index % 4) ^ flip)
    return lines, line_perm, table


def tie(*values):
    return lax.optimization_barrier(values)


def pick_rows(patches, window):
    rows, width = patches.shape
    tokens = rows // window

    def body(patches_ref, picked_ref, stats_ref):
        taken = lax.broadcasted_iota(jnp.int32, (tokens, rows), 1)
        first = lax.broadcasted_iota(jnp.int32, (tokens, rows), 0) * window
        for slot in range(window):
            chosen = (taken == first + slot).astype(jnp.bfloat16)
            values = jnp.dot(chosen, patches_ref[...], preferred_element_type=jnp.float32)
            picked_ref[slot] = values.astype(jnp.bfloat16)
            sums = jnp.sum(values, axis=1, keepdims=True)
            squares = jnp.sum(values * values, axis=1, keepdims=True)
            stats_ref[slot, :, :128] = jnp.broadcast_to(sums, (tokens, 128))
            stats_ref[slot, :, 128:] = jnp.broadcast_to(squares, (tokens, 128))

    vmem = pl.BlockSpec(memory_space=pltpu.VMEM)
    return pl.pallas_call(
        body,
        out_shape=(
            jax.ShapeDtypeStruct((window, tokens, width), jnp.bfloat16),
            jax.ShapeDtypeStruct((window, tokens, 256), jnp.float32),
        ),
        in_specs=[vmem],
        out_specs=(vmem, vmem),
        compiler_params=pltpu.CompilerParams(vmem_limit_bytes=VMEM),
        cost_estimate=pl.CostEstimate(flops=1000, bytes_accessed=16 << 20, transcendentals=0),
    )(patches)


def merge(picked, stats, gain_bias, merge_weight):
    window, tokens, width = picked.shape
    features = merge_weight.shape[2]
    count = len(stats)

    def body(picked_ref, gain_bias_ref, *refs):
        stats_refs, (weight_ref, out_ref) = refs[:count], refs[count:]

        @pl.when(pl.program_id(0) == 0)
        def _():
            out_ref[...] = jnp.zeros_like(out_ref)

        sums = sum(ref[0] for ref in stats_refs) / DV
        row_mean = sums[:, 0:1]
        row_scale = lax.rsqrt(sums[:, 128:129] - row_mean * row_mean + EPSILON)
        gain_bias = gain_bias_ref[...].astype(jnp.float32)
        normed = (
            (picked_ref[0].astype(jnp.float32) - row_mean) * row_scale * gain_bias[0:1]
            + gain_bias[1:2]
        ).astype(jnp.bfloat16)
        out_ref[...] += jnp.dot(normed, weight_ref[0], preferred_element_type=jnp.float32)

    def by_slot(*shape):
        return pl.BlockSpec((1, *shape), lambda i: (i, 0, 0))

    def whole(shape):
        return pl.BlockSpec(shape, lambda i: (0, 0))

    return pl.pallas_call(
        body,
        out_shape=jax.ShapeDtypeStruct((tokens, features), jnp.float32),
        grid=(window,),
        in_specs=[by_slot(tokens, width), whole((2, width))]
        + [by_slot(tokens, 256)] * count
        + [by_slot(width, features)],
        out_specs=whole((tokens, features)),
        compiler_params=pltpu.CompilerParams(vmem_limit_bytes=VMEM),
        cost_estimate=LIGHT,
    )(picked, gain_bias, *stats, merge_weight)


def combine(tp_index, order, texts, images, gain_column):
    n_tp = len(texts)
    width, positions = texts[0].shape
    slots = images[0].shape[0]
    count = order.shape[0]
    rows = width * n_tp // count
    share = width // rows

    def body(index_ref, order_ref, gain_ref, *refs):
        text_refs, image_refs = refs[:n_tp], refs[n_tp : 2 * n_tp]
        out_ref, value_ref = refs[2 * n_tp :]
        code = image_refs[0][:, width : width + 2].astype(jnp.float32)
        local = code[:, 0:1] * 256.0 + code[:, 1:2] - 1.0
        place = lax.broadcasted_iota(jnp.int32, (slots, positions), 1).astype(jnp.float32)
        hit = jnp.where(local == place, 1.0, 0.0)
        covered = jnp.max(hit, axis=0, keepdims=True)
        hit = hit.astype(jnp.bfloat16)
        squares = jnp.zeros((1, positions), jnp.float32)
        for distance in range(n_tp):
            first = lax.rem(index_ref[0] + n_tp - distance, n_tp) * share
            image = lax.dot_general(
                image_refs[distance][...],
                hit,
                (((0,), (0,)), ((), ())),
                preferred_element_type=jnp.float32,
            )[:width]
            value = jnp.where(covered > 0.0, image, text_refs[distance][...].astype(jnp.float32))
            squares += jnp.sum(value * value, axis=0, keepdims=True)
            for block in range(share):
                value_ref[first + block] = value[block * rows : (block + 1) * rows]
        scale = lax.rsqrt(squares / (width * n_tp) + EPSILON)
        for block in range(count):
            source = order_ref[block]
            gain = gain_ref[source].astype(jnp.float32)
            out_ref[block] = (value_ref[source] * scale * gain).astype(out_ref.dtype)

    vmem = pl.BlockSpec(memory_space=pltpu.VMEM)
    smem = pl.BlockSpec(memory_space=pltpu.SMEM)
    return pl.pallas_call(
        body,
        out_shape=jax.ShapeDtypeStruct((count, rows, positions), jnp.bfloat16),
        in_specs=[smem, smem] + [vmem] * (1 + 2 * n_tp),
        out_specs=vmem,
        scratch_shapes=[pltpu.VMEM((count, rows, positions), jnp.float32)],
        compiler_params=pltpu.CompilerParams(vmem_limit_bytes=VMEM),
        cost_estimate=LIGHT,
    )(tp_index, order, gain_column, *texts, *images)


def shards(
    n_req, n_tp,
    patches, ln_gain, ln_bias, merge_weight, text_rows, norm_gain, qkv_weight, token_pos, text_len,
):
    row_count, width = text_rows.shape
    me = lax.axis_index("req")
    tp_index = lax.axis_index("tp").reshape(1)
    lines, line_perm, table = ring_tables(n_req)
    x_perm = [(i, i ^ 1) for i in range(n_req)]
    y_perm = [(i, i ^ 2) for i in range(n_req)]
    rows, columns = qkv_weight.shape
    cut = (columns + 255) // 256 * 128

    def along_line(block):
        return lax.ppermute(block, "req", line_perm)

    def to_sides(block):
        return lax.ppermute(block, "req", x_perm), lax.ppermute(block, "req", y_perm)

    def to_corner(by_x, by_y):
        left = lax.ppermute(by_y[:, :cut], "req", x_perm)
        right = lax.ppermute(by_x[:, cut:], "req", y_perm)
        return jnp.concatenate([left, right], axis=1)

    held = [qkv_weight]
    held.append(along_line(held[0]))
    sides = [to_sides(held[0])]
    corners = []
    picked, stats_own = pick_rows(patches, merge_weight.shape[0])
    stats = [stats_own] + [tp_shift(stats_own, n_tp, d) for d in range(1, n_tp)]
    gain_bias = jnp.stack([ln_gain, ln_bias])
    text_turned = text_rows.T
    texts = [text_turned] + [tp_shift(text_turned, n_tp, d) for d in range(1, n_tp)]

    token_count = token_pos.shape[0]
    target = lax.div(token_pos, row_count)
    same = target[:, None] == target[None, :]
    ids = jnp.arange(token_count, dtype=jnp.int32)
    before = jnp.sum((same & (ids[None, :] < ids[:, None])).astype(jnp.int32), axis=1)
    slot = target * IMG_CAP + before
    slot_count = n_req * IMG_CAP
    code = lax.rem(token_pos, row_count) + 1
    code_cols = jnp.stack([lax.div(code, 256), lax.rem(code, 256)], axis=1).astype(jnp.bfloat16)

    partial_value = merge(picked, stats, gain_bias, merge_weight)

    partial_value, held[1], sides[0], slot, code_cols = tie(
        partial_value, held[1], sides[0], slot, code_cols
    )
    held.append(along_line(held[1]))
    sides.append(to_sides(held[1]))
    corners.append(to_corner(*sides[0]))
    merged = tp_scatter_sum(partial_value, n_tp, 1).astype(jnp.bfloat16)
    padding = (-width - 2) % 128
    payload = jnp.concatenate(
        [merged, code_cols, jnp.zeros((token_count, padding), jnp.bfloat16)], axis=1
    )
    place = (
        jnp.arange(slot_count, dtype=jnp.int32)[:, None] == slot[None, :]
    ).astype(jnp.bfloat16)
    outgoing = jnp.dot(place, payload, preferred_element_type=jnp.float32).astype(jnp.bfloat16)
    arrived = lax.all_to_all(
        outgoing.reshape(n_req, IMG_CAP, -1), "req", split_axis=0, concat_axis=0
    ).reshape(slot_count, -1)

    held[2], sides[1], norm_gain, me = tie(held[2], sides[1], norm_gain, me)
    gain_column = norm_gain.reshape(n_req, rows, 1)
    order = lax.dynamic_slice_in_dim(jnp.asarray(table), me, 1, 0).reshape(-1)
    held.append(along_line(held[2]))
    sides.append(to_sides(held[2]))
    images = [arrived] + [tp_shift(arrived, n_tp, d) for d in range(1, n_tp)]
    blocks = combine(tp_index, order, texts, images, gain_column)

    held[3], corners[0] = tie(held[3], corners[0])
    corners.append(along_line(corners[0]))
    held[3], sides[2] = tie(held[3], sides[2])
    sides.append(to_sides(held[3]))
    for step in range(4, lines):
        held.append(along_line(held[step - 1]))
        sides.append(to_sides(held[step]))
    for step in range(2, lines - 2):
        corners.append(along_line(corners[step - 1]))
    corners.append(to_corner(*sides[-2]))

    def add_product(total, first, weights):
        weight = jnp.concatenate(weights, axis=0)
        count = weight.shape[0]
        source = blocks[first : first + count // rows].reshape(count, row_count)
        if total is None:
            weight, source = tie(weight, source)
        else:
            weight, source, total = tie(weight, source, total)
        part = lax.dot_general(
            source, weight, (((0,), (0,)), ((), ())), preferred_element_type=jnp.float32
        )
        return part if total is None else total + part

    total = add_product(None, 0, [held[0], *sides[0], corners[0]])
    total = add_product(total, 4, [held[1], *sides[1]])

    total, sides[-1] = tie(total, sides[-1])
    corners.append(to_corner(*sides[-1]))
    for step in range(2, lines - 1):
        total = add_product(total, step * 3 + 1, [held[step], *sides[step]])
    total, late = tie(total, [held[-1], *sides[-1]])
    total = add_product(total, lines * 3 - 2, late)

    position = me * row_count + jnp.arange(row_count, dtype=jnp.int32)
    request_ids = jnp.arange(text_len.shape[0], dtype=jnp.int32)
    limits = jnp.sum(
        jnp.where(
            lax.div(position, SEQ)[:, None] == request_ids[None, :], text_len[None, :], 0
        ),
        axis=1,
    )
    keep = lax.rem(position, SEQ) < limits
    total = add_product(total, lines * 3 + 1, corners[1:])
    return jnp.where(keep[:, None], total, 0.0).astype(jnp.bfloat16)


def solution(mesh):
    placed = (
        P("req", "tp"),
        P("tp"),
        P("tp"),
        P(None, "tp", None),
        P("req", "tp"),
        P(),
        P("req", "tp"),
        P("req"),
        P(),
    )
    body = functools.partial(shards, mesh.shape["req"], mesh.shape["tp"])
    return jax.shard_map(
        body, mesh=mesh, in_specs=placed, out_specs=P("req", "tp"), check_vma=False
    )
```

```python
import functools

import jax
import jax.numpy as jnp
import numpy as np
from jax import lax
from jax.experimental import pallas as pl
from jax.experimental.pallas import tpu as pltpu
from jax.sharding import PartitionSpec as P

DV = 1664
SEQ = 4096
IMG_CAP = 16
EPSILON = 1e-06
VMEM = 32 << 20
LIGHT = pl.CostEstimate(flops=1000, bytes_accessed=1000, transcendentals=0)


def folded_ring(count):
    odd = list(range(1, count, 2))
    even = list(range(0, count, 2))
    return even[:1] + odd + even[:0:-1]


def tp_shift(value, n_tp, distance):
    return lax.ppermute(value, "tp", [(i, (i + distance) % n_tp) for i in range(n_tp)])


def tp_scatter_sum(value, n_tp, axis):
    me = lax.axis_index("tp")
    width = value.shape[axis] // n_tp
    total = lax.dynamic_slice_in_dim(value, me * width, width, axis)
    for distance in range(1, n_tp):
        block = lax.dynamic_slice_in_dim(value, (me + distance) % n_tp * width, width, axis)
        total = total + tp_shift(block, n_tp, distance)
    return total


def ring_tables(n_req):
    lines = n_req // 4
    order = folded_ring(lines)
    following = {order[i]: order[(i + 1) % lines] for i in range(lines)}
    line_perm = [(z * 4 + p, following[z] * 4 + p) for z in range(lines) for p in range(4)]
    arrivals = [(0, flip) for flip in range(4)]
    arrivals += [(step, flip) for step in range(1, lines) for flip in range(3)]
    arrivals += [(step, 3) for step in range(1, lines)]
    table = np.zeros((n_req, n_req), np.int32)
    for index in range(n_req):
        for place, (step, flip) in enumerate(arrivals):
            z = order[(order.index(index // 4) - step) % lines]
            table[index, place] = z * 4 + ((index % 4) ^ flip)
    return lines, line_perm, table


def tie(*values):
    return lax.optimization_barrier(values)


def pick_rows(patches, window):
    rows, width = patches.shape
    tokens = rows // window

    def body(patches_ref, picked_ref, stats_ref):
        taken = lax.broadcasted_iota(jnp.int32, (tokens, rows), 1)
        first = lax.broadcasted_iota(jnp.int32, (tokens, rows), 0) * window
        for slot in range(window):
            chosen = (taken == first + slot).astype(jnp.bfloat16)
            values = jnp.dot(chosen, patches_ref[...], preferred_element_type=jnp.float32)
            picked_ref[slot] = values.astype(jnp.bfloat16)
            sums = jnp.sum(values, axis=1, keepdims=True)
            squares = jnp.sum(values * values, axis=1, keepdims=True)
            stats_ref[slot, :, :128] = jnp.broadcast_to(sums, (tokens, 128))
            stats_ref[slot, :, 128:] = jnp.broadcast_to(squares, (tokens, 128))

    vmem = pl.BlockSpec(memory_space=pltpu.VMEM)
    return pl.pallas_call(
        body,
        out_shape=(
            jax.ShapeDtypeStruct((window, tokens, width), jnp.bfloat16),
            jax.ShapeDtypeStruct((window, tokens, 256), jnp.float32),
        ),
        in_specs=[vmem],
        out_specs=(vmem, vmem),
        compiler_params=pltpu.CompilerParams(vmem_limit_bytes=VMEM),
        cost_estimate=pl.CostEstimate(flops=1000, bytes_accessed=16 << 20, transcendentals=0),
    )(patches)


def merge(picked, stats, gain_bias, merge_weight):
    window, tokens, width = picked.shape
    features = merge_weight.shape[2]
    count = len(stats)

    def body(picked_ref, gain_bias_ref, *refs):
        stats_refs, (weight_ref, out_ref) = refs[:count], refs[count:]

        @pl.when(pl.program_id(0) == 0)
        def _():
            out_ref[...] = jnp.zeros_like(out_ref)

        sums = sum(ref[0] for ref in stats_refs) / DV
        row_mean = sums[:, 0:1]
        row_scale = lax.rsqrt(sums[:, 128:129] - row_mean * row_mean + EPSILON)
        gain_bias = gain_bias_ref[...].astype(jnp.float32)
        normed = (
            (picked_ref[0].astype(jnp.float32) - row_mean) * row_scale * gain_bias[0:1]
            + gain_bias[1:2]
        ).astype(jnp.bfloat16)
        out_ref[...] += jnp.dot(normed, weight_ref[0], preferred_element_type=jnp.float32)

    def by_slot(*shape):
        return pl.BlockSpec((1, *shape), lambda i: (i, 0, 0))

    def whole(shape):
        return pl.BlockSpec(shape, lambda i: (0, 0))

    return pl.pallas_call(
        body,
        out_shape=jax.ShapeDtypeStruct((tokens, features), jnp.float32),
        grid=(window,),
        in_specs=[by_slot(tokens, width), whole((2, width))]
        + [by_slot(tokens, 256)] * count
        + [by_slot(width, features)],
        out_specs=whole((tokens, features)),
        compiler_params=pltpu.CompilerParams(vmem_limit_bytes=VMEM),
        cost_estimate=LIGHT,
    )(picked, gain_bias, *stats, merge_weight)


def combine(tp_index, order, texts, images, gain_column):
    n_tp = len(texts)
    width, positions = texts[0].shape
    slots = images[0].shape[0]
    count = order.shape[0]
    rows = width * n_tp // count
    share = width // rows

    def body(index_ref, order_ref, gain_ref, *refs):
        text_refs, image_refs = refs[:n_tp], refs[n_tp : 2 * n_tp]
        out_ref, value_ref = refs[2 * n_tp :]
        code = image_refs[0][:, width : width + 2].astype(jnp.float32)
        local = code[:, 0:1] * 256.0 + code[:, 1:2] - 1.0
        place = lax.broadcasted_iota(jnp.int32, (slots, positions), 1).astype(jnp.float32)
        hit = jnp.where(local == place, 1.0, 0.0)
        covered = jnp.max(hit, axis=0, keepdims=True)
        hit = hit.astype(jnp.bfloat16)
        squares = jnp.zeros((1, positions), jnp.float32)
        for distance in range(n_tp):
            first = lax.rem(index_ref[0] + n_tp - distance, n_tp) * share
            image = lax.dot_general(
                image_refs[distance][...],
                hit,
                (((0,), (0,)), ((), ())),
                preferred_element_type=jnp.float32,
            )[:width]
            value = jnp.where(covered > 0.0, image, text_refs[distance][...].astype(jnp.float32))
            squares += jnp.sum(value * value, axis=0, keepdims=True)
            for block in range(share):
                value_ref[first + block] = value[block * rows : (block + 1) * rows]
        scale = lax.rsqrt(squares / (width * n_tp) + EPSILON)
        for block in range(count):
            source = order_ref[block]
            gain = gain_ref[source].astype(jnp.float32)
            out_ref[block] = (value_ref[source] * scale * gain).astype(out_ref.dtype)

    vmem = pl.BlockSpec(memory_space=pltpu.VMEM)
    smem = pl.BlockSpec(memory_space=pltpu.SMEM)
    return pl.pallas_call(
        body,
        out_shape=jax.ShapeDtypeStruct((count, rows, positions), jnp.bfloat16),
        in_specs=[smem, smem] + [vmem] * (1 + 2 * n_tp),
        out_specs=vmem,
        scratch_shapes=[pltpu.VMEM((count, rows, positions), jnp.float32)],
        compiler_params=pltpu.CompilerParams(vmem_limit_bytes=VMEM),
        cost_estimate=LIGHT,
    )(tp_index, order, gain_column, *texts, *images)


def shards(
    n_req, n_tp,
    patches, ln_gain, ln_bias, merge_weight, text_rows, norm_gain, qkv_weight, token_pos, text_len,
):
    row_count, width = text_rows.shape
    me = lax.axis_index("req")
    tp_index = lax.axis_index("tp").reshape(1)
    lines, line_perm, table = ring_tables(n_req)
    x_perm = [(i, i ^ 1) for i in range(n_req)]
    y_perm = [(i, i ^ 2) for i in range(n_req)]
    rows, columns = qkv_weight.shape
    cut = (columns + 255) // 256 * 128

    def along_line(block):
        return lax.ppermute(block, "req", line_perm)

    def to_sides(block):
        return lax.ppermute(block, "req", x_perm), lax.ppermute(block, "req", y_perm)

    def to_corner(by_x, by_y):
        left = lax.ppermute(by_y[:, :cut], "req", x_perm)
        right = lax.ppermute(by_x[:, cut:], "req", y_perm)
        return left, right

    held = [qkv_weight]
    held.append(along_line(held[0]))
    sides = [to_sides(held[0])]
    picked, stats_own = pick_rows(patches, merge_weight.shape[0])
    stats = [stats_own] + [tp_shift(stats_own, n_tp, d) for d in range(1, n_tp)]
    gain_bias = jnp.stack([ln_gain, ln_bias])
    text_turned = text_rows.T
    texts = [text_turned] + [tp_shift(text_turned, n_tp, d) for d in range(1, n_tp)]

    token_count = token_pos.shape[0]
    target = lax.div(token_pos, row_count)
    same = target[:, None] == target[None, :]
    ids = jnp.arange(token_count, dtype=jnp.int32)
    before = jnp.sum((same & (ids[None, :] < ids[:, None])).astype(jnp.int32), axis=1)
    slot = target * IMG_CAP + before
    slot_count = n_req * IMG_CAP
    code = lax.rem(token_pos, row_count) + 1
    code_cols = jnp.stack([lax.div(code, 256), lax.rem(code, 256)], axis=1).astype(jnp.bfloat16)

    partial_value = merge(picked, stats, gain_bias, merge_weight)

    partial_value, held[1], sides[0], slot, code_cols = tie(
        partial_value, held[1], sides[0], slot, code_cols
    )
    held.append(along_line(held[1]))
    sides.append(to_sides(held[1]))
    merged = tp_scatter_sum(partial_value, n_tp, 1).astype(jnp.bfloat16)
    merged, sides[0] = tie(merged, sides[0])
    halves = to_corner(*sides[0])
    padding = (-width - 2) % 128
    payload = jnp.concatenate(
        [merged, code_cols, jnp.zeros((token_count, padding), jnp.bfloat16)], axis=1
    )
    place = (
        jnp.arange(slot_count, dtype=jnp.int32)[:, None] == slot[None, :]
    ).astype(jnp.bfloat16)
    outgoing = jnp.dot(place, payload, preferred_element_type=jnp.float32).astype(jnp.bfloat16)
    arrived = lax.all_to_all(
        outgoing.reshape(n_req, IMG_CAP, -1), "req", split_axis=0, concat_axis=0
    ).reshape(slot_count, -1)

    held[2], sides[1], norm_gain, me = tie(held[2], sides[1], norm_gain, me)
    gain_column = norm_gain.reshape(n_req, rows, 1)
    order = lax.dynamic_slice_in_dim(jnp.asarray(table), me, 1, 0).reshape(-1)
    held.append(along_line(held[2]))
    sides.append(to_sides(held[2]))
    images = [arrived] + [tp_shift(arrived, n_tp, d) for d in range(1, n_tp)]
    blocks = combine(tp_index, order, texts, images, gain_column)

    held[3], sides[2], halves = tie(held[3], sides[2], halves)
    sides.append(to_sides(held[3]))
    corners = [jnp.concatenate(halves, axis=1)]
    corners.append(along_line(corners[0]))
    for step in range(4, lines):
        held.append(along_line(held[step - 1]))
        sides.append(to_sides(held[step]))
    for step in range(2, lines - 2):
        corners.append(along_line(corners[step - 1]))
    corners.append(jnp.concatenate(to_corner(*sides[-2]), axis=1))

    def add_product(total, first, weights):
        weight = jnp.concatenate(weights, axis=0)
        count = weight.shape[0]
        source = blocks[first : first + count // rows].reshape(count, row_count)
        if total is None:
            weight, source = tie(weight, source)
        else:
            weight, source, total = tie(weight, source, total)
        part = lax.dot_general(
            source, weight, (((0,), (0,)), ((), ())), preferred_element_type=jnp.float32
        )
        return part if total is None else total + part

    total = add_product(None, 0, [held[0], *sides[0], corners[0]])
    total = add_product(total, 4, [held[1], *sides[1]])

    total, sides[-1] = tie(total, sides[-1])
    corners.append(jnp.concatenate(to_corner(*sides[-1]), axis=1))
    for step in range(2, lines - 1):
        total = add_product(total, step * 3 + 1, [held[step], *sides[step]])
    total, late = tie(total, [held[-1], *sides[-1]])
    total = add_product(total, lines * 3 - 2, late)

    position = me * row_count + jnp.arange(row_count, dtype=jnp.int32)
    request_ids = jnp.arange(text_len.shape[0], dtype=jnp.int32)
    limits = jnp.sum(
        jnp.where(
            lax.div(position, SEQ)[:, None] == request_ids[None, :], text_len[None, :], 0
        ),
        axis=1,
    )
    keep = lax.rem(position, SEQ) < limits
    total = add_product(total, lines * 3 + 1, corners[1:])
    return jnp.where(keep[:, None], total, 0.0).astype(jnp.bfloat16)


def solution(mesh):
    placed = (
        P("req", "tp"),
        P("tp"),
        P("tp"),
        P(None, "tp", None),
        P("req", "tp"),
        P(),
        P("req", "tp"),
        P("req"),
        P(),
    )
    body = functools.partial(shards, mesh.shape["req"], mesh.shape["tp"])
    return jax.shard_map(
        body, mesh=mesh, in_specs=placed, out_specs=P("req", "tp"), check_vma=False
    )
```

```python
import functools

import jax
import jax.numpy as jnp
import numpy as np
from jax import lax
from jax.experimental import pallas as pl
from jax.experimental.pallas import tpu as pltpu
from jax.sharding import PartitionSpec as P

DV = 1664
SEQ = 4096
IMG_CAP = 16
EPSILON = 1e-06
VMEM = 32 << 20
LIGHT = pl.CostEstimate(flops=1000, bytes_accessed=1000, transcendentals=0)


def folded_ring(count):
    odd = list(range(1, count, 2))
    even = list(range(0, count, 2))
    return even[:1] + odd + even[:0:-1]


def tp_shift(value, n_tp, distance):
    return lax.ppermute(value, "tp", [(i, (i + distance) % n_tp) for i in range(n_tp)])


def tp_scatter_sum(value, n_tp, axis):
    me = lax.axis_index("tp")
    width = value.shape[axis] // n_tp
    total = lax.dynamic_slice_in_dim(value, me * width, width, axis)
    for distance in range(1, n_tp):
        block = lax.dynamic_slice_in_dim(value, (me + distance) % n_tp * width, width, axis)
        total = total + tp_shift(block, n_tp, distance)
    return total


def ring_tables(n_req):
    lines = n_req // 4
    order = folded_ring(lines)
    following = {order[i]: order[(i + 1) % lines] for i in range(lines)}
    line_perm = [(z * 4 + p, following[z] * 4 + p) for z in range(lines) for p in range(4)]
    arrivals = [(0, flip) for flip in range(4)]
    arrivals += [(step, flip) for step in range(1, lines) for flip in range(3)]
    arrivals += [(step, 3) for step in range(1, lines)]
    table = np.zeros((n_req, n_req), np.int32)
    for index in range(n_req):
        for place, (step, flip) in enumerate(arrivals):
            z = order[(order.index(index // 4) - step) % lines]
            table[index, place] = z * 4 + ((index % 4) ^ flip)
    return lines, line_perm, table


def tie(*values):
    return lax.optimization_barrier(values)


def pick_rows(patches, window):
    rows, width = patches.shape
    tokens = rows // window

    def body(patches_ref, picked_ref, stats_ref):
        taken = lax.broadcasted_iota(jnp.int32, (tokens, rows), 1)
        first = lax.broadcasted_iota(jnp.int32, (tokens, rows), 0) * window
        for slot in range(window):
            chosen = (taken == first + slot).astype(jnp.bfloat16)
            values = jnp.dot(chosen, patches_ref[...], preferred_element_type=jnp.float32)
            picked_ref[slot] = values.astype(jnp.bfloat16)
            sums = jnp.sum(values, axis=1, keepdims=True)
            squares = jnp.sum(values * values, axis=1, keepdims=True)
            stats_ref[slot, :, :128] = jnp.broadcast_to(sums, (tokens, 128))
            stats_ref[slot, :, 128:] = jnp.broadcast_to(squares, (tokens, 128))

    vmem = pl.BlockSpec(memory_space=pltpu.VMEM)
    return pl.pallas_call(
        body,
        out_shape=(
            jax.ShapeDtypeStruct((window, tokens, width), jnp.bfloat16),
            jax.ShapeDtypeStruct((window, tokens, 256), jnp.float32),
        ),
        in_specs=[vmem],
        out_specs=(vmem, vmem),
        compiler_params=pltpu.CompilerParams(vmem_limit_bytes=VMEM),
        cost_estimate=pl.CostEstimate(flops=1000, bytes_accessed=16 << 20, transcendentals=0),
    )(patches)


def merge(picked, stats, gain_bias, merge_weight):
    window, tokens, width = picked.shape
    features = merge_weight.shape[2]
    count = len(stats)

    def body(picked_ref, gain_bias_ref, *refs):
        stats_refs, (weight_ref, out_ref) = refs[:count], refs[count:]

        @pl.when(pl.program_id(0) == 0)
        def _():
            out_ref[...] = jnp.zeros_like(out_ref)

        sums = sum(ref[0] for ref in stats_refs) / DV
        row_mean = sums[:, 0:1]
        row_scale = lax.rsqrt(sums[:, 128:129] - row_mean * row_mean + EPSILON)
        gain_bias = gain_bias_ref[...].astype(jnp.float32)
        normed = (
            (picked_ref[0].astype(jnp.float32) - row_mean) * row_scale * gain_bias[0:1]
            + gain_bias[1:2]
        ).astype(jnp.bfloat16)
        out_ref[...] += jnp.dot(normed, weight_ref[0], preferred_element_type=jnp.float32)

    def by_slot(*shape):
        return pl.BlockSpec((1, *shape), lambda i: (i, 0, 0))

    def whole(shape):
        return pl.BlockSpec(shape, lambda i: (0, 0))

    return pl.pallas_call(
        body,
        out_shape=jax.ShapeDtypeStruct((tokens, features), jnp.float32),
        grid=(window,),
        in_specs=[by_slot(tokens, width), whole((2, width))]
        + [by_slot(tokens, 256)] * count
        + [by_slot(width, features)],
        out_specs=whole((tokens, features)),
        compiler_params=pltpu.CompilerParams(vmem_limit_bytes=VMEM),
        cost_estimate=LIGHT,
    )(picked, gain_bias, *stats, merge_weight)


def combine(tp_index, order, texts, images, gain_column):
    n_tp = len(texts)
    width, positions = texts[0].shape
    slots = images[0].shape[0]
    count = order.shape[0]
    rows = width * n_tp // count
    share = width // rows

    def body(index_ref, order_ref, gain_ref, *refs):
        text_refs, image_refs = refs[:n_tp], refs[n_tp : 2 * n_tp]
        out_ref, value_ref = refs[2 * n_tp :]
        code = image_refs[0][:, width : width + 2].astype(jnp.float32)
        local = code[:, 0:1] * 256.0 + code[:, 1:2] - 1.0
        place = lax.broadcasted_iota(jnp.int32, (slots, positions), 1).astype(jnp.float32)
        hit = jnp.where(local == place, 1.0, 0.0)
        covered = jnp.max(hit, axis=0, keepdims=True)
        hit = hit.astype(jnp.bfloat16)
        squares = jnp.zeros((1, positions), jnp.float32)
        for distance in range(n_tp):
            first = lax.rem(index_ref[0] + n_tp - distance, n_tp) * share
            image = lax.dot_general(
                image_refs[distance][...],
                hit,
                (((0,), (0,)), ((), ())),
                preferred_element_type=jnp.float32,
            )[:width]
            value = jnp.where(covered > 0.0, image, text_refs[distance][...].astype(jnp.float32))
            squares += jnp.sum(value * value, axis=0, keepdims=True)
            for block in range(share):
                value_ref[first + block] = value[block * rows : (block + 1) * rows]
        scale = lax.rsqrt(squares / (width * n_tp) + EPSILON)
        for block in range(count):
            source = order_ref[block]
            gain = gain_ref[source].astype(jnp.float32)
            out_ref[block] = (value_ref[source] * scale * gain).astype(out_ref.dtype)

    vmem = pl.BlockSpec(memory_space=pltpu.VMEM)
    smem = pl.BlockSpec(memory_space=pltpu.SMEM)
    return pl.pallas_call(
        body,
        out_shape=jax.ShapeDtypeStruct((count, rows, positions), jnp.bfloat16),
        in_specs=[smem, smem] + [vmem] * (1 + 2 * n_tp),
        out_specs=vmem,
        scratch_shapes=[pltpu.VMEM((count, rows, positions), jnp.float32)],
        compiler_params=pltpu.CompilerParams(vmem_limit_bytes=VMEM),
        cost_estimate=LIGHT,
    )(tp_index, order, gain_column, *texts, *images)


def shards(
    n_req, n_tp,
    patches, ln_gain, ln_bias, merge_weight, text_rows, norm_gain, qkv_weight, token_pos, text_len,
):
    row_count, width = text_rows.shape
    me = lax.axis_index("req")
    tp_index = lax.axis_index("tp").reshape(1)
    lines, line_perm, table = ring_tables(n_req)
    x_perm = [(i, i ^ 1) for i in range(n_req)]
    y_perm = [(i, i ^ 2) for i in range(n_req)]
    rows, columns = qkv_weight.shape
    cut = (columns + 255) // 256 * 128

    def along_line(block):
        return lax.ppermute(block, "req", line_perm)

    def to_sides(block):
        return lax.ppermute(block, "req", x_perm), lax.ppermute(block, "req", y_perm)

    def to_corner(by_x, by_y):
        left = lax.ppermute(by_y[:, :cut], "req", x_perm)
        right = lax.ppermute(by_x[:, cut:], "req", y_perm)
        return left, right

    held = [qkv_weight]
    held.append(along_line(held[0]))
    sides = [to_sides(held[0])]
    picked, stats_own = pick_rows(patches, merge_weight.shape[0])
    stats = [stats_own] + [tp_shift(stats_own, n_tp, d) for d in range(1, n_tp)]
    gain_bias = jnp.stack([ln_gain, ln_bias])
    text_turned = text_rows.T
    texts = [text_turned] + [tp_shift(text_turned, n_tp, d) for d in range(1, n_tp)]

    token_count = token_pos.shape[0]
    target = lax.div(token_pos, row_count)
    same = target[:, None] == target[None, :]
    ids = jnp.arange(token_count, dtype=jnp.int32)
    before = jnp.sum((same & (ids[None, :] < ids[:, None])).astype(jnp.int32), axis=1)
    slot = target * IMG_CAP + before
    slot_count = n_req * IMG_CAP
    code = lax.rem(token_pos, row_count) + 1
    code_cols = jnp.stack([lax.div(code, 256), lax.rem(code, 256)], axis=1).astype(jnp.bfloat16)

    partial_value = merge(picked, stats, gain_bias, merge_weight)

    partial_value, held[1], sides[0], slot, code_cols = tie(
        partial_value, held[1], sides[0], slot, code_cols
    )
    held.append(along_line(held[1]))
    sides.append(to_sides(held[1]))
    merged = tp_scatter_sum(partial_value, n_tp, 1).astype(jnp.bfloat16)
    merged, sides[0] = tie(merged, sides[0])
    halves = to_corner(*sides[0])
    padding = (-width - 2) % 128
    payload = jnp.concatenate(
        [merged, code_cols, jnp.zeros((token_count, padding), jnp.bfloat16)], axis=1
    )
    place = (
        jnp.arange(slot_count, dtype=jnp.int32)[:, None] == slot[None, :]
    ).astype(jnp.bfloat16)
    outgoing = jnp.dot(place, payload, preferred_element_type=jnp.float32).astype(jnp.bfloat16)
    arrived = lax.all_to_all(
        outgoing.reshape(n_req, IMG_CAP, -1), "req", split_axis=0, concat_axis=0
    ).reshape(slot_count, -1)

    held[2], sides[1], norm_gain, me = tie(held[2], sides[1], norm_gain, me)
    gain_column = norm_gain.reshape(n_req, rows, 1)
    order = lax.dynamic_slice_in_dim(jnp.asarray(table), me, 1, 0).reshape(-1)
    held.append(along_line(held[2]))
    sides.append(to_sides(held[2]))
    images = [arrived] + [tp_shift(arrived, n_tp, d) for d in range(1, n_tp)]
    blocks = combine(tp_index, order, texts, images, gain_column)

    corners = [jnp.concatenate(halves, axis=1)]
    first = jnp.concatenate([held[0], *sides[0], corners[0]], axis=0)
    second = jnp.concatenate([held[1], *sides[1]], axis=0)
    held[3], sides[2], corners[0], first, second = tie(
        held[3], sides[2], corners[0], first, second
    )
    sides.append(to_sides(held[3]))
    corners.append(along_line(corners[0]))
    for step in range(4, lines):
        held.append(along_line(held[step - 1]))
        sides.append(to_sides(held[step]))
    for step in range(2, lines - 2):
        corners.append(along_line(corners[step - 1]))
    corners.append(jnp.concatenate(to_corner(*sides[-2]), axis=1))

    def add_product(total, first, weights):
        weight = jnp.concatenate(weights, axis=0)
        count = weight.shape[0]
        source = blocks[first : first + count // rows].reshape(count, row_count)
        if total is None:
            weight, source = tie(weight, source)
        else:
            weight, source, total = tie(weight, source, total)
        part = lax.dot_general(
            source, weight, (((0,), (0,)), ((), ())), preferred_element_type=jnp.float32
        )
        return part if total is None else total + part

    total = add_product(None, 0, [first])
    total = add_product(total, 4, [second])

    total, sides[-1] = tie(total, sides[-1])
    corners.append(jnp.concatenate(to_corner(*sides[-1]), axis=1))
    for step in range(2, lines - 1):
        total = add_product(total, step * 3 + 1, [held[step], *sides[step]])
    total, late = tie(total, [held[-1], *sides[-1]])
    total = add_product(total, lines * 3 - 2, late)

    position = me * row_count + jnp.arange(row_count, dtype=jnp.int32)
    request_ids = jnp.arange(text_len.shape[0], dtype=jnp.int32)
    limits = jnp.sum(
        jnp.where(
            lax.div(position, SEQ)[:, None] == request_ids[None, :], text_len[None, :], 0
        ),
        axis=1,
    )
    keep = lax.rem(position, SEQ) < limits
    total = add_product(total, lines * 3 + 1, corners[1:])
    return jnp.where(keep[:, None], total, 0.0).astype(jnp.bfloat16)


def solution(mesh):
    placed = (
        P("req", "tp"),
        P("tp"),
        P("tp"),
        P(None, "tp", None),
        P("req", "tp"),
        P(),
        P("req", "tp"),
        P("req"),
        P(),
    )
    body = functools.partial(shards, mesh.shape["req"], mesh.shape["tp"])
    return jax.shard_map(
        body, mesh=mesh, in_specs=placed, out_specs=P("req", "tp"), check_vma=False
    )
```

```python
import functools

import jax
import jax.numpy as jnp
import numpy as np
from jax import lax
from jax.experimental import pallas as pl
from jax.experimental.pallas import tpu as pltpu
from jax.sharding import PartitionSpec as P

DV = 1664
SEQ = 4096
IMG_CAP = 16
EPSILON = 1e-06
VMEM = 32 << 20
LIGHT = pl.CostEstimate(flops=1000, bytes_accessed=1000, transcendentals=0)


def folded_ring(count):
    odd = list(range(1, count, 2))
    even = list(range(0, count, 2))
    return even[:1] + odd + even[:0:-1]


def tp_shift(value, n_tp, distance):
    return lax.ppermute(value, "tp", [(i, (i + distance) % n_tp) for i in range(n_tp)])


def tp_scatter_sum(value, n_tp, axis):
    me = lax.axis_index("tp")
    width = value.shape[axis] // n_tp
    total = lax.dynamic_slice_in_dim(value, me * width, width, axis)
    for distance in range(1, n_tp):
        block = lax.dynamic_slice_in_dim(value, (me + distance) % n_tp * width, width, axis)
        total = total + tp_shift(block, n_tp, distance)
    return total


def ring_tables(n_req):
    lines = n_req // 4
    order = folded_ring(lines)
    following = {order[i]: order[(i + 1) % lines] for i in range(lines)}
    line_perm = [(z * 4 + p, following[z] * 4 + p) for z in range(lines) for p in range(4)]
    arrivals = [(0, flip) for flip in range(4)]
    arrivals += [(step, flip) for step in range(1, lines) for flip in range(3)]
    arrivals += [(step, 3) for step in range(1, lines)]
    table = np.zeros((n_req, n_req), np.int32)
    for index in range(n_req):
        for place, (step, flip) in enumerate(arrivals):
            z = order[(order.index(index // 4) - step) % lines]
            table[index, place] = z * 4 + ((index % 4) ^ flip)
    return lines, line_perm, table


def tie(*values):
    return lax.optimization_barrier(values)


def pick_rows(patches, window):
    rows, width = patches.shape
    tokens = rows // window

    def body(patches_ref, picked_ref, stats_ref):
        taken = lax.broadcasted_iota(jnp.int32, (tokens, rows), 1)
        first = lax.broadcasted_iota(jnp.int32, (tokens, rows), 0) * window
        for slot in range(window):
            chosen = (taken == first + slot).astype(jnp.bfloat16)
            values = jnp.dot(chosen, patches_ref[...], preferred_element_type=jnp.float32)
            picked_ref[slot] = values.astype(jnp.bfloat16)
            sums = jnp.sum(values, axis=1, keepdims=True)
            squares = jnp.sum(values * values, axis=1, keepdims=True)
            stats_ref[slot, :, :128] = jnp.broadcast_to(sums, (tokens, 128))
            stats_ref[slot, :, 128:] = jnp.broadcast_to(squares, (tokens, 128))

    vmem = pl.BlockSpec(memory_space=pltpu.VMEM)
    return pl.pallas_call(
        body,
        out_shape=(
            jax.ShapeDtypeStruct((window, tokens, width), jnp.bfloat16),
            jax.ShapeDtypeStruct((window, tokens, 256), jnp.float32),
        ),
        in_specs=[vmem],
        out_specs=(vmem, vmem),
        compiler_params=pltpu.CompilerParams(vmem_limit_bytes=VMEM),
        cost_estimate=pl.CostEstimate(flops=1000, bytes_accessed=16 << 20, transcendentals=0),
    )(patches)


def merge(picked, stats, gain_bias, merge_weight):
    window, tokens, width = picked.shape
    features = merge_weight.shape[2]
    count = len(stats)

    def body(picked_ref, gain_bias_ref, *refs):
        stats_refs, (weight_ref, out_ref) = refs[:count], refs[count:]

        @pl.when(pl.program_id(0) == 0)
        def _():
            out_ref[...] = jnp.zeros_like(out_ref)

        sums = sum(ref[0] for ref in stats_refs) / DV
        row_mean = sums[:, 0:1]
        row_scale = lax.rsqrt(sums[:, 128:129] - row_mean * row_mean + EPSILON)
        gain_bias = gain_bias_ref[...].astype(jnp.float32)
        normed = (
            (picked_ref[0].astype(jnp.float32) - row_mean) * row_scale * gain_bias[0:1]
            + gain_bias[1:2]
        ).astype(jnp.bfloat16)
        out_ref[...] += jnp.dot(normed, weight_ref[0], preferred_element_type=jnp.float32)

    def by_slot(*shape):
        return pl.BlockSpec((1, *shape), lambda i: (i, 0, 0))

    def whole(shape):
        return pl.BlockSpec(shape, lambda i: (0, 0))

    return pl.pallas_call(
        body,
        out_shape=jax.ShapeDtypeStruct((tokens, features), jnp.float32),
        grid=(window,),
        in_specs=[by_slot(tokens, width), whole((2, width))]
        + [by_slot(tokens, 256)] * count
        + [by_slot(width, features)],
        out_specs=whole((tokens, features)),
        compiler_params=pltpu.CompilerParams(vmem_limit_bytes=VMEM),
        cost_estimate=LIGHT,
    )(picked, gain_bias, *stats, merge_weight)


def combine(tp_index, order, texts, images, gain_column):
    n_tp = len(texts)
    width, positions = texts[0].shape
    slots = images[0].shape[0]
    count = order.shape[0]
    rows = width * n_tp // count
    share = width // rows

    def body(index_ref, order_ref, gain_ref, *refs):
        text_refs, image_refs = refs[:n_tp], refs[n_tp : 2 * n_tp]
        out_ref, value_ref = refs[2 * n_tp :]
        code = image_refs[0][:, width : width + 2].astype(jnp.float32)
        local = code[:, 0:1] * 256.0 + code[:, 1:2] - 1.0
        place = lax.broadcasted_iota(jnp.int32, (slots, positions), 1).astype(jnp.float32)
        hit = jnp.where(local == place, 1.0, 0.0)
        covered = jnp.max(hit, axis=0, keepdims=True)
        hit = hit.astype(jnp.bfloat16)
        squares = jnp.zeros((1, positions), jnp.float32)
        for distance in range(n_tp):
            first = lax.rem(index_ref[0] + n_tp - distance, n_tp) * share
            image = lax.dot_general(
                image_refs[distance][...],
                hit,
                (((0,), (0,)), ((), ())),
                preferred_element_type=jnp.float32,
            )[:width]
            value = jnp.where(covered > 0.0, image, text_refs[distance][...].astype(jnp.float32))
            squares += jnp.sum(value * value, axis=0, keepdims=True)
            for block in range(share):
                value_ref[first + block] = value[block * rows : (block + 1) * rows]
        scale = lax.rsqrt(squares / (width * n_tp) + EPSILON)
        for block in range(count):
            source = order_ref[block]
            gain = gain_ref[source].astype(jnp.float32)
            out_ref[block] = (value_ref[source] * scale * gain).astype(out_ref.dtype)

    vmem = pl.BlockSpec(memory_space=pltpu.VMEM)
    smem = pl.BlockSpec(memory_space=pltpu.SMEM)
    return pl.pallas_call(
        body,
        out_shape=jax.ShapeDtypeStruct((count, rows, positions), jnp.bfloat16),
        in_specs=[smem, smem] + [vmem] * (1 + 2 * n_tp),
        out_specs=vmem,
        scratch_shapes=[pltpu.VMEM((count, rows, positions), jnp.float32)],
        compiler_params=pltpu.CompilerParams(vmem_limit_bytes=VMEM),
        cost_estimate=LIGHT,
    )(tp_index, order, gain_column, *texts, *images)


def shards(
    n_req, n_tp,
    patches, ln_gain, ln_bias, merge_weight, text_rows, norm_gain, qkv_weight, token_pos, text_len,
):
    row_count, width = text_rows.shape
    me = lax.axis_index("req")
    tp_index = lax.axis_index("tp").reshape(1)
    lines, line_perm, table = ring_tables(n_req)
    x_perm = [(i, i ^ 1) for i in range(n_req)]
    y_perm = [(i, i ^ 2) for i in range(n_req)]
    rows, columns = qkv_weight.shape
    cut = (columns + 255) // 256 * 128

    def along_line(block):
        return lax.ppermute(block, "req", line_perm)

    def from_line(step):
        if step == lines - 1:
            return lax.ppermute(own, "req", [(to, source) for source, to in line_perm])
        return along_line(held[step - 1])

    def to_sides(block):
        return lax.ppermute(block, "req", x_perm), lax.ppermute(block, "req", y_perm)

    def to_corner(by_x, by_y):
        left = lax.ppermute(by_y[:, :cut], "req", x_perm)
        right = lax.ppermute(by_x[:, cut:], "req", y_perm)
        return left, right

    own = qkv_weight
    held = [own]
    held.append(along_line(held[0]))
    sides = [to_sides(held[0])]
    picked, stats_own = pick_rows(patches, merge_weight.shape[0])
    stats = [stats_own] + [tp_shift(stats_own, n_tp, d) for d in range(1, n_tp)]
    gain_bias = jnp.stack([ln_gain, ln_bias])
    text_turned = text_rows.T
    texts = [text_turned] + [tp_shift(text_turned, n_tp, d) for d in range(1, n_tp)]

    token_count = token_pos.shape[0]
    target = lax.div(token_pos, row_count)
    same = target[:, None] == target[None, :]
    ids = jnp.arange(token_count, dtype=jnp.int32)
    before = jnp.sum((same & (ids[None, :] < ids[:, None])).astype(jnp.int32), axis=1)
    slot = target * IMG_CAP + before
    slot_count = n_req * IMG_CAP
    code = lax.rem(token_pos, row_count) + 1
    code_cols = jnp.stack([lax.div(code, 256), lax.rem(code, 256)], axis=1).astype(jnp.bfloat16)

    partial_value = merge(picked, stats, gain_bias, merge_weight)

    partial_value, held[1], sides[0], slot, code_cols, own = tie(
        partial_value, held[1], sides[0], slot, code_cols, own
    )
    held.append(along_line(held[1]))
    sides.append(to_sides(held[1]))
    merged = tp_scatter_sum(partial_value, n_tp, 1).astype(jnp.bfloat16)
    merged, sides[0] = tie(merged, sides[0])
    halves = to_corner(*sides[0])
    padding = (-width - 2) % 128
    payload = jnp.concatenate(
        [merged, code_cols, jnp.zeros((token_count, padding), jnp.bfloat16)], axis=1
    )
    place = (
        jnp.arange(slot_count, dtype=jnp.int32)[:, None] == slot[None, :]
    ).astype(jnp.bfloat16)
    outgoing = jnp.dot(place, payload, preferred_element_type=jnp.float32).astype(jnp.bfloat16)
    arrived = lax.all_to_all(
        outgoing.reshape(n_req, IMG_CAP, -1), "req", split_axis=0, concat_axis=0
    ).reshape(slot_count, -1)

    held[2], sides[1], norm_gain, me = tie(held[2], sides[1], norm_gain, me)
    gain_column = norm_gain.reshape(n_req, rows, 1)
    order = lax.dynamic_slice_in_dim(jnp.asarray(table), me, 1, 0).reshape(-1)
    held.append(from_line(3))
    sides.append(to_sides(held[2]))
    halves, held[3] = tie(halves, held[3])
    images = [arrived] + [tp_shift(arrived, n_tp, d) for d in range(1, n_tp)]
    blocks = combine(tp_index, order, texts, images, gain_column)

    corners = [jnp.concatenate(halves, axis=1)]
    first = jnp.concatenate([held[0], *sides[0], corners[0]], axis=0)
    second = jnp.concatenate([held[1], *sides[1]], axis=0)
    held[3], sides[2], corners[0], first, second = tie(
        held[3], sides[2], corners[0], first, second
    )
    sides.append(to_sides(held[3]))
    corners.append(along_line(corners[0]))
    for step in range(4, lines):
        held.append(from_line(step))
        sides.append(to_sides(held[step]))
    for step in range(2, lines - 2):
        corners.append(along_line(corners[step - 1]))
    corners.append(jnp.concatenate(to_corner(*sides[-2]), axis=1))

    def add_product(total, first, weights):
        weight = jnp.concatenate(weights, axis=0)
        count = weight.shape[0]
        source = blocks[first : first + count // rows].reshape(count, row_count)
        if total is None:
            weight, source = tie(weight, source)
        else:
            weight, source, total = tie(weight, source, total)
        part = lax.dot_general(
            source, weight, (((0,), (0,)), ((), ())), preferred_element_type=jnp.float32
        )
        return part if total is None else total + part

    total = add_product(None, 0, [first])
    total = add_product(total, 4, [second])

    total, sides[-1] = tie(total, sides[-1])
    corners.append(jnp.concatenate(to_corner(*sides[-1]), axis=1))
    for step in range(2, lines - 1):
        total = add_product(total, step * 3 + 1, [held[step], *sides[step]])
    total, late = tie(total, [held[-1], *sides[-1]])
    total = add_product(total, lines * 3 - 2, late)

    position = me * row_count + jnp.arange(row_count, dtype=jnp.int32)
    request_ids = jnp.arange(text_len.shape[0], dtype=jnp.int32)
    limits = jnp.sum(
        jnp.where(
            lax.div(position, SEQ)[:, None] == request_ids[None, :], text_len[None, :], 0
        ),
        axis=1,
    )
    keep = lax.rem(position, SEQ) < limits
    total = add_product(total, lines * 3 + 1, corners[1:])
    return jnp.where(keep[:, None], total, 0.0).astype(jnp.bfloat16)


def solution(mesh):
    placed = (
        P("req", "tp"),
        P("tp"),
        P("tp"),
        P(None, "tp", None),
        P("req", "tp"),
        P(),
        P("req", "tp"),
        P("req"),
        P(),
    )
    body = functools.partial(shards, mesh.shape["req"], mesh.shape["tp"])
    return jax.shard_map(
        body, mesh=mesh, in_specs=placed, out_specs=P("req", "tp"), check_vma=False
    )
```

```python
import functools

import jax
import jax.numpy as jnp
import numpy as np
from jax import lax
from jax.experimental import pallas as pl
from jax.experimental.pallas import tpu as pltpu
from jax.sharding import PartitionSpec as P

DV = 1664
SEQ = 4096
IMG_CAP = 16
EPSILON = 1e-06
VMEM = 32 << 20
LIGHT = pl.CostEstimate(flops=1000, bytes_accessed=1000, transcendentals=0)


def folded_ring(count):
    odd = list(range(1, count, 2))
    even = list(range(0, count, 2))
    return even[:1] + odd + even[:0:-1]


def tp_shift(value, n_tp, distance):
    return lax.ppermute(value, "tp", [(i, (i + distance) % n_tp) for i in range(n_tp)])


def tp_scatter_sum(value, n_tp, axis):
    me = lax.axis_index("tp")
    width = value.shape[axis] // n_tp
    total = lax.dynamic_slice_in_dim(value, me * width, width, axis)
    for distance in range(1, n_tp):
        block = lax.dynamic_slice_in_dim(value, (me + distance) % n_tp * width, width, axis)
        total = total + tp_shift(block, n_tp, distance)
    return total


def ring_tables(n_req):
    lines = n_req // 4
    order = folded_ring(lines)
    following = {order[i]: order[(i + 1) % lines] for i in range(lines)}
    line_perm = [(z * 4 + p, following[z] * 4 + p) for z in range(lines) for p in range(4)]
    arrivals = [(step, flip) for step in range(lines) for flip in range(3)]
    arrivals += [(step, 3) for step in range(lines)]
    table = np.zeros((n_req, n_req), np.int32)
    for index in range(n_req):
        for place, (step, flip) in enumerate(arrivals):
            z = order[(order.index(index // 4) - step) % lines]
            table[index, place] = z * 4 + ((index % 4) ^ flip)
    return lines, line_perm, table


def tie(*values):
    return lax.optimization_barrier(values)


def pick_rows(patches, window):
    rows, width = patches.shape
    tokens = rows // window

    def body(patches_ref, picked_ref, stats_ref):
        taken = lax.broadcasted_iota(jnp.int32, (tokens, rows), 1)
        first = lax.broadcasted_iota(jnp.int32, (tokens, rows), 0) * window
        for slot in range(window):
            chosen = (taken == first + slot).astype(jnp.bfloat16)
            values = jnp.dot(chosen, patches_ref[...], preferred_element_type=jnp.float32)
            picked_ref[slot] = values.astype(jnp.bfloat16)
            sums = jnp.sum(values, axis=1, keepdims=True)
            squares = jnp.sum(values * values, axis=1, keepdims=True)
            stats_ref[slot, :, :128] = jnp.broadcast_to(sums, (tokens, 128))
            stats_ref[slot, :, 128:] = jnp.broadcast_to(squares, (tokens, 128))

    vmem = pl.BlockSpec(memory_space=pltpu.VMEM)
    return pl.pallas_call(
        body,
        out_shape=(
            jax.ShapeDtypeStruct((window, tokens, width), jnp.bfloat16),
            jax.ShapeDtypeStruct((window, tokens, 256), jnp.float32),
        ),
        in_specs=[vmem],
        out_specs=(vmem, vmem),
        compiler_params=pltpu.CompilerParams(vmem_limit_bytes=VMEM),
        cost_estimate=pl.CostEstimate(flops=1000, bytes_accessed=16 << 20, transcendentals=0),
    )(patches)


def merge(picked, stats, gain_bias, merge_weight):
    window, tokens, width = picked.shape
    features = merge_weight.shape[2]
    count = len(stats)

    def body(picked_ref, gain_bias_ref, *refs):
        stats_refs, (weight_ref, out_ref) = refs[:count], refs[count:]

        @pl.when(pl.program_id(0) == 0)
        def _():
            out_ref[...] = jnp.zeros_like(out_ref)

        sums = sum(ref[0] for ref in stats_refs) / DV
        row_mean = sums[:, 0:1]
        row_scale = lax.rsqrt(sums[:, 128:129] - row_mean * row_mean + EPSILON)
        gain_bias = gain_bias_ref[...].astype(jnp.float32)
        normed = (
            (picked_ref[0].astype(jnp.float32) - row_mean) * row_scale * gain_bias[0:1]
            + gain_bias[1:2]
        ).astype(jnp.bfloat16)
        out_ref[...] += jnp.dot(normed, weight_ref[0], preferred_element_type=jnp.float32)

    def by_slot(*shape):
        return pl.BlockSpec((1, *shape), lambda i: (i, 0, 0))

    def whole(shape):
        return pl.BlockSpec(shape, lambda i: (0, 0))

    return pl.pallas_call(
        body,
        out_shape=jax.ShapeDtypeStruct((tokens, features), jnp.float32),
        grid=(window,),
        in_specs=[by_slot(tokens, width), whole((2, width))]
        + [by_slot(tokens, 256)] * count
        + [by_slot(width, features)],
        out_specs=whole((tokens, features)),
        compiler_params=pltpu.CompilerParams(vmem_limit_bytes=VMEM),
        cost_estimate=LIGHT,
    )(picked, gain_bias, *stats, merge_weight)


def combine(tp_index, order, texts, images, gain_column):
    n_tp = len(texts)
    width, positions = texts[0].shape
    slots = images[0].shape[0]
    count = order.shape[0]
    rows = width * n_tp // count
    share = width // rows

    def body(index_ref, order_ref, gain_ref, *refs):
        text_refs, image_refs = refs[:n_tp], refs[n_tp : 2 * n_tp]
        out_ref, value_ref = refs[2 * n_tp :]
        code = image_refs[0][:, width : width + 2].astype(jnp.float32)
        local = code[:, 0:1] * 256.0 + code[:, 1:2] - 1.0
        place = lax.broadcasted_iota(jnp.int32, (slots, positions), 1).astype(jnp.float32)
        hit = jnp.where(local == place, 1.0, 0.0)
        covered = jnp.max(hit, axis=0, keepdims=True)
        hit = hit.astype(jnp.bfloat16)
        squares = jnp.zeros((1, positions), jnp.float32)
        for distance in range(n_tp):
            first = lax.rem(index_ref[0] + n_tp - distance, n_tp) * share
            image = lax.dot_general(
                image_refs[distance][...],
                hit,
                (((0,), (0,)), ((), ())),
                preferred_element_type=jnp.float32,
            )[:width]
            value = jnp.where(covered > 0.0, image, text_refs[distance][...].astype(jnp.float32))
            squares += jnp.sum(value * value, axis=0, keepdims=True)
            for block in range(share):
                value_ref[first + block] = value[block * rows : (block + 1) * rows]
        scale = lax.rsqrt(squares / (width * n_tp) + EPSILON)
        for block in range(count):
            source = order_ref[block]
            gain = gain_ref[source].astype(jnp.float32)
            out_ref[block] = (value_ref[source] * scale * gain).astype(out_ref.dtype)

    vmem = pl.BlockSpec(memory_space=pltpu.VMEM)
    smem = pl.BlockSpec(memory_space=pltpu.SMEM)
    return pl.pallas_call(
        body,
        out_shape=jax.ShapeDtypeStruct((count, rows, positions), jnp.bfloat16),
        in_specs=[smem, smem] + [vmem] * (1 + 2 * n_tp),
        out_specs=vmem,
        scratch_shapes=[pltpu.VMEM((count, rows, positions), jnp.float32)],
        compiler_params=pltpu.CompilerParams(vmem_limit_bytes=VMEM),
        cost_estimate=LIGHT,
    )(tp_index, order, gain_column, *texts, *images)


def shards(
    n_req, n_tp,
    patches, ln_gain, ln_bias, merge_weight, text_rows, norm_gain, qkv_weight, token_pos, text_len,
):
    row_count, width = text_rows.shape
    me = lax.axis_index("req")
    tp_index = lax.axis_index("tp").reshape(1)
    lines, line_perm, table = ring_tables(n_req)
    x_perm = [(i, i ^ 1) for i in range(n_req)]
    y_perm = [(i, i ^ 2) for i in range(n_req)]
    rows, columns = qkv_weight.shape
    cut = (columns + 255) // 256 * 128

    def along_line(block):
        return lax.ppermute(block, "req", line_perm)

    def to_sides(block):
        return lax.ppermute(block, "req", x_perm), lax.ppermute(block, "req", y_perm)

    def to_corner(by_x, by_y):
        left = lax.ppermute(by_y[:, :cut], "req", x_perm)
        right = lax.ppermute(by_x[:, cut:], "req", y_perm)
        return left, right

    held = [qkv_weight]
    held.append(along_line(held[0]))
    sides = [to_sides(held[0])]
    picked, stats_own = pick_rows(patches, merge_weight.shape[0])
    stats = [stats_own] + [tp_shift(stats_own, n_tp, d) for d in range(1, n_tp)]
    gain_bias = jnp.stack([ln_gain, ln_bias])
    text_turned = text_rows.T
    texts = [text_turned] + [tp_shift(text_turned, n_tp, d) for d in range(1, n_tp)]

    token_count = token_pos.shape[0]
    target = lax.div(token_pos, row_count)
    same = target[:, None] == target[None, :]
    ids = jnp.arange(token_count, dtype=jnp.int32)
    before = jnp.sum((same & (ids[None, :] < ids[:, None])).astype(jnp.int32), axis=1)
    slot = target * IMG_CAP + before
    slot_count = n_req * IMG_CAP
    code = lax.rem(token_pos, row_count) + 1
    code_cols = jnp.stack([lax.div(code, 256), lax.rem(code, 256)], axis=1).astype(jnp.bfloat16)

    partial_value = merge(picked, stats, gain_bias, merge_weight)

    partial_value, held[1], sides[0], slot, code_cols = tie(
        partial_value, held[1], sides[0], slot, code_cols
    )
    held.append(along_line(held[1]))
    sides.append(to_sides(held[1]))
    merged = tp_scatter_sum(partial_value, n_tp, 1).astype(jnp.bfloat16)
    merged, sides[0] = tie(merged, sides[0])
    halves = to_corner(*sides[0])
    padding = (-width - 2) % 128
    payload = jnp.concatenate(
        [merged, code_cols, jnp.zeros((token_count, padding), jnp.bfloat16)], axis=1
    )
    place = (
        jnp.arange(slot_count, dtype=jnp.int32)[:, None] == slot[None, :]
    ).astype(jnp.bfloat16)
    outgoing = jnp.dot(place, payload, preferred_element_type=jnp.float32).astype(jnp.bfloat16)
    arrived = lax.all_to_all(
        outgoing.reshape(n_req, IMG_CAP, -1), "req", split_axis=0, concat_axis=0
    ).reshape(slot_count, -1)

    held.append(along_line(held[2]))
    held[2], sides[1], norm_gain, me = tie(held[2], sides[1], norm_gain, me)
    gain_column = norm_gain.reshape(n_req, rows, 1)
    order = lax.dynamic_slice_in_dim(jnp.asarray(table), me, 1, 0).reshape(-1)
    sides.append(to_sides(held[2]))
    images = [arrived] + [tp_shift(arrived, n_tp, d) for d in range(1, n_tp)]
    blocks = combine(tp_index, order, texts, images, gain_column)

    first = jnp.concatenate([held[0], *sides[0]], axis=0)
    second = jnp.concatenate([held[1], *sides[1]], axis=0)
    held[3], sides[2], halves, first, second = tie(held[3], sides[2], halves, first, second)
    sides.append(to_sides(held[3]))
    corners = [jnp.concatenate(halves, axis=1)]
    corners.append(along_line(corners[0]))
    for step in range(4, lines):
        held.append(along_line(held[step - 1]))
        sides.append(to_sides(held[step]))
    for step in range(2, lines - 2):
        corners.append(along_line(corners[step - 1]))
    corners.append(jnp.concatenate(to_corner(*sides[-2]), axis=1))

    def add_product(total, first, weights):
        weight = jnp.concatenate(weights, axis=0)
        count = weight.shape[0]
        source = blocks[first : first + count // rows].reshape(count, row_count)
        if total is None:
            weight, source = tie(weight, source)
        else:
            weight, source, total = tie(weight, source, total)
        part = lax.dot_general(
            source, weight, (((0,), (0,)), ((), ())), preferred_element_type=jnp.float32
        )
        return part if total is None else total + part

    total = add_product(None, 0, [first])
    total = add_product(total, 3, [second])

    total, sides[-1] = tie(total, sides[-1])
    corners.append(jnp.concatenate(to_corner(*sides[-1]), axis=1))
    for step in range(2, lines - 1):
        total = add_product(total, step * 3, [held[step], *sides[step]])
    total, late = tie(total, [held[-1], *sides[-1]])
    total = add_product(total, lines * 3 - 3, late)

    position = me * row_count + jnp.arange(row_count, dtype=jnp.int32)
    request_ids = jnp.arange(text_len.shape[0], dtype=jnp.int32)
    limits = jnp.sum(
        jnp.where(
            lax.div(position, SEQ)[:, None] == request_ids[None, :], text_len[None, :], 0
        ),
        axis=1,
    )
    keep = lax.rem(position, SEQ) < limits
    total = add_product(total, lines * 3, corners)
    return jnp.where(keep[:, None], total, 0.0).astype(jnp.bfloat16)


def solution(mesh):
    placed = (
        P("req", "tp"),
        P("tp"),
        P("tp"),
        P(None, "tp", None),
        P("req", "tp"),
        P(),
        P("req", "tp"),
        P("req"),
        P(),
    )
    body = functools.partial(shards, mesh.shape["req"], mesh.shape["tp"])
    return jax.shard_map(
        body, mesh=mesh, in_specs=placed, out_specs=P("req", "tp"), check_vma=False
    )
```

```python
import functools

import jax
import jax.numpy as jnp
import numpy as np
from jax import lax
from jax.experimental import pallas as pl
from jax.experimental.pallas import tpu as pltpu
from jax.sharding import PartitionSpec as P

DV = 1664
SEQ = 4096
IMG_CAP = 16
EPSILON = 1e-06
VMEM = 32 << 20
LIGHT = pl.CostEstimate(flops=1000, bytes_accessed=1000, transcendentals=0)


def folded_ring(count):
    odd = list(range(1, count, 2))
    even = list(range(0, count, 2))
    return even[:1] + odd + even[:0:-1]


def tp_shift(value, n_tp, distance):
    return lax.ppermute(value, "tp", [(i, (i + distance) % n_tp) for i in range(n_tp)])


def ring_tables(n_req):
    lines = n_req // 4
    order = folded_ring(lines)
    following = {order[i]: order[(i + 1) % lines] for i in range(lines)}
    line_perm = [(z * 4 + p, following[z] * 4 + p) for z in range(lines) for p in range(4)]
    arrivals = [(0, flip) for flip in range(4)]
    arrivals += [(step, flip) for step in range(1, lines) for flip in range(3)]
    arrivals += [(step, 3) for step in range(1, lines)]
    table = np.zeros((n_req, n_req), np.int32)
    for index in range(n_req):
        for place, (step, flip) in enumerate(arrivals):
            z = order[(order.index(index // 4) - step) % lines]
            table[index, place] = z * 4 + ((index % 4) ^ flip)
    return lines, line_perm, table


def tie(*values):
    return lax.optimization_barrier(values)


def pick_rows(patches, window):
    rows, width = patches.shape
    tokens = rows // window

    def body(patches_ref, picked_ref, stats_ref):
        taken = lax.broadcasted_iota(jnp.int32, (tokens, rows), 1)
        first = lax.broadcasted_iota(jnp.int32, (tokens, rows), 0) * window
        for slot in range(window):
            chosen = (taken == first + slot).astype(jnp.bfloat16)
            values = jnp.dot(chosen, patches_ref[...], preferred_element_type=jnp.float32)
            picked_ref[slot] = values.astype(jnp.bfloat16)
            sums = jnp.sum(values, axis=1, keepdims=True)
            squares = jnp.sum(values * values, axis=1, keepdims=True)
            stats_ref[slot, :, :128] = jnp.broadcast_to(sums, (tokens, 128))
            stats_ref[slot, :, 128:] = jnp.broadcast_to(squares, (tokens, 128))

    vmem = pl.BlockSpec(memory_space=pltpu.VMEM)
    return pl.pallas_call(
        body,
        out_shape=(
            jax.ShapeDtypeStruct((window, tokens, width), jnp.bfloat16),
            jax.ShapeDtypeStruct((window, tokens, 256), jnp.float32),
        ),
        in_specs=[vmem],
        out_specs=(vmem, vmem),
        compiler_params=pltpu.CompilerParams(vmem_limit_bytes=VMEM),
        cost_estimate=pl.CostEstimate(flops=1000, bytes_accessed=16 << 20, transcendentals=0),
    )(patches)


def merge(tp_index, picked, stats, gain_bias, merge_weight):
    window, tokens, width = picked.shape
    features = merge_weight.shape[2]
    count = len(stats)
    share = features // count

    def body(index_ref, picked_ref, gain_bias_ref, *refs):
        stats_refs, (weight_ref, *out_refs, total_ref) = refs[:count], refs[count:]

        @pl.when(pl.program_id(0) == 0)
        def _():
            total_ref[...] = jnp.zeros_like(total_ref)

        sums = sum(ref[0] for ref in stats_refs) / DV
        row_mean = sums[:, 0:1]
        row_scale = lax.rsqrt(sums[:, 128:129] - row_mean * row_mean + EPSILON)
        gain_bias = gain_bias_ref[...].astype(jnp.float32)
        normed = (
            (picked_ref[0].astype(jnp.float32) - row_mean) * row_scale * gain_bias[0:1]
            + gain_bias[1:2]
        ).astype(jnp.bfloat16)
        total_ref[...] += jnp.dot(normed, weight_ref[0], preferred_element_type=jnp.float32)

        for index in range(count):

            @pl.when((pl.program_id(0) == window - 1) & (index_ref[0] == index))
            def _():
                for distance, out_ref in enumerate(out_refs):
                    first = (index + distance) % count * share
                    out_ref[...] = total_ref[:, first : first + share]

    def by_slot(*shape):
        return pl.BlockSpec((1, *shape), lambda i: (i, 0, 0))

    def whole(shape):
        return pl.BlockSpec(shape, lambda i: (0, 0))

    return pl.pallas_call(
        body,
        out_shape=[jax.ShapeDtypeStruct((tokens, share), jnp.float32)] * count,
        grid=(window,),
        in_specs=[pl.BlockSpec(memory_space=pltpu.SMEM)]
        + [by_slot(tokens, width), whole((2, width))]
        + [by_slot(tokens, 256)] * count
        + [by_slot(width, features)],
        out_specs=[whole((tokens, share))] * count,
        scratch_shapes=[pltpu.VMEM((tokens, features), jnp.float32)],
        compiler_params=pltpu.CompilerParams(vmem_limit_bytes=VMEM),
        cost_estimate=LIGHT,
    )(tp_index, picked, gain_bias, *stats, merge_weight)


def combine(tp_index, order, texts, images, gain_column):
    n_tp = len(texts)
    width, positions = texts[0].shape
    slots = images[0].shape[0]
    count = order.shape[0]
    rows = width * n_tp // count
    share = width // rows

    def body(index_ref, order_ref, gain_ref, *refs):
        text_refs, image_refs = refs[:n_tp], refs[n_tp : 2 * n_tp]
        out_ref, value_ref = refs[2 * n_tp :]
        code = image_refs[0][:, width : width + 2].astype(jnp.float32)
        local = code[:, 0:1] * 256.0 + code[:, 1:2] - 1.0
        place = lax.broadcasted_iota(jnp.int32, (slots, positions), 1).astype(jnp.float32)
        hit = jnp.where(local == place, 1.0, 0.0)
        covered = jnp.max(hit, axis=0, keepdims=True)
        hit = hit.astype(jnp.bfloat16)
        squares = jnp.zeros((1, positions), jnp.float32)
        for distance in range(n_tp):
            first = lax.rem(index_ref[0] + n_tp - distance, n_tp) * share
            image = lax.dot_general(
                image_refs[distance][...],
                hit,
                (((0,), (0,)), ((), ())),
                preferred_element_type=jnp.float32,
            )[:width]
            value = jnp.where(covered > 0.0, image, text_refs[distance][...].astype(jnp.float32))
            squares += jnp.sum(value * value, axis=0, keepdims=True)
            for block in range(share):
                value_ref[first + block] = value[block * rows : (block + 1) * rows]
        scale = lax.rsqrt(squares / (width * n_tp) + EPSILON)
        for block in range(count):
            source = order_ref[block]
            gain = gain_ref[source].astype(jnp.float32)
            out_ref[block] = (value_ref[source] * scale * gain).astype(out_ref.dtype)

    vmem = pl.BlockSpec(memory_space=pltpu.VMEM)
    smem = pl.BlockSpec(memory_space=pltpu.SMEM)
    return pl.pallas_call(
        body,
        out_shape=jax.ShapeDtypeStruct((count, rows, positions), jnp.bfloat16),
        in_specs=[smem, smem] + [vmem] * (1 + 2 * n_tp),
        out_specs=vmem,
        scratch_shapes=[pltpu.VMEM((count, rows, positions), jnp.float32)],
        compiler_params=pltpu.CompilerParams(vmem_limit_bytes=VMEM),
        cost_estimate=LIGHT,
    )(tp_index, order, gain_column, *texts, *images)


def shards(
    n_req, n_tp,
    patches, ln_gain, ln_bias, merge_weight, text_rows, norm_gain, qkv_weight, token_pos, text_len,
):
    row_count, width = text_rows.shape
    me = lax.axis_index("req")
    tp_index = lax.axis_index("tp").reshape(1)
    lines, line_perm, table = ring_tables(n_req)
    x_perm = [(i, i ^ 1) for i in range(n_req)]
    y_perm = [(i, i ^ 2) for i in range(n_req)]
    rows, columns = qkv_weight.shape
    cut = (columns + 255) // 256 * 128

    def along_line(block):
        return lax.ppermute(block, "req", line_perm)

    def to_sides(block):
        return lax.ppermute(block, "req", x_perm), lax.ppermute(block, "req", y_perm)

    def to_corner(by_x, by_y):
        left = lax.ppermute(by_y[:, :cut], "req", x_perm)
        right = lax.ppermute(by_x[:, cut:], "req", y_perm)
        return left, right

    held = [qkv_weight]
    held.append(along_line(held[0]))
    sides = [to_sides(held[0])]
    picked, stats_own = pick_rows(patches, merge_weight.shape[0])
    stats = [stats_own] + [tp_shift(stats_own, n_tp, d) for d in range(1, n_tp)]
    gain_bias = jnp.stack([ln_gain, ln_bias])
    text_turned = text_rows.T
    texts = [text_turned] + [tp_shift(text_turned, n_tp, d) for d in range(1, n_tp)]

    token_count = token_pos.shape[0]
    target = lax.div(token_pos, row_count)
    same = target[:, None] == target[None, :]
    ids = jnp.arange(token_count, dtype=jnp.int32)
    before = jnp.sum((same & (ids[None, :] < ids[:, None])).astype(jnp.int32), axis=1)
    slot = target * IMG_CAP + before
    slot_count = n_req * IMG_CAP
    code = lax.rem(token_pos, row_count) + 1
    code_cols = jnp.stack([lax.div(code, 256), lax.rem(code, 256)], axis=1).astype(jnp.bfloat16)

    partial_value = merge(tp_index, picked, stats, gain_bias, merge_weight)

    partial_value, held[1], sides[0], slot, code_cols = tie(
        partial_value, held[1], sides[0], slot, code_cols
    )
    held.append(along_line(held[1]))
    sides.append(to_sides(held[1]))
    merged = partial_value[0]
    for distance in range(1, n_tp):
        merged = merged + tp_shift(partial_value[distance], n_tp, distance)
    merged = merged.astype(jnp.bfloat16)
    merged, sides[0] = tie(merged, sides[0])
    halves = to_corner(*sides[0])
    padding = (-width - 2) % 128
    payload = jnp.concatenate(
        [merged, code_cols, jnp.zeros((token_count, padding), jnp.bfloat16)], axis=1
    )
    place = (
        jnp.arange(slot_count, dtype=jnp.int32)[:, None] == slot[None, :]
    ).astype(jnp.bfloat16)
    outgoing = jnp.dot(place, payload, preferred_element_type=jnp.float32).astype(jnp.bfloat16)
    arrived = lax.all_to_all(
        outgoing.reshape(n_req, IMG_CAP, -1), "req", split_axis=0, concat_axis=0
    ).reshape(slot_count, -1)

    held[2], sides[1], norm_gain, me = tie(held[2], sides[1], norm_gain, me)
    gain_column = norm_gain.reshape(n_req, rows, 1)
    order = lax.dynamic_slice_in_dim(jnp.asarray(table), me, 1, 0).reshape(-1)
    held.append(along_line(held[2]))
    sides.append(to_sides(held[2]))
    images = [arrived] + [tp_shift(arrived, n_tp, d) for d in range(1, n_tp)]
    blocks = combine(tp_index, order, texts, images, gain_column)

    corners = [jnp.concatenate(halves, axis=1)]
    first = jnp.concatenate([held[0], *sides[0], corners[0]], axis=0)
    second = jnp.concatenate([held[1], *sides[1]], axis=0)
    held[3], sides[2], corners[0], first, second = tie(
        held[3], sides[2], corners[0], first, second
    )
    sides.append(to_sides(held[3]))
    corners.append(along_line(corners[0]))
    for step in range(4, lines):
        held.append(along_line(held[step - 1]))
        sides.append(to_sides(held[step]))
    for step in range(2, lines - 2):
        corners.append(along_line(corners[step - 1]))
    corners.append(jnp.concatenate(to_corner(*sides[-2]), axis=1))

    def add_product(total, first, weights):
        weight = jnp.concatenate(weights, axis=0)
        count = weight.shape[0]
        source = blocks[first : first + count // rows].reshape(count, row_count)
        if total is None:
            weight, source = tie(weight, source)
        else:
            weight, source, total = tie(weight, source, total)
        part = lax.dot_general(
            source, weight, (((0,), (0,)), ((), ())), preferred_element_type=jnp.float32
        )
        return part if total is None else total + part

    total = add_product(None, 0, [first])
    total = add_product(total, 4, [second])

    total, sides[-1] = tie(total, sides[-1])
    corners.append(jnp.concatenate(to_corner(*sides[-1]), axis=1))
    for step in range(2, lines - 1):
        total = add_product(total, step * 3 + 1, [held[step], *sides[step]])
    total, late = tie(total, [held[-1], *sides[-1]])
    total = add_product(total, lines * 3 - 2, late)

    position = me * row_count + jnp.arange(row_count, dtype=jnp.int32)
    request_ids = jnp.arange(text_len.shape[0], dtype=jnp.int32)
    limits = jnp.sum(
        jnp.where(
            lax.div(position, SEQ)[:, None] == request_ids[None, :], text_len[None, :], 0
        ),
        axis=1,
    )
    keep = lax.rem(position, SEQ) < limits
    total = add_product(total, lines * 3 + 1, corners[1:])
    return jnp.where(keep[:, None], total, 0.0).astype(jnp.bfloat16)


def solution(mesh):
    placed = (
        P("req", "tp"),
        P("tp"),
        P("tp"),
        P(None, "tp", None),
        P("req", "tp"),
        P(),
        P("req", "tp"),
        P("req"),
        P(),
    )
    body = functools.partial(shards, mesh.shape["req"], mesh.shape["tp"])
    return jax.shard_map(
        body, mesh=mesh, in_specs=placed, out_specs=P("req", "tp"), check_vma=False
    )
```

```python
import functools

import jax
import jax.numpy as jnp
import numpy as np
from jax import lax
from jax.experimental import pallas as pl
from jax.experimental.pallas import tpu as pltpu
from jax.sharding import PartitionSpec as P

DV = 1664
SEQ = 4096
IMG_CAP = 16
EPSILON = 1e-06
VMEM = 32 << 20
LIGHT = pl.CostEstimate(flops=1000, bytes_accessed=1000, transcendentals=0)


def folded_ring(count):
    odd = list(range(1, count, 2))
    even = list(range(0, count, 2))
    return even[:1] + odd + even[:0:-1]


def tp_shift(value, n_tp, distance):
    return lax.ppermute(value, "tp", [(i, (i + distance) % n_tp) for i in range(n_tp)])


def ring_tables(n_req):
    lines = n_req // 4
    order = folded_ring(lines)
    following = {order[i]: order[(i + 1) % lines] for i in range(lines)}
    line_perm = [(z * 4 + p, following[z] * 4 + p) for z in range(lines) for p in range(4)]
    arrivals = [(0, 0), (0, 1), (0, 2), (1, 0), (1, 1), (1, 2), (0, 3)]
    arrivals += [(step, flip) for step in range(2, lines) for flip in range(3)]
    arrivals += [(step, 3) for step in range(1, lines)]
    table = np.zeros((n_req, n_req), np.int32)
    for index in range(n_req):
        for place, (step, flip) in enumerate(arrivals):
            z = order[(order.index(index // 4) - step) % lines]
            table[index, place] = z * 4 + ((index % 4) ^ flip)
    return lines, line_perm, table


def tie(*values):
    return lax.optimization_barrier(values)


def pick_rows(patches, window):
    rows, width = patches.shape
    tokens = rows // window

    def body(patches_ref, picked_ref, stats_ref):
        taken = lax.broadcasted_iota(jnp.int32, (tokens, rows), 1)
        first = lax.broadcasted_iota(jnp.int32, (tokens, rows), 0) * window
        for slot in range(window):
            chosen = (taken == first + slot).astype(jnp.bfloat16)
            values = jnp.dot(chosen, patches_ref[...], preferred_element_type=jnp.float32)
            picked_ref[slot] = values.astype(jnp.bfloat16)
            sums = jnp.sum(values, axis=1, keepdims=True)
            squares = jnp.sum(values * values, axis=1, keepdims=True)
            stats_ref[slot, :, :128] = jnp.broadcast_to(sums, (tokens, 128))
            stats_ref[slot, :, 128:] = jnp.broadcast_to(squares, (tokens, 128))

    vmem = pl.BlockSpec(memory_space=pltpu.VMEM)
    return pl.pallas_call(
        body,
        out_shape=(
            jax.ShapeDtypeStruct((window, tokens, width), jnp.bfloat16),
            jax.ShapeDtypeStruct((window, tokens, 256), jnp.float32),
        ),
        in_specs=[vmem],
        out_specs=(vmem, vmem),
        compiler_params=pltpu.CompilerParams(vmem_limit_bytes=VMEM),
        cost_estimate=pl.CostEstimate(flops=1000, bytes_accessed=16 << 20, transcendentals=0),
    )(patches)


def merge(tp_index, picked, stats, gain_bias, merge_weight):
    window, tokens, width = picked.shape
    features = merge_weight.shape[2]
    count = len(stats)
    share = features // count

    def body(index_ref, picked_ref, gain_bias_ref, *refs):
        stats_refs, (weight_ref, *out_refs, total_ref) = refs[:count], refs[count:]

        @pl.when(pl.program_id(0) == 0)
        def _():
            total_ref[...] = jnp.zeros_like(total_ref)

        sums = sum(ref[0] for ref in stats_refs) / DV
        row_mean = sums[:, 0:1]
        row_scale = lax.rsqrt(sums[:, 128:129] - row_mean * row_mean + EPSILON)
        gain_bias = gain_bias_ref[...].astype(jnp.float32)
        normed = (
            (picked_ref[0].astype(jnp.float32) - row_mean) * row_scale * gain_bias[0:1]
            + gain_bias[1:2]
        ).astype(jnp.bfloat16)
        total_ref[...] += jnp.dot(normed, weight_ref[0], preferred_element_type=jnp.float32)

        for index in range(count):

            @pl.when((pl.program_id(0) == window - 1) & (index_ref[0] == index))
            def _():
                for distance, out_ref in enumerate(out_refs):
                    first = (index + distance) % count * share
                    out_ref[...] = total_ref[:, first : first + share]

    def by_slot(*shape):
        return pl.BlockSpec((1, *shape), lambda i: (i, 0, 0))

    def whole(shape):
        return pl.BlockSpec(shape, lambda i: (0, 0))

    return pl.pallas_call(
        body,
        out_shape=[jax.ShapeDtypeStruct((tokens, share), jnp.float32)] * count,
        grid=(window,),
        in_specs=[pl.BlockSpec(memory_space=pltpu.SMEM)]
        + [by_slot(tokens, width), whole((2, width))]
        + [by_slot(tokens, 256)] * count
        + [by_slot(width, features)],
        out_specs=[whole((tokens, share))] * count,
        scratch_shapes=[pltpu.VMEM((tokens, features), jnp.float32)],
        compiler_params=pltpu.CompilerParams(vmem_limit_bytes=VMEM),
        cost_estimate=LIGHT,
    )(tp_index, picked, gain_bias, *stats, merge_weight)


def combine(tp_index, order, texts, images, gain_column):
    n_tp = len(texts)
    width, positions = texts[0].shape
    slots = images[0].shape[0]
    count = order.shape[0]
    rows = width * n_tp // count
    share = width // rows

    def body(index_ref, order_ref, gain_ref, *refs):
        text_refs, image_refs = refs[:n_tp], refs[n_tp : 2 * n_tp]
        out_ref, value_ref = refs[2 * n_tp :]
        code = image_refs[0][:, width : width + 2].astype(jnp.float32)
        local = code[:, 0:1] * 256.0 + code[:, 1:2] - 1.0
        place = lax.broadcasted_iota(jnp.int32, (slots, positions), 1).astype(jnp.float32)
        hit = jnp.where(local == place, 1.0, 0.0)
        covered = jnp.max(hit, axis=0, keepdims=True)
        hit = hit.astype(jnp.bfloat16)
        squares = jnp.zeros((1, positions), jnp.float32)
        for distance in range(n_tp):
            first = lax.rem(index_ref[0] + n_tp - distance, n_tp) * share
            image = lax.dot_general(
                image_refs[distance][...],
                hit,
                (((0,), (0,)), ((), ())),
                preferred_element_type=jnp.float32,
            )[:width]
            value = jnp.where(covered > 0.0, image, text_refs[distance][...].astype(jnp.float32))
            squares += jnp.sum(value * value, axis=0, keepdims=True)
            for block in range(share):
                value_ref[first + block] = value[block * rows : (block + 1) * rows]
        scale = lax.rsqrt(squares / (width * n_tp) + EPSILON)
        for block in range(count):
            source = order_ref[block]
            gain = gain_ref[source].astype(jnp.float32)
            out_ref[block] = (value_ref[source] * scale * gain).astype(out_ref.dtype)

    vmem = pl.BlockSpec(memory_space=pltpu.VMEM)
    smem = pl.BlockSpec(memory_space=pltpu.SMEM)
    return pl.pallas_call(
        body,
        out_shape=jax.ShapeDtypeStruct((count, rows, positions), jnp.bfloat16),
        in_specs=[smem, smem] + [vmem] * (1 + 2 * n_tp),
        out_specs=vmem,
        scratch_shapes=[pltpu.VMEM((count, rows, positions), jnp.float32)],
        compiler_params=pltpu.CompilerParams(vmem_limit_bytes=VMEM),
        cost_estimate=LIGHT,
    )(tp_index, order, gain_column, *texts, *images)


def shards(
    n_req, n_tp,
    patches, ln_gain, ln_bias, merge_weight, text_rows, norm_gain, qkv_weight, token_pos, text_len,
):
    row_count, width = text_rows.shape
    me = lax.axis_index("req")
    tp_index = lax.axis_index("tp").reshape(1)
    lines, line_perm, table = ring_tables(n_req)
    x_perm = [(i, i ^ 1) for i in range(n_req)]
    y_perm = [(i, i ^ 2) for i in range(n_req)]
    rows, columns = qkv_weight.shape
    cut = (columns + 255) // 256 * 128

    def along_line(block):
        return lax.ppermute(block, "req", line_perm)

    def to_sides(block):
        return lax.ppermute(block, "req", x_perm), lax.ppermute(block, "req", y_perm)

    def to_corner(by_x, by_y):
        left = lax.ppermute(by_y[:, :cut], "req", x_perm)
        right = lax.ppermute(by_x[:, cut:], "req", y_perm)
        return left, right

    held = [qkv_weight]
    held.append(along_line(held[0]))
    sides = [to_sides(held[0])]
    picked, stats_own = pick_rows(patches, merge_weight.shape[0])
    stats = [stats_own] + [tp_shift(stats_own, n_tp, d) for d in range(1, n_tp)]
    gain_bias = jnp.stack([ln_gain, ln_bias])
    text_turned = text_rows.T
    texts = [text_turned] + [tp_shift(text_turned, n_tp, d) for d in range(1, n_tp)]

    token_count = token_pos.shape[0]
    target = lax.div(token_pos, row_count)
    same = target[:, None] == target[None, :]
    ids = jnp.arange(token_count, dtype=jnp.int32)
    before = jnp.sum((same & (ids[None, :] < ids[:, None])).astype(jnp.int32), axis=1)
    slot = target * IMG_CAP + before
    slot_count = n_req * IMG_CAP
    code = lax.rem(token_pos, row_count) + 1
    code_cols = jnp.stack([lax.div(code, 256), lax.rem(code, 256)], axis=1).astype(jnp.bfloat16)

    partial_value = merge(tp_index, picked, stats, gain_bias, merge_weight)

    partial_value, held[1], sides[0], slot, code_cols = tie(
        partial_value, held[1], sides[0], slot, code_cols
    )
    held.append(along_line(held[1]))
    sides.append(to_sides(held[1]))
    merged = partial_value[0]
    for distance in range(1, n_tp):
        merged = merged + tp_shift(partial_value[distance], n_tp, distance)
    merged = merged.astype(jnp.bfloat16)
    merged, sides[0] = tie(merged, sides[0])
    halves = to_corner(*sides[0])
    padding = (-width - 2) % 128
    payload = jnp.concatenate(
        [merged, code_cols, jnp.zeros((token_count, padding), jnp.bfloat16)], axis=1
    )
    place = (
        jnp.arange(slot_count, dtype=jnp.int32)[:, None] == slot[None, :]
    ).astype(jnp.bfloat16)
    outgoing = jnp.dot(place, payload, preferred_element_type=jnp.float32).astype(jnp.bfloat16)
    arrived = lax.all_to_all(
        outgoing.reshape(n_req, IMG_CAP, -1), "req", split_axis=0, concat_axis=0
    ).reshape(slot_count, -1)

    held[2], sides[1], norm_gain, me = tie(held[2], sides[1], norm_gain, me)
    gain_column = norm_gain.reshape(n_req, rows, 1)
    order = lax.dynamic_slice_in_dim(jnp.asarray(table), me, 1, 0).reshape(-1)
    held.append(along_line(held[2]))
    sides.append(to_sides(held[2]))
    images = [arrived] + [tp_shift(arrived, n_tp, d) for d in range(1, n_tp)]
    blocks = combine(tp_index, order, texts, images, gain_column)

    first = jnp.concatenate([held[0], *sides[0]], axis=0)
    last_sides = sides[2]
    held[3], sides[2], halves, first = tie(held[3], sides[2], halves, first)
    sides.append(to_sides(held[3]))
    corners = [jnp.concatenate(halves, axis=1)]
    second = jnp.concatenate([held[1], *sides[1], corners[0]], axis=0)
    corners.append(along_line(corners[0]))
    for step in range(4, lines):
        held.append(along_line(held[step - 1]))
        sides.append(to_sides(held[step]))
    for step in range(2, lines - 2):
        corners.append(along_line(corners[step - 1]))
    corners.append(jnp.concatenate(to_corner(*(last_sides if lines == 4 else sides[-2])), axis=1))

    def add_product(total, first, weights):
        weight = jnp.concatenate(weights, axis=0)
        count = weight.shape[0]
        source = blocks[first : first + count // rows].reshape(count, row_count)
        if total is None:
            weight, source = tie(weight, source)
        else:
            weight, source, total = tie(weight, source, total)
        part = lax.dot_general(
            source, weight, (((0,), (0,)), ((), ())), preferred_element_type=jnp.float32
        )
        return part if total is None else total + part

    total = add_product(None, 0, [first])
    total = add_product(total, 3, [second])

    total, sides[-1] = tie(total, sides[-1])
    corners.append(jnp.concatenate(to_corner(*sides[-1]), axis=1))
    for step in range(2, lines - 1):
        total = add_product(total, step * 3 + 1, [held[step], *sides[step]])
    total, late = tie(total, [held[-1], *sides[-1]])
    total = add_product(total, lines * 3 - 2, late)

    position = me * row_count + jnp.arange(row_count, dtype=jnp.int32)
    request_ids = jnp.arange(text_len.shape[0], dtype=jnp.int32)
    limits = jnp.sum(
        jnp.where(
            lax.div(position, SEQ)[:, None] == request_ids[None, :], text_len[None, :], 0
        ),
        axis=1,
    )
    keep = lax.rem(position, SEQ) < limits
    total = add_product(total, lines * 3 + 1, corners[1:])
    return jnp.where(keep[:, None], total, 0.0).astype(jnp.bfloat16)


def solution(mesh):
    placed = (
        P("req", "tp"),
        P("tp"),
        P("tp"),
        P(None, "tp", None),
        P("req", "tp"),
        P(),
        P("req", "tp"),
        P("req"),
        P(),
    )
    body = functools.partial(shards, mesh.shape["req"], mesh.shape["tp"])
    return jax.shard_map(
        body, mesh=mesh, in_specs=placed, out_specs=P("req", "tp"), check_vma=False
    )
```

```python
import functools

import jax
import jax.numpy as jnp
import numpy as np
from jax import lax
from jax.experimental import pallas as pl
from jax.experimental.pallas import tpu as pltpu
from jax.sharding import PartitionSpec as P

DV = 1664
SEQ = 4096
IMG_CAP = 16
EPSILON = 1e-06
VMEM = 32 << 20
LIGHT = pl.CostEstimate(flops=1000, bytes_accessed=1000, transcendentals=0)


def folded_ring(count):
    odd = list(range(1, count, 2))
    even = list(range(0, count, 2))
    return even[:1] + odd + even[:0:-1]


def tp_shift(value, n_tp, distance):
    return lax.ppermute(value, "tp", [(i, (i + distance) % n_tp) for i in range(n_tp)])


def ring_tables(n_req):
    lines = n_req // 4
    order = folded_ring(lines)
    following = {order[i]: order[(i + 1) % lines] for i in range(lines)}
    line_perm = [(z * 4 + p, following[z] * 4 + p) for z in range(lines) for p in range(4)]
    arrivals = [(0, flip) for flip in range(4)]
    arrivals += [(step, flip) for step in range(1, lines) for flip in range(3)]
    arrivals += [(step, 3) for step in range(1, lines)]
    table = np.zeros((n_req, n_req), np.int32)
    for index in range(n_req):
        for place, (step, flip) in enumerate(arrivals):
            z = order[(order.index(index // 4) - step) % lines]
            table[index, place] = z * 4 + ((index % 4) ^ flip)
    return lines, line_perm, table


def tie(*values):
    return lax.optimization_barrier(values)


def pick_rows(patches, window):
    rows, width = patches.shape
    tokens = rows // window

    def body(patches_ref, picked_ref, stats_ref):
        taken = lax.broadcasted_iota(jnp.int32, (tokens, rows), 1)
        first = lax.broadcasted_iota(jnp.int32, (tokens, rows), 0) * window
        for slot in range(window):
            chosen = (taken == first + slot).astype(jnp.bfloat16)
            values = jnp.dot(chosen, patches_ref[...], preferred_element_type=jnp.float32)
            picked_ref[slot] = values.astype(jnp.bfloat16)
            sums = jnp.sum(values, axis=1, keepdims=True)
            squares = jnp.sum(values * values, axis=1, keepdims=True)
            stats_ref[slot, :, :128] = jnp.broadcast_to(sums, (tokens, 128))
            stats_ref[slot, :, 128:] = jnp.broadcast_to(squares, (tokens, 128))

    vmem = pl.BlockSpec(memory_space=pltpu.VMEM)
    return pl.pallas_call(
        body,
        out_shape=(
            jax.ShapeDtypeStruct((window, tokens, width), jnp.bfloat16),
            jax.ShapeDtypeStruct((window, tokens, 256), jnp.float32),
        ),
        in_specs=[vmem],
        out_specs=(vmem, vmem),
        compiler_params=pltpu.CompilerParams(vmem_limit_bytes=VMEM),
        cost_estimate=pl.CostEstimate(flops=1000, bytes_accessed=16 << 20, transcendentals=0),
    )(patches)


def merge(tp_index, picked, stats, gain_bias, merge_weight):
    window, tokens, width = picked.shape
    features = merge_weight.shape[2]
    count = len(stats)
    share = features // count

    def body(index_ref, picked_ref, gain_bias_ref, *refs):
        stats_refs, (weight_ref, *out_refs, total_ref) = refs[:count], refs[count:]

        @pl.when(pl.program_id(0) == 0)
        def _():
            total_ref[...] = jnp.zeros_like(total_ref)

        sums = sum(ref[0] for ref in stats_refs) / DV
        row_mean = sums[:, 0:1]
        row_scale = lax.rsqrt(sums[:, 128:129] - row_mean * row_mean + EPSILON)
        gain_bias = gain_bias_ref[...].astype(jnp.float32)
        normed = (
            (picked_ref[0].astype(jnp.float32) - row_mean) * row_scale * gain_bias[0:1]
            + gain_bias[1:2]
        ).astype(jnp.bfloat16)
        total_ref[...] += jnp.dot(normed, weight_ref[0], preferred_element_type=jnp.float32)

        for index in range(count):

            @pl.when((pl.program_id(0) == window - 1) & (index_ref[0] == index))
            def _():
                for distance, out_ref in enumerate(out_refs):
                    first = (index + distance) % count * share
                    out_ref[...] = total_ref[:, first : first + share]

    def by_slot(*shape):
        return pl.BlockSpec((1, *shape), lambda i: (i, 0, 0))

    def whole(shape):
        return pl.BlockSpec(shape, lambda i: (0, 0))

    return pl.pallas_call(
        body,
        out_shape=[jax.ShapeDtypeStruct((tokens, share), jnp.float32)] * count,
        grid=(window,),
        in_specs=[pl.BlockSpec(memory_space=pltpu.SMEM)]
        + [by_slot(tokens, width), whole((2, width))]
        + [by_slot(tokens, 256)] * count
        + [by_slot(width, features)],
        out_specs=[whole((tokens, share))] * count,
        scratch_shapes=[pltpu.VMEM((tokens, features), jnp.float32)],
        compiler_params=pltpu.CompilerParams(vmem_limit_bytes=VMEM),
        cost_estimate=LIGHT,
    )(tp_index, picked, gain_bias, *stats, merge_weight)


def combine(tp_index, order, texts, images, gain_column):
    n_tp = len(texts)
    width, positions = texts[0].shape
    slots = images[0].shape[0]
    count = order.shape[0]
    rows = width * n_tp // count
    share = width // rows

    def body(index_ref, order_ref, gain_ref, *refs):
        text_refs, image_refs = refs[:n_tp], refs[n_tp : 2 * n_tp]
        out_ref, value_ref = refs[2 * n_tp :]
        code = image_refs[0][:, width : width + 2].astype(jnp.float32)
        local = code[:, 0:1] * 256.0 + code[:, 1:2] - 1.0
        place = lax.broadcasted_iota(jnp.int32, (slots, positions), 1).astype(jnp.float32)
        hit = jnp.where(local == place, 1.0, 0.0)
        covered = jnp.max(hit, axis=0, keepdims=True)
        hit = hit.astype(jnp.bfloat16)
        squares = jnp.zeros((1, positions), jnp.float32)
        for distance in range(n_tp):
            first = lax.rem(index_ref[0] + n_tp - distance, n_tp) * share
            image = lax.dot_general(
                image_refs[distance][...],
                hit,
                (((0,), (0,)), ((), ())),
                preferred_element_type=jnp.float32,
            )[:width]
            value = jnp.where(covered > 0.0, image, text_refs[distance][...].astype(jnp.float32))
            squares += jnp.sum(value * value, axis=0, keepdims=True)
            for block in range(share):
                value_ref[first + block] = value[block * rows : (block + 1) * rows]
        scale = lax.rsqrt(squares / (width * n_tp) + EPSILON)
        for block in range(count):
            source = order_ref[block]
            gain = gain_ref[source].astype(jnp.float32)
            out_ref[block] = (value_ref[source] * scale * gain).astype(out_ref.dtype)

    vmem = pl.BlockSpec(memory_space=pltpu.VMEM)
    smem = pl.BlockSpec(memory_space=pltpu.SMEM)
    return pl.pallas_call(
        body,
        out_shape=jax.ShapeDtypeStruct((count, rows, positions), jnp.bfloat16),
        in_specs=[smem, smem] + [vmem] * (1 + 2 * n_tp),
        out_specs=vmem,
        scratch_shapes=[pltpu.VMEM((count, rows, positions), jnp.float32)],
        compiler_params=pltpu.CompilerParams(vmem_limit_bytes=VMEM),
        cost_estimate=LIGHT,
    )(tp_index, order, gain_column, *texts, *images)


def shards(
    n_req, n_tp,
    patches, ln_gain, ln_bias, merge_weight, text_rows, norm_gain, qkv_weight, token_pos, text_len,
):
    row_count, width = text_rows.shape
    me = lax.axis_index("req")
    tp_index = lax.axis_index("tp").reshape(1)
    lines, line_perm, table = ring_tables(n_req)
    x_perm = [(i, i ^ 1) for i in range(n_req)]
    y_perm = [(i, i ^ 2) for i in range(n_req)]
    rows, columns = qkv_weight.shape
    cut = (columns + 255) // 256 * 128

    def along_line(block):
        return lax.ppermute(block, "req", line_perm)

    def to_sides(block):
        return lax.ppermute(block, "req", x_perm), lax.ppermute(block, "req", y_perm)

    def to_corner(by_x, by_y):
        left = lax.ppermute(by_y[:, :cut], "req", x_perm)
        right = lax.ppermute(by_x[:, cut:], "req", y_perm)
        return left, right

    held = [qkv_weight]
    held.append(along_line(held[0]))
    sides = [to_sides(held[0])]
    picked, stats_own = pick_rows(patches, merge_weight.shape[0])
    stats = [stats_own] + [tp_shift(stats_own, n_tp, d) for d in range(1, n_tp)]
    gain_bias = jnp.stack([ln_gain, ln_bias])
    text_turned = text_rows.T
    texts = [text_turned] + [tp_shift(text_turned, n_tp, d) for d in range(1, n_tp)]

    partial_value = merge(tp_index, picked, stats, gain_bias, merge_weight)

    partial_value, held[1], token_pos = tie(partial_value, held[1], token_pos)
    token_count = token_pos.shape[0]
    target = lax.div(token_pos, row_count)
    same = target[:, None] == target[None, :]
    ids = jnp.arange(token_count, dtype=jnp.int32)
    before = jnp.sum((same & (ids[None, :] < ids[:, None])).astype(jnp.int32), axis=1)
    slot = target * IMG_CAP + before
    slot_count = n_req * IMG_CAP
    code = lax.rem(token_pos, row_count) + 1
    code_cols = jnp.stack([lax.div(code, 256), lax.rem(code, 256)], axis=1).astype(jnp.bfloat16)
    held.append(along_line(held[1]))
    sides.append(to_sides(held[1]))
    merged = partial_value[0]
    for distance in range(1, n_tp):
        merged = merged + tp_shift(partial_value[distance], n_tp, distance)
    merged = merged.astype(jnp.bfloat16)
    merged, sides[0] = tie(merged, sides[0])
    halves = to_corner(*sides[0])
    padding = (-width - 2) % 128
    payload = jnp.concatenate(
        [merged, code_cols, jnp.zeros((token_count, padding), jnp.bfloat16)], axis=1
    )
    place = (
        jnp.arange(slot_count, dtype=jnp.int32)[:, None] == slot[None, :]
    ).astype(jnp.bfloat16)
    outgoing = jnp.dot(place, payload, preferred_element_type=jnp.float32).astype(jnp.bfloat16)
    arrived = lax.all_to_all(
        outgoing.reshape(n_req, IMG_CAP, -1), "req", split_axis=0, concat_axis=0
    ).reshape(slot_count, -1)

    held[2], sides[1], norm_gain, me = tie(held[2], sides[1], norm_gain, me)
    gain_column = norm_gain.reshape(n_req, rows, 1)
    order = lax.dynamic_slice_in_dim(jnp.asarray(table), me, 1, 0).reshape(-1)
    held.append(along_line(held[2]))
    sides.append(to_sides(held[2]))
    images = [arrived] + [tp_shift(arrived, n_tp, d) for d in range(1, n_tp)]
    blocks = combine(tp_index, order, texts, images, gain_column)

    corners = [jnp.concatenate(halves, axis=1)]
    first = jnp.concatenate([held[0], *sides[0], corners[0]], axis=0)
    second = jnp.concatenate([held[1], *sides[1]], axis=0)
    held[3], sides[2], corners[0], first, second = tie(
        held[3], sides[2], corners[0], first, second
    )
    sides.append(to_sides(held[3]))
    corners.append(along_line(corners[0]))
    for step in range(4, lines):
        held.append(along_line(held[step - 1]))
        sides.append(to_sides(held[step]))
    for step in range(2, lines - 2):
        corners.append(along_line(corners[step - 1]))
    corners.append(jnp.concatenate(to_corner(*sides[-2]), axis=1))

    def add_product(total, first, weights):
        weight = jnp.concatenate(weights, axis=0)
        count = weight.shape[0]
        source = blocks[first : first + count // rows].reshape(count, row_count)
        if total is None:
            weight, source = tie(weight, source)
        else:
            weight, source, total = tie(weight, source, total)
        part = lax.dot_general(
            source, weight, (((0,), (0,)), ((), ())), preferred_element_type=jnp.float32
        )
        return part if total is None else total + part

    total = add_product(None, 0, [first])
    total = add_product(total, 4, [second])

    total, sides[-1] = tie(total, sides[-1])
    corners.append(jnp.concatenate(to_corner(*sides[-1]), axis=1))
    for step in range(2, lines - 1):
        total = add_product(total, step * 3 + 1, [held[step], *sides[step]])
    total, late = tie(total, [held[-1], *sides[-1]])
    total = add_product(total, lines * 3 - 2, late)

    position = me * row_count + jnp.arange(row_count, dtype=jnp.int32)
    request_ids = jnp.arange(text_len.shape[0], dtype=jnp.int32)
    limits = jnp.sum(
        jnp.where(
            lax.div(position, SEQ)[:, None] == request_ids[None, :], text_len[None, :], 0
        ),
        axis=1,
    )
    keep = lax.rem(position, SEQ) < limits
    total = add_product(total, lines * 3 + 1, corners[1:])
    return jnp.where(keep[:, None], total, 0.0).astype(jnp.bfloat16)


def solution(mesh):
    placed = (
        P("req", "tp"),
        P("tp"),
        P("tp"),
        P(None, "tp", None),
        P("req", "tp"),
        P(),
        P("req", "tp"),
        P("req"),
        P(),
    )
    body = functools.partial(shards, mesh.shape["req"], mesh.shape["tp"])
    return jax.shard_map(
        body, mesh=mesh, in_specs=placed, out_specs=P("req", "tp"), check_vma=False
    )
```

```python
import functools

import jax
import jax.numpy as jnp
import numpy as np
from jax import lax
from jax.experimental import pallas as pl
from jax.experimental.pallas import tpu as pltpu
from jax.sharding import PartitionSpec as P

DV = 1664
SEQ = 4096
IMG_CAP = 16
EPSILON = 1e-06
VMEM = 32 << 20
LIGHT = pl.CostEstimate(flops=1000, bytes_accessed=1000, transcendentals=0)


def folded_ring(count):
    odd = list(range(1, count, 2))
    even = list(range(0, count, 2))
    return even[:1] + odd + even[:0:-1]


def tp_shift(value, n_tp, distance):
    return lax.ppermute(value, "tp", [(i, (i + distance) % n_tp) for i in range(n_tp)])


def ring_tables(n_req):
    lines = n_req // 4
    order = folded_ring(lines)
    following = {order[i]: order[(i + 1) % lines] for i in range(lines)}
    line_perm = [(z * 4 + p, following[z] * 4 + p) for z in range(lines) for p in range(4)]
    arrivals = [(0, flip) for flip in range(4)]
    arrivals += [(step, flip) for step in range(1, lines) for flip in range(3)]
    arrivals += [(step, 3) for step in range(1, lines)]
    table = np.zeros((n_req, n_req), np.int32)
    for index in range(n_req):
        for place, (step, flip) in enumerate(arrivals):
            z = order[(order.index(index // 4) - step) % lines]
            table[index, place] = z * 4 + ((index % 4) ^ flip)
    return lines, line_perm, table


def tie(*values):
    return lax.optimization_barrier(values)


def pick_rows(patches, window):
    rows, width = patches.shape
    tokens = rows // window

    def body(patches_ref, picked_ref, stats_ref):
        taken = lax.broadcasted_iota(jnp.int32, (tokens, rows), 1)
        first = lax.broadcasted_iota(jnp.int32, (tokens, rows), 0) * window
        for slot in range(window):
            chosen = (taken == first + slot).astype(jnp.bfloat16)
            values = jnp.dot(chosen, patches_ref[...], preferred_element_type=jnp.float32)
            picked_ref[slot] = values.astype(jnp.bfloat16)
            sums = jnp.sum(values, axis=1, keepdims=True)
            squares = jnp.sum(values * values, axis=1, keepdims=True)
            stats_ref[slot, :, :128] = jnp.broadcast_to(sums, (tokens, 128))
            stats_ref[slot, :, 128:] = jnp.broadcast_to(squares, (tokens, 128))

    vmem = pl.BlockSpec(memory_space=pltpu.VMEM)
    return pl.pallas_call(
        body,
        out_shape=(
            jax.ShapeDtypeStruct((window, tokens, width), jnp.bfloat16),
            jax.ShapeDtypeStruct((window, tokens, 256), jnp.float32),
        ),
        in_specs=[vmem],
        out_specs=(vmem, vmem),
        compiler_params=pltpu.CompilerParams(vmem_limit_bytes=VMEM),
        cost_estimate=pl.CostEstimate(flops=1000, bytes_accessed=16 << 20, transcendentals=0),
    )(patches)


def merge(tp_index, picked, stats, gain_bias, merge_weight):
    window, tokens, width = picked.shape
    features = merge_weight.shape[2]
    count = len(stats)
    share = features // count

    def body(index_ref, picked_ref, gain_bias_ref, *refs):
        stats_refs, (weight_ref, *out_refs, total_ref) = refs[:count], refs[count:]

        @pl.when(pl.program_id(0) == 0)
        def _():
            total_ref[...] = jnp.zeros_like(total_ref)

        sums = sum(ref[0] for ref in stats_refs) / DV
        row_mean = sums[:, 0:1]
        row_scale = lax.rsqrt(sums[:, 128:129] - row_mean * row_mean + EPSILON)
        gain_bias = gain_bias_ref[...].astype(jnp.float32)
        normed = (
            (picked_ref[0].astype(jnp.float32) - row_mean) * row_scale * gain_bias[0:1]
            + gain_bias[1:2]
        ).astype(jnp.bfloat16)
        total_ref[...] += jnp.dot(normed, weight_ref[0], preferred_element_type=jnp.float32)

        for index in range(count):

            @pl.when((pl.program_id(0) == window - 1) & (index_ref[0] == index))
            def _():
                for distance, out_ref in enumerate(out_refs):
                    first = (index + distance) % count * share
                    out_ref[...] = total_ref[:, first : first + share]

    def by_slot(*shape):
        return pl.BlockSpec((1, *shape), lambda i: (i, 0, 0))

    def whole(shape):
        return pl.BlockSpec(shape, lambda i: (0, 0))

    return pl.pallas_call(
        body,
        out_shape=[jax.ShapeDtypeStruct((tokens, share), jnp.float32)] * count,
        grid=(window,),
        in_specs=[pl.BlockSpec(memory_space=pltpu.SMEM)]
        + [by_slot(tokens, width), whole((2, width))]
        + [by_slot(tokens, 256)] * count
        + [by_slot(width, features)],
        out_specs=[whole((tokens, share))] * count,
        scratch_shapes=[pltpu.VMEM((tokens, features), jnp.float32)],
        compiler_params=pltpu.CompilerParams(vmem_limit_bytes=VMEM),
        cost_estimate=LIGHT,
    )(tp_index, picked, gain_bias, *stats, merge_weight)


def combine(tp_index, order, texts, images, gain_column):
    n_tp = len(texts)
    width, positions = texts[0].shape
    slots = images[0].shape[0]
    count = order.shape[0]
    rows = width * n_tp // count
    share = width // rows

    def body(index_ref, order_ref, gain_ref, *refs):
        text_refs, image_refs = refs[:n_tp], refs[n_tp : 2 * n_tp]
        out_ref, value_ref = refs[2 * n_tp :]
        code = image_refs[0][:, width : width + 2].astype(jnp.float32)
        local = code[:, 0:1] * 256.0 + code[:, 1:2] - 1.0
        place = lax.broadcasted_iota(jnp.int32, (slots, positions), 1).astype(jnp.float32)
        hit = jnp.where(local == place, 1.0, 0.0)
        covered = jnp.max(hit, axis=0, keepdims=True)
        hit = hit.astype(jnp.bfloat16)
        squares = jnp.zeros((1, positions), jnp.float32)
        for distance in range(n_tp):
            first = lax.rem(index_ref[0] + n_tp - distance, n_tp) * share
            image = lax.dot_general(
                image_refs[distance][...],
                hit,
                (((0,), (0,)), ((), ())),
                preferred_element_type=jnp.float32,
            )[:width]
            value = jnp.where(covered > 0.0, image, text_refs[distance][...].astype(jnp.float32))
            squares += jnp.sum(value * value, axis=0, keepdims=True)
            for block in range(share):
                value_ref[first + block] = value[block * rows : (block + 1) * rows]
        scale = lax.rsqrt(squares / (width * n_tp) + EPSILON)
        for block in range(count):
            source = order_ref[block]
            gain = gain_ref[source].astype(jnp.float32)
            out_ref[block] = (value_ref[source] * scale * gain).astype(out_ref.dtype)

    vmem = pl.BlockSpec(memory_space=pltpu.VMEM)
    smem = pl.BlockSpec(memory_space=pltpu.SMEM)
    return pl.pallas_call(
        body,
        out_shape=jax.ShapeDtypeStruct((count, rows, positions), jnp.bfloat16),
        in_specs=[smem, smem] + [vmem] * (1 + 2 * n_tp),
        out_specs=vmem,
        scratch_shapes=[pltpu.VMEM((count, rows, positions), jnp.float32)],
        compiler_params=pltpu.CompilerParams(vmem_limit_bytes=VMEM),
        cost_estimate=LIGHT,
    )(tp_index, order, gain_column, *texts, *images)


def shards(
    n_req, n_tp,
    patches, ln_gain, ln_bias, merge_weight, text_rows, norm_gain, qkv_weight, token_pos, text_len,
):
    row_count, width = text_rows.shape
    me = lax.axis_index("req")
    tp_index = lax.axis_index("tp").reshape(1)
    lines, line_perm, table = ring_tables(n_req)
    x_perm = [(i, i ^ 1) for i in range(n_req)]
    y_perm = [(i, i ^ 2) for i in range(n_req)]
    rows, columns = qkv_weight.shape
    cut = (columns + 255) // 256 * 128

    def along_line(block):
        return lax.ppermute(block, "req", line_perm)

    def to_sides(block):
        return lax.ppermute(block, "req", x_perm), lax.ppermute(block, "req", y_perm)

    def to_corner(by_x, by_y):
        left = lax.ppermute(by_y[:, :cut], "req", x_perm)
        right = lax.ppermute(by_x[:, cut:], "req", y_perm)
        return left, right

    held = [qkv_weight]
    held.append(along_line(held[0]))
    sides = [to_sides(held[0])]
    picked, stats_own = pick_rows(patches, merge_weight.shape[0])
    stats = [stats_own] + [tp_shift(stats_own, n_tp, d) for d in range(1, n_tp)]
    gain_bias = jnp.stack([ln_gain, ln_bias])
    text_turned = text_rows.T
    texts = [text_turned] + [tp_shift(text_turned, n_tp, d) for d in range(1, n_tp)]

    partial_value = merge(tp_index, picked, stats, gain_bias, merge_weight)

    partial_value, held[1], token_pos = tie(partial_value, held[1], token_pos)
    token_count = token_pos.shape[0]
    target = lax.div(token_pos, row_count)
    same = target[:, None] == target[None, :]
    ids = jnp.arange(token_count, dtype=jnp.int32)
    before = jnp.sum((same & (ids[None, :] < ids[:, None])).astype(jnp.int32), axis=1)
    slot = target * IMG_CAP + before
    slot_count = n_req * IMG_CAP
    code = lax.rem(token_pos, row_count) + 1
    code_cols = jnp.stack([lax.div(code, 256), lax.rem(code, 256)], axis=1).astype(jnp.bfloat16)
    held.append(along_line(held[1]))
    sides.append(to_sides(held[1]))
    merged = partial_value[0]
    for distance in range(1, n_tp):
        merged = merged + tp_shift(partial_value[distance], n_tp, distance)
    merged = merged.astype(jnp.bfloat16)
    merged, sides[0] = tie(merged, sides[0])
    halves = to_corner(*sides[0])
    padding = (-width - 2) % 128
    payload = jnp.concatenate(
        [merged, code_cols, jnp.zeros((token_count, padding), jnp.bfloat16)], axis=1
    )
    place = (
        jnp.arange(slot_count, dtype=jnp.int32)[:, None] == slot[None, :]
    ).astype(jnp.bfloat16)
    outgoing = jnp.dot(place, payload, preferred_element_type=jnp.float32).astype(jnp.bfloat16)
    arrived = lax.all_to_all(
        outgoing.reshape(n_req, IMG_CAP, -1), "req", split_axis=0, concat_axis=0
    ).reshape(slot_count, -1)

    held[2], norm_gain, me = tie(held[2], norm_gain, me)
    gain_column = norm_gain.reshape(n_req, rows, 1)
    order = lax.dynamic_slice_in_dim(jnp.asarray(table), me, 1, 0).reshape(-1)
    held.append(along_line(held[2]))
    sides.append(to_sides(held[2]))
    images = [arrived] + [tp_shift(arrived, n_tp, d) for d in range(1, n_tp)]
    blocks = combine(tp_index, order, texts, images, gain_column)

    corners = [jnp.concatenate(halves, axis=1)]
    first = jnp.concatenate([held[0], *sides[0], corners[0]], axis=0)
    second = jnp.concatenate([held[1], *sides[1]], axis=0)
    held[3], sides[2], corners[0], first, second = tie(
        held[3], sides[2], corners[0], first, second
    )
    sides.append(to_sides(held[3]))
    corners.append(along_line(corners[0]))
    for step in range(4, lines):
        held.append(along_line(held[step - 1]))
        sides.append(to_sides(held[step]))
    for step in range(2, lines - 2):
        corners.append(along_line(corners[step - 1]))
    corners.append(jnp.concatenate(to_corner(*sides[-2]), axis=1))

    def add_product(total, first, weights):
        weight = jnp.concatenate(weights, axis=0)
        count = weight.shape[0]
        source = blocks[first : first + count // rows].reshape(count, row_count)
        if total is None:
            weight, source = tie(weight, source)
        else:
            weight, source, total = tie(weight, source, total)
        part = lax.dot_general(
            source, weight, (((0,), (0,)), ((), ())), preferred_element_type=jnp.float32
        )
        return part if total is None else total + part

    total = add_product(None, 0, [first])
    total = add_product(total, 4, [second])

    total, sides[-1] = tie(total, sides[-1])
    corners.append(jnp.concatenate(to_corner(*sides[-1]), axis=1))
    for step in range(2, lines - 1):
        total = add_product(total, step * 3 + 1, [held[step], *sides[step]])
    total, late = tie(total, [held[-1], *sides[-1]])
    total = add_product(total, lines * 3 - 2, late)

    position = me * row_count + jnp.arange(row_count, dtype=jnp.int32)
    request_ids = jnp.arange(text_len.shape[0], dtype=jnp.int32)
    limits = jnp.sum(
        jnp.where(
            lax.div(position, SEQ)[:, None] == request_ids[None, :], text_len[None, :], 0
        ),
        axis=1,
    )
    keep = lax.rem(position, SEQ) < limits
    total = add_product(total, lines * 3 + 1, corners[1:])
    return jnp.where(keep[:, None], total, 0.0).astype(jnp.bfloat16)


def solution(mesh):
    placed = (
        P("req", "tp"),
        P("tp"),
        P("tp"),
        P(None, "tp", None),
        P("req", "tp"),
        P(),
        P("req", "tp"),
        P("req"),
        P(),
    )
    body = functools.partial(shards, mesh.shape["req"], mesh.shape["tp"])
    return jax.shard_map(
        body, mesh=mesh, in_specs=placed, out_specs=P("req", "tp"), check_vma=False
    )
```
